32 devices in a mesh: tm: 8 (over y, x, core), agent: 4 (over z).
Axes of the slice: x: 2, y: 2, z: 4, core: 2. Of those that a mesh axis runs over, the one named last changes fastest.
Arguments:
- states: bfloat16 [48, 512, 512], P('tm', 'agent'), may hold values from -30 to 30
- neighbours: int32 [4, 4], replicated, may hold values from 0 to 3, as said below
- w_query_t: bfloat16 [512, 512], replicated, may hold values from -16 to 16
- w_key_t: bfloat16 [512, 512], replicated, may hold values from -16 to 16
- w_value_t: bfloat16 [512, 512], replicated, may hold values from -0.25 to 0.25
- w_out_t: bfloat16 [512, 512], replicated, may hold values from -0.25 to 0.25
- w_query_a: bfloat16 [512, 512], replicated, may hold values from -16 to 16
- w_key_a: bfloat16 [512, 512], replicated, may hold values from -16 to 16
- w_value_a: bfloat16 [512, 512], replicated, may hold values from -0.25 to 0.25
- w_out_a: bfloat16 [512, 512], replicated, may hold values from -0.25 to 0.25
- w_in: bfloat16 [512, 2048], replicated, may hold values from -0.25 to 0.25
- w_mlp_out: bfloat16 [2048, 512], replicated, may hold values from -0.125 to 0.125
Outputs:
- mixed: bfloat16 [48, 512, 512], P('tm', 'agent')
The draws below stay inside these ranges and needn't reach their ends.
Inputs may be any that keep to these rules, and one draw needn't show every extreme that they name: neighbours[b] lists 4 different blocks, the first of them b itself.
All inputs are finite; a program needn't handle non-finite values.
Results may differ from the reference program's by a relative error of at most 0.006.
Values may be sent and summed in bfloat16 or wider, within the bound.
No kernel may reach another device: no remote copies, remote signals or barrier semaphores. Data moves between devices by JAX's collectives and lax.ppermute only.
A program may use at most 128 MiB of HBM per device.

```python
import math
import jax
import jax.numpy as jnp
from jax import lax

D = 512
HEADS = 8
FF = 2048
BLK = 128
NEIGH = 4
TIME = 48
NBLK = 4
AGENTS = 512


def draw_states(key, part):
    fold = jax.random.fold_in
    base = jax.random.normal(fold(key, 1), (TIME, AGENTS, D), jnp.float32)
    row_scale = jnp.exp(jax.random.uniform(fold(key, 2), (TIME, AGENTS, 1), jnp.float32) * math.log(10.0))
    col_scale = jnp.exp(jax.random.uniform(fold(key, 3), (1, 1, D), jnp.float32) * math.log(10.0))
    return jnp.clip(base * row_scale * col_scale / 10.0, -30.0, 30.0).astype(jnp.bfloat16)


def paired_weights(key, salt):
    fold = jax.random.fold_in
    query_w = jax.random.normal(fold(key, salt), (D, D), jnp.float32) * D ** (-0.5)
    key_w = jax.random.normal(fold(key, salt + 1), (D, D), jnp.float32) * D ** (-0.5)
    return (query_w, key_w)


def draw_w_query_t(key, part):
    return paired_weights(key, 10)[0].astype(jnp.bfloat16)


def draw_w_key_t(key, part):
    return paired_weights(key, 10)[1].astype(jnp.bfloat16)


def draw_w_query_a(key, part):
    return paired_weights(key, 20)[0].astype(jnp.bfloat16)


def draw_w_key_a(key, part):
    return paired_weights(key, 20)[1].astype(jnp.bfloat16)


def draw_neighbours(key, part):
    row_keys = jax.random.split(jax.random.fold_in(key, 30), NBLK)

    def one_row(row_key, block):
        order = jax.random.permutation(row_key, NBLK - 1)[:NEIGH - 1].astype(jnp.int32)
        others = order + (order >= block).astype(jnp.int32)
        return jnp.concatenate([block[None], others])
    return jax.vmap(one_row)(row_keys, jnp.arange(NBLK, dtype=jnp.int32))


def centred(own_key, extent, deviation, limit, kind=jnp.bfloat16):
    entries = jax.random.normal(own_key, extent, jnp.float32) * deviation
    return jnp.minimum(jnp.maximum(entries, -limit), limit).astype(kind)


def setup_inputs(seed: int = 0) -> dict:
    streams_of = jax.random.split(jax.random.key(seed), 13)
    states = draw_states(jax.random.fold_in(streams_of[12], 71), 0)
    neighbours = draw_neighbours(jax.random.fold_in(streams_of[12], 71), 0)
    w_query_t = draw_w_query_t(jax.random.fold_in(streams_of[12], 71), 0)
    w_key_t = draw_w_key_t(jax.random.fold_in(streams_of[12], 71), 0)
    w_value_t = centred(streams_of[4], (D, D), D ** -0.5, 0.25)
    w_out_t = centred(streams_of[5], (D, D), D ** -0.5, 0.25)
    w_query_a = draw_w_query_a(jax.random.fold_in(streams_of[12], 71), 0)
    w_key_a = draw_w_key_a(jax.random.fold_in(streams_of[12], 71), 0)
    w_value_a = centred(streams_of[8], (D, D), D ** -0.5, 0.25)
    w_out_a = centred(streams_of[9], (D, D), D ** -0.5, 0.25)
    w_in = centred(streams_of[10], (D, FF), D ** -0.5, 0.25)
    w_mlp_out = centred(streams_of[11], (FF, D), FF ** -0.5, 0.125)
    return {"states": states, "neighbours": neighbours, "w_query_t": w_query_t, "w_key_t": w_key_t, "w_value_t": w_value_t, "w_out_t": w_out_t, "w_query_a": w_query_a, "w_key_a": w_key_a, "w_value_a": w_value_a, "w_out_a": w_out_a, "w_in": w_in, "w_mlp_out": w_mlp_out}


negative_floor = -1e+30
epsilon = 1e-06

def rms_normed(values):
    wide = values.astype(jnp.float32)
    scale = lax.rsqrt(lax.optimization_barrier(jnp.mean(wide * wide, axis=-1, keepdims=True)) + epsilon)
    return (wide * scale).astype(jnp.bfloat16)

def project(normed, weight):
    return jnp.dot(normed, weight, preferred_element_type=jnp.float32).astype(jnp.bfloat16)

def attend(query, keys, values, allowed):
    batch, query_len, features = query.shape
    key_len = keys.shape[1]
    head_size = features // HEADS
    query_h = query.reshape(batch, query_len, HEADS, head_size).astype(jnp.float32)
    keys_h = keys.reshape(batch, key_len, HEADS, head_size).astype(jnp.float32)
    values_h = values.reshape(batch, key_len, HEADS, head_size).astype(jnp.float32)
    scores = jnp.einsum('bqhe,bkhe->bhqk', query_h, keys_h) * head_size ** (-0.5)
    scores = jnp.where(allowed[:, None], scores, negative_floor)
    largest = lax.optimization_barrier(jnp.max(scores, axis=-1, keepdims=True))
    weights = jnp.where(allowed[:, None], jnp.exp(scores - largest), 0.0)
    totals = lax.optimization_barrier(jnp.sum(weights, axis=-1))
    rounded = lax.optimization_barrier(weights.astype(jnp.bfloat16)).astype(jnp.float32)
    summed = jnp.einsum('bhqk,bkhe->bqhe', rounded, values_h)
    result = summed / jnp.transpose(totals, (0, 2, 1))[..., None]
    return result.reshape(batch, query_len, features).astype(jnp.bfloat16)

def reference(states, neighbours, w_query_t, w_key_t, w_value_t, w_out_t, w_query_a, w_key_a, w_value_a, w_out_a, w_in, w_mlp_out):

    def time_block(block_states):
        normed = rms_normed(block_states)
        query = jnp.swapaxes(project(normed, w_query_t), 0, 1)
        keys = jnp.swapaxes(project(normed, w_key_t), 0, 1)
        values = jnp.swapaxes(project(normed, w_value_t), 0, 1)
        steps = jnp.arange(TIME)
        allowed = (steps[None, :] <= steps[:, None])[None]
        mixed_time = jnp.swapaxes(attend(query, keys, values, allowed), 0, 1)
        added = block_states.astype(jnp.float32) + jnp.dot(mixed_time, w_out_t, preferred_element_type=jnp.float32)
        return added.astype(jnp.bfloat16)
    blocks = jnp.transpose(states.reshape(TIME, NBLK, BLK, D), (1, 0, 2, 3))
    after_time = jnp.transpose(lax.map(time_block, blocks), (1, 0, 2, 3)).reshape(TIME, AGENTS, D)

    def agent_step(row_states):
        normed = rms_normed(row_states)
        query = project(normed, w_query_a).reshape(NBLK, BLK, D)
        keys = project(normed, w_key_a).reshape(NBLK, BLK, D)[neighbours].reshape(NBLK, NEIGH * BLK, D)
        values = project(normed, w_value_a).reshape(NBLK, BLK, D)[neighbours].reshape(NBLK, NEIGH * BLK, D)
        allowed = jnp.ones((1, BLK, NEIGH * BLK), dtype=bool)
        mixed_agent = attend(query, keys, values, allowed).reshape(AGENTS, D)
        after_agent = (row_states.astype(jnp.float32) + jnp.dot(mixed_agent, w_out_a, preferred_element_type=jnp.float32)).astype(jnp.bfloat16)
        inner = jax.nn.gelu(jnp.dot(rms_normed(after_agent), w_in, preferred_element_type=jnp.float32), approximate=True).astype(jnp.bfloat16)
        final = after_agent.astype(jnp.float32) + jnp.dot(inner, w_mlp_out, preferred_element_type=jnp.float32)
        return final.astype(jnp.bfloat16)
    return lax.map(agent_step, after_time)
```

```python
import functools
import math

import jax
import jax.numpy as jnp
from jax import lax
from jax.experimental import pallas as pl
from jax.experimental.pallas import tpu as pltpu
from jax.sharding import PartitionSpec as P

HEADS = 8


negative_floor = -1e30
epsilon = 1e-06


def rms_normed(values):
    wide = values.astype(jnp.float32)
    scale = lax.rsqrt(jnp.mean(wide * wide, axis=-1, keepdims=True) + epsilon)
    return (wide * scale).astype(jnp.bfloat16)


def project(normed, weight):
    return jnp.dot(normed, weight, preferred_element_type=jnp.float32).astype(jnp.bfloat16)


def attend(query, keys, values, allowed):
    batch, query_len, features = query.shape
    key_len = keys.shape[1]
    head_size = features // HEADS
    query_h = query.reshape(batch, query_len, HEADS, head_size)
    keys_h = keys.reshape(batch, key_len, HEADS, head_size)
    values_h = values.reshape(batch, key_len, HEADS, head_size)
    scores = jnp.einsum(
        "bqhe,bkhe->bhqk", query_h, keys_h, preferred_element_type=jnp.float32
    ) * head_size ** (-0.5)
    scores = jnp.where(allowed[:, None], scores, negative_floor)
    largest = jnp.max(scores, axis=-1, keepdims=True)
    weights = jnp.where(allowed[:, None], jnp.exp(scores - largest), 0.0)
    totals = jnp.sum(weights, axis=-1)
    summed = jnp.einsum(
        "bhqk,bkhe->bqhe",
        weights.astype(jnp.bfloat16),
        values_h,
        preferred_element_type=jnp.float32,
    )
    result = summed / jnp.transpose(totals, (0, 2, 1))[..., None]
    return result.reshape(batch, query_len, features).astype(jnp.bfloat16)


def general_time(states, w_query_t, w_key_t, w_value_t, w_out_t):
    local_steps = states.shape[0]
    normed = rms_normed(states)
    query = jnp.swapaxes(project(normed, w_query_t), 0, 1)
    keys = lax.all_gather(project(normed, w_key_t), "tm", axis=0, tiled=True)
    values = lax.all_gather(project(normed, w_value_t), "tm", axis=0, tiled=True)
    query_time = lax.axis_index("tm") * local_steps + jnp.arange(local_steps)
    allowed = (jnp.arange(keys.shape[0])[None, :] <= query_time[:, None])[None]
    mixed = attend(query, jnp.swapaxes(keys, 0, 1), jnp.swapaxes(values, 0, 1), allowed)
    return (
        states.astype(jnp.float32)
        + jnp.dot(jnp.swapaxes(mixed, 0, 1), w_out_t, preferred_element_type=jnp.float32)
    ).astype(jnp.bfloat16)


def general_agent(
    after_time, neighbours, w_query_a, w_key_a, w_value_a, w_out_a, w_in, w_mlp_out
):
    local_steps, local_agents, features = after_time.shape
    second_normed = rms_normed(after_time)
    agent_query = project(second_normed, w_query_a)
    block_count = lax.axis_size("agent")
    chosen_blocks = lax.dynamic_slice_in_dim(neighbours, lax.axis_index("agent"), 1, 0)[0]
    neighbour_count = neighbours.shape[1]
    everyone = lax.all_gather(second_normed, "agent", axis=1, tiled=True)
    picked = jnp.take(
        everyone.reshape(local_steps, block_count, local_agents, features), chosen_blocks, axis=1
    )
    picked = picked.reshape(local_steps, neighbour_count * local_agents, features)
    agent_key = project(picked, w_key_a)
    agent_value = project(picked, w_value_a)
    allowed_all = jnp.ones((1, local_agents, neighbour_count * local_agents), dtype=bool)
    agent_mixed = attend(agent_query, agent_key, agent_value, allowed_all)
    after_agent = (
        after_time.astype(jnp.float32)
        + jnp.dot(agent_mixed, w_out_a, preferred_element_type=jnp.float32)
    ).astype(jnp.bfloat16)
    inner = jax.nn.gelu(
        jnp.dot(rms_normed(after_agent), w_in, preferred_element_type=jnp.float32), approximate=True
    ).astype(jnp.bfloat16)
    final = after_agent.astype(jnp.float32) + jnp.dot(
        inner, w_mlp_out, preferred_element_type=jnp.float32
    )
    return final.astype(jnp.bfloat16)


NT = (((1,), (1,)), ((), ()))


def softmax_parts(scores, factor):
    largest = jnp.max(scores, axis=-1, keepdims=True)
    weights = jnp.exp2((scores - largest) * factor)
    return weights.astype(jnp.bfloat16), jnp.sum(weights, axis=-1, keepdims=True)


def pair_attention(query, keys, values, factor, bias=None):
    half = query.shape[1] // 2
    zero = jnp.zeros_like(keys)
    first_k = lax.broadcasted_iota(jnp.int32, keys.shape, 1) < half
    first_q = lax.broadcasted_iota(jnp.int32, query.shape, 1) < half
    sums, totals = None, []
    for mine in (first_k, jnp.logical_not(first_k)):
        scores = lax.dot_general(
            query, jnp.where(mine, keys, zero), NT, preferred_element_type=jnp.float32
        )
        if bias is not None:
            scores = scores + bias
        weights, total = softmax_parts(scores, factor)
        part = jnp.dot(
            weights, jnp.where(mine, values, zero), preferred_element_type=jnp.float32
        )
        sums = part if sums is None else sums + part
        totals.append(total)
    return sums / jnp.where(first_q, totals[0], totals[1])


def time_kernel(size, first, *refs):
    pieces, (w_query, w_key, w_value, w_out) = refs[:size], refs[size : size + 4]
    outs_a, outs_b = refs[size + 4 : 2 * size + 4], refs[2 * size + 4 : 3 * size + 4]
    wide, normed, query, keys, values, mixed = refs[3 * size + 4 :]
    steps, agents, features = pieces[0].shape
    rows = steps * agents
    total_steps = steps * size
    me = lax.axis_index("tm")
    lanes_of = [slice(c * 128, (c + 1) * 128) for c in range(features // 128)]
    for k in range(size):
        start = pl.multiple_of(jnp.bitwise_xor(me, k) * rows, rows)
        piece = pieces[k][...].reshape(rows, features).astype(jnp.float32)
        for c, lanes in enumerate(lanes_of):
            wide[c, pl.ds(start, rows), :] = piece[:, lanes]
    for agent in range(agents):
        at = pl.ds(agent, total_steps, stride=agents)
        own = jnp.concatenate([wide[c, at, :] for c in range(len(lanes_of))], axis=1)
        scale = lax.rsqrt(jnp.mean(own * own, axis=-1, keepdims=True) + epsilon)
        normed[pl.ds(agent * total_steps, total_steps), :] = (own * scale).astype(jnp.bfloat16)
    for weight, result in ((w_query, query), (w_key, keys), (w_value, values)):
        result[...] = jnp.dot(
            normed[...], weight[...], preferred_element_type=jnp.float32
        ).astype(jnp.bfloat16)

    group = 2 * total_steps
    row = lax.broadcasted_iota(jnp.int32, (group, group), 0)
    column = lax.broadcasted_iota(jnp.int32, (group, group), 1)
    same = (row >= total_steps) == (column >= total_steps)
    bias = jnp.where(jnp.logical_and(same, column <= row), 0.0, negative_floor)
    head_size = features // HEADS
    factor = math.log2(math.e) * head_size**-0.5

    def one_group(g, carry):
        at = pl.ds(pl.multiple_of(g * group, group), group)
        for pair in range(HEADS // 2):
            lanes = pl.ds(pair * 2 * head_size, 2 * head_size)
            mixed[at, lanes] = pair_attention(
                query[at, lanes], keys[at, lanes], values[at, lanes], factor, bias
            ).astype(jnp.bfloat16)
        return carry

    lax.fori_loop(0, agents // 2, one_group, 0)
    added = jnp.dot(mixed[...], w_out[...], preferred_element_type=jnp.float32)
    for agent in range(agents):
        at = pl.ds(agent, total_steps, stride=agents)
        mine = added[agent * total_steps : (agent + 1) * total_steps]
        for c, lanes in enumerate(lanes_of):
            wide[c, at, :] = wide[c, at, :] + mine[:, lanes]
    for k in range(size):
        start = pl.multiple_of(jnp.bitwise_xor(me, k) * rows, rows)
        piece = jnp.concatenate(
            [wide[c, pl.ds(start, rows), :] for c in range(len(lanes_of))], axis=1
        )
        piece = piece.astype(jnp.bfloat16).reshape(pieces[0].shape)
        outs_a[k][...] = piece[:first]
        outs_b[k][...] = piece[first:]


def time_stage(pieces, weights, first):
    size = len(pieces)
    steps, agents, features = pieces[0].shape
    rows = steps * agents * size
    kind = jnp.bfloat16
    return pl.pallas_call(
        functools.partial(time_kernel, size, first),
        out_shape=[jax.ShapeDtypeStruct((first, agents, features), kind)] * size
        + [jax.ShapeDtypeStruct((steps - first, agents, features), kind)] * size,
        in_specs=[pl.BlockSpec(memory_space=pltpu.VMEM)] * (size + 4),
        out_specs=[pl.BlockSpec(memory_space=pltpu.VMEM)] * (2 * size),
        scratch_shapes=[pltpu.VMEM((features // 128, rows, 128), jnp.float32)]
        + [pltpu.VMEM((rows, features), kind)] * 5,
        compiler_params=pltpu.CompilerParams(vmem_limit_bytes=32 * 2**20),
        name="time_attention",
    )(*pieces, *weights)


def pack_kernel(size, choose, *refs):
    pieces, outs = refs[:size], refs[size:]
    agents = pieces[0].shape[1]
    me, plane = lax.axis_index("tm"), lax.axis_index("agent")
    for out, step in zip(outs, choose(plane)):
        for k in range(size):
            start = pl.multiple_of(jnp.bitwise_xor(me, k) * agents, agents)
            out[pl.ds(start, agents), :] = pieces[k][step]


def pack_stage(pieces, choose, count):
    size = len(pieces)
    _, agents, features = pieces[0].shape
    return pl.pallas_call(
        functools.partial(pack_kernel, size, choose),
        out_shape=[jax.ShapeDtypeStruct((agents * size, features), jnp.bfloat16)] * count,
        in_specs=[pl.BlockSpec(memory_space=pltpu.VMEM)] * size,
        out_specs=[pl.BlockSpec(memory_space=pltpu.VMEM)] * count,
        name="pack_steps",
    )(*pieces)


def agent_body(count, *refs):
    blocks = refs[:count]
    w_query, w_key, w_value, w_out, w_in, w_mlp_out = refs[count : count + 6]
    outs = refs[count + 6 : 2 * count + 6]
    normed, query, keys, values, mixed, after, inner = refs[2 * count + 6 :]
    agents, features = blocks[0].shape
    head_size = features // HEADS
    factor = math.log2(math.e) * head_size**-0.5
    for b in range(count):
        wide = blocks[b][...].astype(jnp.float32)
        scale = lax.rsqrt(jnp.mean(wide * wide, axis=-1, keepdims=True) + epsilon)
        normed[pl.ds(b * agents, agents), :] = (wide * scale).astype(jnp.bfloat16)
    for weight, result in ((w_query, query), (w_key, keys), (w_value, values)):
        result[...] = jnp.dot(
            normed[...], weight[...], preferred_element_type=jnp.float32
        ).astype(jnp.bfloat16)

    def one_block(b, carry):
        at = pl.ds(pl.multiple_of(b * agents, agents), agents)
        for pair in range(HEADS // 2):
            lanes = pl.ds(pair * 2 * head_size, 2 * head_size)
            mixed[at, lanes] = pair_attention(
                query[at, lanes], keys[:, lanes], values[:, lanes], factor
            ).astype(jnp.bfloat16)
        return carry

    lax.fori_loop(0, count, one_block, 0)
    added = jnp.dot(mixed[...], w_out[...], preferred_element_type=jnp.float32)
    for b in range(count):
        own = (blocks[b][...].astype(jnp.float32) + added[b * agents : (b + 1) * agents]).astype(
            jnp.bfloat16
        )
        after[pl.ds(b * agents, agents), :] = own
        wide = own.astype(jnp.float32)
        scale = lax.rsqrt(jnp.mean(wide * wide, axis=-1, keepdims=True) + epsilon)
        normed[pl.ds(b * agents, agents), :] = (wide * scale).astype(jnp.bfloat16)
    hidden = w_in.shape[1]
    for start in range(0, hidden, features):
        inner[:, pl.ds(start, features)] = jax.nn.gelu(
            jnp.dot(
                normed[...], w_in[:, pl.ds(start, features)], preferred_element_type=jnp.float32
            ),
            approximate=True,
        ).astype(jnp.bfloat16)
    final = after[...].astype(jnp.float32) + jnp.dot(
        inner[...], w_mlp_out[...], preferred_element_type=jnp.float32
    )
    for b in range(count):
        outs[b][...] = final[b * agents : (b + 1) * agents].astype(jnp.bfloat16)


def agent_kernel(count, middle_only, *refs):
    if middle_only:
        plane = lax.axis_index("agent")

        @pl.when(jnp.logical_or(plane == 1, plane == 2))
        def _():
            agent_body(count, *refs)

    else:
        agent_body(count, *refs)


def agent_stage(blocks, weights, middle_only):
    count = len(blocks)
    agents, features = blocks[0].shape
    hidden = weights[4].shape[1]
    rows = count * agents
    kind = jnp.bfloat16
    return pl.pallas_call(
        functools.partial(agent_kernel, count, middle_only),
        out_shape=[jax.ShapeDtypeStruct((agents, features), kind)] * count,
        in_specs=[pl.BlockSpec(memory_space=pltpu.VMEM)] * (count + 6),
        out_specs=[pl.BlockSpec(memory_space=pltpu.VMEM)] * count,
        scratch_shapes=[pltpu.VMEM((rows, features), kind)] * 6
        + [pltpu.VMEM((rows, hidden), kind)],
        compiler_params=pltpu.CompilerParams(vmem_limit_bytes=40 * 2**20),
        name="agent_step",
    )(*blocks, *weights)


def xor_pairs(size, k, targets=None):
    return [(j, j ^ k) for j in range(size) if targets is None or j ^ k in targets]


def exchange(parts, axis, targets=None):
    size = len(parts)
    return [parts[0]] + [
        lax.ppermute(parts[k], axis, xor_pairs(size, k, targets)) for k in range(1, size)
    ]


def picked(plane, values):
    result = jnp.int32(values[0])
    for place in range(1, len(values)):
        result = jnp.where(plane == place, values[place], result)
    return result


def whole_steps(plane):
    return [jnp.bitwise_xor(plane, k) for k in range(4)]


def extra_steps(plane):
    return [
        picked(plane, (0, 0, 1, 0)),
        picked(plane, (0, 0, 0, 1)),
        picked(plane, (1, 0, 0, 0)),
        picked(plane, (0, 1, 0, 0)),
    ]


def local(
    states,
    neighbours,
    w_query_t,
    w_key_t,
    w_value_t,
    w_out_t,
    w_query_a,
    w_key_a,
    w_value_a,
    w_out_a,
    w_in,
    w_mlp_out,
):
    local_steps, local_agents, features = states.shape
    size, planes = lax.axis_size("tm"), lax.axis_size("agent")
    share = local_agents // size
    time_weights = (w_query_t, w_key_t, w_value_t, w_out_t)
    agent_weights = (w_query_a, w_key_a, w_value_a, w_out_a, w_in, w_mlp_out)
    fits = (
        size & (size - 1) == 0
        and share * size == local_agents
        and share % 16 == 0
        and planes == 4
        and neighbours.shape == (4, 4)
        and local_steps == 6
    )
    if not fits:
        after_time = general_time(states, *time_weights)
        return general_agent(after_time, neighbours, *agent_weights)

    me, plane = lax.axis_index("tm"), lax.axis_index("agent")
    parts = [
        lax.dynamic_slice_in_dim(states, jnp.bitwise_xor(me, k) * share, share, 1)
        for k in range(size)
    ]
    pieces = exchange(parts, "tm")
    shared = time_stage(pieces, time_weights, 4)
    pieces_a = exchange(shared[:size], "tm")
    pieces_b = exchange(shared[size:], "tm")
    blocks_a = exchange(pack_stage(pieces_a, whole_steps, 4), "agent")
    blocks_b = exchange(pack_stage(pieces_b, extra_steps, 4), "agent", (1, 2))
    done_a = exchange(agent_stage(blocks_a, agent_weights, False), "agent")
    result_b = agent_stage(blocks_b, agent_weights, True)
    done_b = [result_b[0]] + [
        lax.ppermute(result_b[k], "agent", [(j, j ^ k) for j in (1, 2)]) for k in range(1, 4)
    ]
    finals = jnp.stack(done_a)
    first = [
        lax.dynamic_index_in_dim(finals, jnp.bitwise_xor(plane, t), 0, False) for t in range(4)
    ]
    extra = jnp.stack(done_b)
    fourth = lax.dynamic_index_in_dim(extra, picked(plane, (1, 0, 3, 2)), 0, False)
    fifth = lax.dynamic_index_in_dim(extra, picked(plane, (2, 3, 0, 1)), 0, False)
    return jnp.stack(first + [fourth, fifth])


def solution(mesh):
    placed = (P("tm", "agent", None), P(), P(), P(), P(), P(), P(), P(), P(), P(), P(), P())
    return jax.shard_map(
        local, mesh=mesh, in_specs=placed, out_specs=P("tm", "agent", None), check_vma=False
    )
```

```python
import functools
import math

import jax
import jax.numpy as jnp
from jax import lax
from jax.experimental import pallas as pl
from jax.experimental.pallas import tpu as pltpu
from jax.sharding import PartitionSpec as P

HEADS = 8


negative_floor = -1e30
epsilon = 1e-06


def rms_normed(values):
    wide = values.astype(jnp.float32)
    scale = lax.rsqrt(jnp.mean(wide * wide, axis=-1, keepdims=True) + epsilon)
    return (wide * scale).astype(jnp.bfloat16)


def project(normed, weight):
    return jnp.dot(normed, weight, preferred_element_type=jnp.float32).astype(jnp.bfloat16)


def attend(query, keys, values, allowed):
    batch, query_len, features = query.shape
    key_len = keys.shape[1]
    head_size = features // HEADS
    query_h = query.reshape(batch, query_len, HEADS, head_size)
    keys_h = keys.reshape(batch, key_len, HEADS, head_size)
    values_h = values.reshape(batch, key_len, HEADS, head_size)
    scores = jnp.einsum(
        "bqhe,bkhe->bhqk", query_h, keys_h, preferred_element_type=jnp.float32
    ) * head_size ** (-0.5)
    scores = jnp.where(allowed[:, None], scores, negative_floor)
    largest = jnp.max(scores, axis=-1, keepdims=True)
    weights = jnp.where(allowed[:, None], jnp.exp(scores - largest), 0.0)
    totals = jnp.sum(weights, axis=-1)
    summed = jnp.einsum(
        "bhqk,bkhe->bqhe",
        weights.astype(jnp.bfloat16),
        values_h,
        preferred_element_type=jnp.float32,
    )
    result = summed / jnp.transpose(totals, (0, 2, 1))[..., None]
    return result.reshape(batch, query_len, features).astype(jnp.bfloat16)


def general_time(states, w_query_t, w_key_t, w_value_t, w_out_t):
    local_steps = states.shape[0]
    normed = rms_normed(states)
    query = jnp.swapaxes(project(normed, w_query_t), 0, 1)
    keys = lax.all_gather(project(normed, w_key_t), "tm", axis=0, tiled=True)
    values = lax.all_gather(project(normed, w_value_t), "tm", axis=0, tiled=True)
    query_time = lax.axis_index("tm") * local_steps + jnp.arange(local_steps)
    allowed = (jnp.arange(keys.shape[0])[None, :] <= query_time[:, None])[None]
    mixed = attend(query, jnp.swapaxes(keys, 0, 1), jnp.swapaxes(values, 0, 1), allowed)
    return (
        states.astype(jnp.float32)
        + jnp.dot(jnp.swapaxes(mixed, 0, 1), w_out_t, preferred_element_type=jnp.float32)
    ).astype(jnp.bfloat16)


def general_agent(
    after_time, neighbours, w_query_a, w_key_a, w_value_a, w_out_a, w_in, w_mlp_out
):
    local_steps, local_agents, features = after_time.shape
    second_normed = rms_normed(after_time)
    agent_query = project(second_normed, w_query_a)
    block_count = lax.axis_size("agent")
    chosen_blocks = lax.dynamic_slice_in_dim(neighbours, lax.axis_index("agent"), 1, 0)[0]
    neighbour_count = neighbours.shape[1]
    everyone = lax.all_gather(second_normed, "agent", axis=1, tiled=True)
    picked = jnp.take(
        everyone.reshape(local_steps, block_count, local_agents, features), chosen_blocks, axis=1
    )
    picked = picked.reshape(local_steps, neighbour_count * local_agents, features)
    agent_key = project(picked, w_key_a)
    agent_value = project(picked, w_value_a)
    allowed_all = jnp.ones((1, local_agents, neighbour_count * local_agents), dtype=bool)
    agent_mixed = attend(agent_query, agent_key, agent_value, allowed_all)
    after_agent = (
        after_time.astype(jnp.float32)
        + jnp.dot(agent_mixed, w_out_a, preferred_element_type=jnp.float32)
    ).astype(jnp.bfloat16)
    inner = jax.nn.gelu(
        jnp.dot(rms_normed(after_agent), w_in, preferred_element_type=jnp.float32), approximate=True
    ).astype(jnp.bfloat16)
    final = after_agent.astype(jnp.float32) + jnp.dot(
        inner, w_mlp_out, preferred_element_type=jnp.float32
    )
    return final.astype(jnp.bfloat16)


NT = (((1,), (1,)), ((), ()))
VMEM, HBM = pltpu.VMEM, pltpu.HBM


def spec(space):
    return pl.BlockSpec(memory_space=space)


def norm_of(wide):
    scale = lax.rsqrt(jnp.mean(wide * wide, axis=-1, keepdims=True) + epsilon)
    return (wide * scale).astype(jnp.bfloat16)


def gelu(x):
    inside = x * (math.sqrt(2 / math.pi) + (math.sqrt(2 / math.pi) * 0.044715) * (x * x))
    half = 0.5 * x
    return half + half * jnp.tanh(inside)


def fetch(sources, targets, sems):
    copies = [
        pltpu.make_async_copy(source, target, sems.at[k])
        for k, (source, target) in enumerate(zip(sources, targets))
    ]
    for copy in copies:
        copy.start()
    return copies


def split_heads(values, even, odd, ones=False):
    width = values.shape[1]
    for pair in range(HEADS // 2):
        wide = width // (HEADS // 2)
        own = values[:, pair * wide : (pair + 1) * wide]
        first = lax.broadcasted_iota(jnp.int32, own.shape, 1) < wide // 2
        zero = jnp.zeros_like(own)
        if ones:
            one = jnp.ones_like(own)
            at = 2 * pair * wide
            even[:, at : at + wide] = jnp.where(first, own, zero)
            odd[:, at : at + wide] = jnp.where(first, zero, own)
            even[:, at + wide : at + 2 * wide] = jnp.where(first, one, zero)
            odd[:, at + wide : at + 2 * wide] = jnp.where(first, zero, one)
        else:
            at = pair * wide
            even[:, at : at + wide] = jnp.where(first, own, zero)
            odd[:, at : at + wide] = jnp.where(first, zero, own)


def pair_attention(query, keys, values, factor, bias=None):
    sums = None
    for key, value in zip(keys, values):
        scores = lax.dot_general(query, key, NT, preferred_element_type=jnp.float32)
        if bias is not None:
            scores = scores + bias
        largest = jnp.max(scores, axis=-1, keepdims=True)
        weights = jnp.exp2((scores - largest) * factor).astype(jnp.bfloat16)
        part = jnp.dot(weights, value, preferred_element_type=jnp.float32)
        sums = part if sums is None else sums + part
    wide = query.shape[1]
    return (sums[:, :wide] / sums[:, wide:]).astype(jnp.bfloat16)


def time_kernel(size, *refs):
    pieces, weights = refs[:size], refs[size : size + 4]
    outs = refs[size + 4 : 2 * size + 4]
    wide, normed, query, key_e, key_o, value_e, value_o, mixed = refs[2 * size + 4 : 2 * size + 12]
    w_query, w_key, w_value, w_out, sems = refs[2 * size + 12 :]
    copies = fetch(weights, (w_query, w_key, w_value, w_out), sems)
    steps, agents, features = pieces[0].shape
    rows = steps * agents
    total_steps = steps * size
    me = lax.axis_index("tm")
    lanes_of = [slice(c * 128, (c + 1) * 128) for c in range(features // 128)]
    for k in range(size):
        start = pl.multiple_of(jnp.bitwise_xor(me, k) * rows, rows)
        piece = pieces[k][...].reshape(rows, features).astype(jnp.float32)
        for c, lanes in enumerate(lanes_of):
            wide[c, pl.ds(start, rows), :] = piece[:, lanes]
    for agent in range(agents):
        at = pl.ds(agent, total_steps, stride=agents)
        own = jnp.concatenate([wide[c, at, :] for c in range(len(lanes_of))], axis=1)
        normed[pl.ds(agent * total_steps, total_steps), :] = norm_of(own)
    for copy in copies[:3]:
        copy.wait()
    query[...] = project(normed[...], w_query[...])
    split_heads(project(normed[...], w_key[...]), key_e, key_o)
    split_heads(project(normed[...], w_value[...]), value_e, value_o, True)

    group = 2 * total_steps
    row = lax.broadcasted_iota(jnp.int32, (group, group), 0)
    column = lax.broadcasted_iota(jnp.int32, (group, group), 1)
    same = (row >= total_steps) == (column >= total_steps)
    bias = jnp.where(jnp.logical_and(same, column <= row), 0.0, negative_floor)
    head_size = features // HEADS
    factor = math.log2(math.e) * head_size**-0.5

    def one_group(g, carry):
        at = pl.ds(pl.multiple_of(g * group, group), group)
        for pair in range(HEADS // 2):
            lanes = pl.ds(pair * 2 * head_size, 2 * head_size)
            double = pl.ds(pair * 4 * head_size, 4 * head_size)
            mixed[at, lanes] = pair_attention(
                query[at, lanes],
                (key_e[at, lanes], key_o[at, lanes]),
                (value_e[at, double], value_o[at, double]),
                factor,
                bias,
            )
        return carry

    lax.fori_loop(0, agents // 2, one_group, 0, unroll=True)
    copies[3].wait()
    added = jnp.dot(mixed[...], w_out[...], preferred_element_type=jnp.float32)
    for agent in range(agents):
        at = pl.ds(agent, total_steps, stride=agents)
        mine = added[agent * total_steps : (agent + 1) * total_steps]
        for c, lanes in enumerate(lanes_of):
            wide[c, at, :] = wide[c, at, :] + mine[:, lanes]
    for k in range(size):
        start = pl.multiple_of(jnp.bitwise_xor(me, k) * rows, rows)
        piece = jnp.concatenate(
            [wide[c, pl.ds(start, rows), :] for c in range(len(lanes_of))], axis=1
        )
        outs[k][...] = piece.astype(jnp.bfloat16).reshape(pieces[0].shape)


def time_stage(pieces, weights):
    size = len(pieces)
    steps, agents, features = pieces[0].shape
    rows = steps * agents * size
    kind = jnp.bfloat16
    return pl.pallas_call(
        functools.partial(time_kernel, size),
        out_shape=[jax.ShapeDtypeStruct((steps, agents, features), kind)] * size,
        in_specs=[spec(VMEM)] * size + [spec(HBM)] * 4,
        out_specs=[spec(VMEM)] * size,
        scratch_shapes=[VMEM((features // 128, rows, 128), jnp.float32)]
        + [VMEM((rows, features), kind)] * 4
        + [VMEM((rows, 2 * features), kind)] * 2
        + [VMEM((rows, features), kind)]
        + [VMEM(w.shape, kind) for w in weights]
        + [pltpu.SemaphoreType.DMA((4,))],
        compiler_params=pltpu.CompilerParams(vmem_limit_bytes=24 * 2**20),
        name="time_attention",
    )(*pieces, *weights)


def pack_kernel(size, choose, *refs):
    count = len(choose(0))
    pieces, outs = refs[:size], refs[len(refs) - count :]
    agents = pieces[0].shape[1]
    me, plane = lax.axis_index("tm"), lax.axis_index("agent")
    for out, step in zip(outs, choose(plane)):
        for k in range(size):
            start = pl.multiple_of(jnp.bitwise_xor(me, k) * agents, agents)
            out[pl.ds(start, agents), :] = pieces[k][step]


def pack_stage(pieces, choose, after=()):
    size, count = len(pieces), len(choose(0))
    _, agents, features = pieces[0].shape
    return pl.pallas_call(
        functools.partial(pack_kernel, size, choose),
        out_shape=[jax.ShapeDtypeStruct((agents * size, features), jnp.bfloat16)] * count,
        in_specs=[spec(VMEM)] * size + [spec(pl.ANY)] * len(after),
        out_specs=[spec(VMEM)] * count,
        compiler_params=pltpu.CompilerParams(vmem_limit_bytes=8 * 2**20),
        name="pack_steps",
    )(*pieces, *after)


def agent_body(count, blocks, weights, outs, scratch):
    normed, query, key_e, key_o, value_e, value_o, mixed, after, inner = scratch[:9]
    w_query, w_key, w_value, w_out, w_in, w_mlp_out, sems = scratch[9:]
    copies = fetch(weights, (w_query, w_key, w_value, w_out, w_in, w_mlp_out), sems)
    agents, features = blocks[0].shape
    head_size = features // HEADS
    factor = math.log2(math.e) * head_size**-0.5
    for b in range(count):
        normed[pl.ds(b * agents, agents), :] = norm_of(blocks[b][...].astype(jnp.float32))
    for copy in copies[:3]:
        copy.wait()
    query[...] = project(normed[...], w_query[...])
    split_heads(project(normed[...], w_key[...]), key_e, key_o)
    split_heads(project(normed[...], w_value[...]), value_e, value_o, True)

    for pair in range(HEADS // 2):
        lanes = pl.ds(pair * 2 * head_size, 2 * head_size)
        double = pl.ds(pair * 4 * head_size, 4 * head_size)
        mixed[:, lanes] = pair_attention(
            query[:, lanes],
            (key_e[:, lanes], key_o[:, lanes]),
            (value_e[:, double], value_o[:, double]),
            factor,
        )
    for copy in copies[3:]:
        copy.wait()
    added = jnp.dot(mixed[...], w_out[...], preferred_element_type=jnp.float32)
    for b in range(count):
        at = pl.ds(b * agents, agents)
        own = blocks[b][...].astype(jnp.float32) + added[b * agents : (b + 1) * agents]
        after[at, :] = own.astype(jnp.bfloat16)
        normed[at, :] = norm_of(after[at, :].astype(jnp.float32))
    hidden = w_in.shape[1]
    for start in range(0, hidden, features):
        inner[:, pl.ds(start, features)] = gelu(
            jnp.dot(
                normed[...], w_in[:, pl.ds(start, features)], preferred_element_type=jnp.float32
            )
        ).astype(jnp.bfloat16)
    final = after[...].astype(jnp.float32) + jnp.dot(
        inner[...], w_mlp_out[...], preferred_element_type=jnp.float32
    )
    for b in range(count):
        outs[b][...] = final[b * agents : (b + 1) * agents].astype(jnp.bfloat16)


def agent_kernel(count, middle_only, *refs):
    blocks, weights = refs[:count], refs[count : count + 6]
    outs, scratch = refs[-16 - count : -16], refs[-16:]

    def run():
        agent_body(count, blocks, weights, outs, scratch)

    if middle_only:
        plane = lax.axis_index("agent")
        pl.when(jnp.logical_or(plane == 1, plane == 2))(run)
    else:
        run()


def agent_stage(blocks, weights, middle_only, after=()):
    count = len(blocks)
    agents, features = blocks[0].shape
    hidden = weights[4].shape[1]
    rows = count * agents
    kind = jnp.bfloat16
    return pl.pallas_call(
        functools.partial(agent_kernel, count, middle_only),
        out_shape=[jax.ShapeDtypeStruct((agents, features), kind)] * count,
        in_specs=[spec(VMEM)] * count + [spec(HBM)] * 6 + [spec(pl.ANY)] * len(after),
        out_specs=[spec(VMEM)] * count,
        scratch_shapes=[VMEM((rows, features), kind)] * 4
        + [VMEM((rows, 2 * features), kind)] * 2
        + [VMEM((rows, features), kind)] * 2
        + [VMEM((rows, hidden), kind)]
        + [VMEM(w.shape, kind) for w in weights]
        + [pltpu.SemaphoreType.DMA((6,))],
        compiler_params=pltpu.CompilerParams(vmem_limit_bytes=28 * 2**20),
        name="agent_step",
    )(*blocks, *weights, *after)


def place_kernel(*refs):
    whole, extra, out, sems = refs[:4], refs[4:8], refs[8], refs[9]
    plane = lax.axis_index("agent")
    middle = jnp.logical_or(plane == 1, plane == 2)
    low = plane // 2
    copies = [
        pltpu.make_async_copy(source, out.at[jnp.bitwise_xor(plane, k)], sems.at[k])
        for k, source in enumerate(whole)
    ]
    inner = [
        pltpu.make_async_copy(extra[0], out.at[4 + low], sems.at[4]),
        pltpu.make_async_copy(extra[3], out.at[5 - low], sems.at[5]),
    ]
    outer = [
        pltpu.make_async_copy(extra[1], out.at[4 + low], sems.at[4]),
        pltpu.make_async_copy(extra[2], out.at[5 - low], sems.at[5]),
    ]
    for copy in copies:
        copy.start()

    @pl.when(middle)
    def _():
        for copy in inner:
            copy.start()
        for copy in inner:
            copy.wait()

    @pl.when(jnp.logical_not(middle))
    def _():
        for copy in outer:
            copy.start()
        for copy in outer:
            copy.wait()

    for copy in copies:
        copy.wait()


def place_stage(whole, extra):
    agents, features = whole[0].shape
    return pl.pallas_call(
        place_kernel,
        out_shape=jax.ShapeDtypeStruct((6, agents, features), jnp.bfloat16),
        in_specs=[spec(pl.ANY)] * 8,
        out_specs=spec(pl.ANY),
        scratch_shapes=[pltpu.SemaphoreType.DMA((6,))],
        name="place_steps",
    )(*whole, *extra)


def xor_pairs(size, k, targets=None):
    return [(j, j ^ k) for j in range(size) if targets is None or j ^ k in targets]


def exchange(parts, axis, targets=None):
    size = len(parts)
    return [parts[0]] + [
        lax.ppermute(parts[k], axis, xor_pairs(size, k, targets)) for k in range(1, size)
    ]


def picked(plane, values):
    result = jnp.int32(values[0])
    for place in range(1, len(values)):
        result = jnp.where(plane == place, values[place], result)
    return result


def whole_steps(plane):
    return [jnp.bitwise_xor(plane, k) for k in range(4)]


def extra_steps(plane):
    return [
        4 + picked(plane, (0, 0, 1, 0)),
        4 + picked(plane, (0, 0, 0, 1)),
        4 + picked(plane, (1, 0, 0, 0)),
        4 + picked(plane, (0, 1, 0, 0)),
    ]


def local(
    states,
    neighbours,
    w_query_t,
    w_key_t,
    w_value_t,
    w_out_t,
    w_query_a,
    w_key_a,
    w_value_a,
    w_out_a,
    w_in,
    w_mlp_out,
):
    local_steps, local_agents, features = states.shape
    size, planes = lax.axis_size("tm"), lax.axis_size("agent")
    share = local_agents // size
    time_weights = (w_query_t, w_key_t, w_value_t, w_out_t)
    agent_weights = (w_query_a, w_key_a, w_value_a, w_out_a, w_in, w_mlp_out)
    fits = (
        size & (size - 1) == 0
        and share * size == local_agents
        and share % 16 == 0
        and planes == 4
        and neighbours.shape == (4, 4)
        and local_steps == 6
    )
    if not fits:
        after_time = general_time(states, *time_weights)
        return general_agent(after_time, neighbours, *agent_weights)

    me, plane = lax.axis_index("tm"), lax.axis_index("agent")
    parts = [
        lax.dynamic_slice_in_dim(states, jnp.bitwise_xor(me, k) * share, share, 1)
        for k in range(size)
    ]
    pieces = exchange(parts, "tm")
    pieces = exchange(time_stage(pieces, time_weights), "tm")
    packed_a = pack_stage(pieces, whole_steps)
    packed_b = pack_stage(pieces, extra_steps, packed_a[:1])
    blocks_a = exchange(packed_a, "agent")
    blocks_b = exchange(packed_b, "agent", (1, 2))
    result_a = agent_stage(blocks_a, agent_weights, False)
    done_a = exchange(result_a, "agent")
    result_b = agent_stage(blocks_b, agent_weights, True, result_a[:1])
    done_b = [result_b[0]] + [
        lax.ppermute(result_b[k], "agent", [(j, j ^ k) for j in (1, 2)]) for k in range(1, 4)
    ]
    return place_stage(done_a, done_b)


def solution(mesh):
    placed = (P("tm", "agent", None), P(), P(), P(), P(), P(), P(), P(), P(), P(), P(), P())
    return jax.shard_map(
        local, mesh=mesh, in_specs=placed, out_specs=P("tm", "agent", None), check_vma=False
    )
```

```python
import functools
import math

import jax
import jax.numpy as jnp
from jax import lax
from jax.experimental import pallas as pl
from jax.experimental.pallas import tpu as pltpu
from jax.sharding import PartitionSpec as P

HEADS = 8


negative_floor = -1e30
epsilon = 1e-06


def rms_normed(values):
    wide = values.astype(jnp.float32)
    scale = lax.rsqrt(jnp.mean(wide * wide, axis=-1, keepdims=True) + epsilon)
    return (wide * scale).astype(jnp.bfloat16)


def project(normed, weight):
    return jnp.dot(normed, weight, preferred_element_type=jnp.float32).astype(jnp.bfloat16)


def attend(query, keys, values, allowed):
    batch, query_len, features = query.shape
    key_len = keys.shape[1]
    head_size = features // HEADS
    query_h = query.reshape(batch, query_len, HEADS, head_size)
    keys_h = keys.reshape(batch, key_len, HEADS, head_size)
    values_h = values.reshape(batch, key_len, HEADS, head_size)
    scores = jnp.einsum(
        "bqhe,bkhe->bhqk", query_h, keys_h, preferred_element_type=jnp.float32
    ) * head_size ** (-0.5)
    scores = jnp.where(allowed[:, None], scores, negative_floor)
    largest = jnp.max(scores, axis=-1, keepdims=True)
    weights = jnp.where(allowed[:, None], jnp.exp(scores - largest), 0.0)
    totals = jnp.sum(weights, axis=-1)
    summed = jnp.einsum(
        "bhqk,bkhe->bqhe",
        weights.astype(jnp.bfloat16),
        values_h,
        preferred_element_type=jnp.float32,
    )
    result = summed / jnp.transpose(totals, (0, 2, 1))[..., None]
    return result.reshape(batch, query_len, features).astype(jnp.bfloat16)


def general_time(states, w_query_t, w_key_t, w_value_t, w_out_t):
    local_steps = states.shape[0]
    normed = rms_normed(states)
    query = jnp.swapaxes(project(normed, w_query_t), 0, 1)
    keys = lax.all_gather(project(normed, w_key_t), "tm", axis=0, tiled=True)
    values = lax.all_gather(project(normed, w_value_t), "tm", axis=0, tiled=True)
    query_time = lax.axis_index("tm") * local_steps + jnp.arange(local_steps)
    allowed = (jnp.arange(keys.shape[0])[None, :] <= query_time[:, None])[None]
    mixed = attend(query, jnp.swapaxes(keys, 0, 1), jnp.swapaxes(values, 0, 1), allowed)
    return (
        states.astype(jnp.float32)
        + jnp.dot(jnp.swapaxes(mixed, 0, 1), w_out_t, preferred_element_type=jnp.float32)
    ).astype(jnp.bfloat16)


def general_agent(
    after_time, neighbours, w_query_a, w_key_a, w_value_a, w_out_a, w_in, w_mlp_out
):
    local_steps, local_agents, features = after_time.shape
    second_normed = rms_normed(after_time)
    agent_query = project(second_normed, w_query_a)
    block_count = lax.axis_size("agent")
    chosen_blocks = lax.dynamic_slice_in_dim(neighbours, lax.axis_index("agent"), 1, 0)[0]
    neighbour_count = neighbours.shape[1]
    everyone = lax.all_gather(second_normed, "agent", axis=1, tiled=True)
    picked = jnp.take(
        everyone.reshape(local_steps, block_count, local_agents, features), chosen_blocks, axis=1
    )
    picked = picked.reshape(local_steps, neighbour_count * local_agents, features)
    agent_key = project(picked, w_key_a)
    agent_value = project(picked, w_value_a)
    allowed_all = jnp.ones((1, local_agents, neighbour_count * local_agents), dtype=bool)
    agent_mixed = attend(agent_query, agent_key, agent_value, allowed_all)
    after_agent = (
        after_time.astype(jnp.float32)
        + jnp.dot(agent_mixed, w_out_a, preferred_element_type=jnp.float32)
    ).astype(jnp.bfloat16)
    inner = jax.nn.gelu(
        jnp.dot(rms_normed(after_agent), w_in, preferred_element_type=jnp.float32), approximate=True
    ).astype(jnp.bfloat16)
    final = after_agent.astype(jnp.float32) + jnp.dot(
        inner, w_mlp_out, preferred_element_type=jnp.float32
    )
    return final.astype(jnp.bfloat16)


NT = (((1,), (1,)), ((), ()))
VMEM, HBM = pltpu.VMEM, pltpu.HBM


def spec(space):
    return pl.BlockSpec(memory_space=space)


def norm_of(wide):
    scale = lax.rsqrt(jnp.mean(wide * wide, axis=-1, keepdims=True) + epsilon)
    return (wide * scale).astype(jnp.bfloat16)


def gelu(x):
    inside = x * (math.sqrt(2 / math.pi) + (math.sqrt(2 / math.pi) * 0.044715) * (x * x))
    half = 0.5 * x
    return half + half * jnp.tanh(inside)


def in_hbm(weights):
    return [pltpu.with_memory_space_constraint(w, HBM) for w in weights]


def fetch(sources, targets, sems):
    copies = [
        pltpu.make_async_copy(source, target, sems.at[k])
        for k, (source, target) in enumerate(zip(sources, targets))
    ]
    for copy in copies:
        copy.start()
    return copies


def split_heads(values, even, odd, ones=False):
    width = values.shape[1]
    for pair in range(HEADS // 2):
        wide = width // (HEADS // 2)
        own = values[:, pair * wide : (pair + 1) * wide]
        first = lax.broadcasted_iota(jnp.int32, own.shape, 1) < wide // 2
        zero = jnp.zeros_like(own)
        if ones:
            one = jnp.ones_like(own)
            at = 2 * pair * wide
            even[:, at : at + wide] = jnp.where(first, own, zero)
            odd[:, at : at + wide] = jnp.where(first, zero, own)
            even[:, at + wide : at + 2 * wide] = jnp.where(first, one, zero)
            odd[:, at + wide : at + 2 * wide] = jnp.where(first, zero, one)
        else:
            at = pair * wide
            even[:, at : at + wide] = jnp.where(first, own, zero)
            odd[:, at : at + wide] = jnp.where(first, zero, own)


def pair_attention(query, keys, values, factor, bias=None):
    sums = None
    for key, value in zip(keys, values):
        scores = lax.dot_general(query, key, NT, preferred_element_type=jnp.float32)
        if bias is not None:
            scores = scores + bias
        largest = jnp.max(scores, axis=-1, keepdims=True)
        weights = jnp.exp2((scores - largest) * factor).astype(jnp.bfloat16)
        part = jnp.dot(weights, value, preferred_element_type=jnp.float32)
        sums = part if sums is None else sums + part
    wide = query.shape[1]
    return (sums[:, :wide] / sums[:, wide:]).astype(jnp.bfloat16)


def time_kernel(size, *refs):
    pieces, weights = refs[:size], refs[size : size + 4]
    outs = refs[size + 4 : 2 * size + 4]
    wide, normed, query, key_e, key_o, value_e, value_o, mixed = refs[2 * size + 4 : 2 * size + 12]
    w_query, w_key, w_value, w_out, sems = refs[2 * size + 12 :]
    copies = fetch(weights, (w_query, w_key, w_value, w_out), sems)
    steps, agents, features = pieces[0].shape
    rows = steps * agents
    total_steps = steps * size
    me = lax.axis_index("tm")
    lanes_of = [slice(c * 128, (c + 1) * 128) for c in range(features // 128)]
    for k in range(size):
        start = pl.multiple_of(jnp.bitwise_xor(me, k) * rows, rows)
        piece = pieces[k][...].reshape(rows, features).astype(jnp.float32)
        for c, lanes in enumerate(lanes_of):
            wide[c, pl.ds(start, rows), :] = piece[:, lanes]
    for agent in range(agents):
        at = pl.ds(agent, total_steps, stride=agents)
        own = jnp.concatenate([wide[c, at, :] for c in range(len(lanes_of))], axis=1)
        normed[pl.ds(agent * total_steps, total_steps), :] = norm_of(own)
    copies[0].wait()
    query[...] = project(normed[...], w_query[...])
    copies[1].wait()
    split_heads(project(normed[...], w_key[...]), key_e, key_o)
    copies[2].wait()
    split_heads(project(normed[...], w_value[...]), value_e, value_o, True)

    group = 2 * total_steps
    row = lax.broadcasted_iota(jnp.int32, (group, group), 0)
    column = lax.broadcasted_iota(jnp.int32, (group, group), 1)
    same = (row >= total_steps) == (column >= total_steps)
    bias = jnp.where(jnp.logical_and(same, column <= row), 0.0, negative_floor)
    head_size = features // HEADS
    factor = math.log2(math.e) * head_size**-0.5

    def one_group(g, carry):
        at = pl.ds(pl.multiple_of(g * group, group), group)
        for pair in range(HEADS // 2):
            lanes = pl.ds(pair * 2 * head_size, 2 * head_size)
            double = pl.ds(pair * 4 * head_size, 4 * head_size)
            mixed[at, lanes] = pair_attention(
                query[at, lanes],
                (key_e[at, lanes], key_o[at, lanes]),
                (value_e[at, double], value_o[at, double]),
                factor,
                bias,
            )
        return carry

    lax.fori_loop(0, agents // 2, one_group, 0, unroll=True)
    copies[3].wait()
    added = jnp.dot(mixed[...], w_out[...], preferred_element_type=jnp.float32)
    for agent in range(agents):
        at = pl.ds(agent, total_steps, stride=agents)
        mine = added[agent * total_steps : (agent + 1) * total_steps]
        for c, lanes in enumerate(lanes_of):
            wide[c, at, :] = wide[c, at, :] + mine[:, lanes]
    for k in range(size):
        start = pl.multiple_of(jnp.bitwise_xor(me, k) * rows, rows)
        piece = jnp.concatenate(
            [wide[c, pl.ds(start, rows), :] for c in range(len(lanes_of))], axis=1
        )
        outs[k][...] = piece.astype(jnp.bfloat16).reshape(pieces[0].shape)


def time_stage(pieces, weights):
    size = len(pieces)
    steps, agents, features = pieces[0].shape
    rows = steps * agents * size
    kind = jnp.bfloat16
    return pl.pallas_call(
        functools.partial(time_kernel, size),
        out_shape=[jax.ShapeDtypeStruct((steps, agents, features), kind)] * size,
        in_specs=[spec(VMEM)] * size + [spec(HBM)] * 4,
        out_specs=[spec(VMEM)] * size,
        scratch_shapes=[VMEM((features // 128, rows, 128), jnp.float32)]
        + [VMEM((rows, features), kind)] * 4
        + [VMEM((rows, 2 * features), kind)] * 2
        + [VMEM((rows, features), kind)]
        + [VMEM(w.shape, kind) for w in weights]
        + [pltpu.SemaphoreType.DMA((4,))],
        compiler_params=pltpu.CompilerParams(vmem_limit_bytes=24 * 2**20),
        name="time_attention",
    )(*pieces, *in_hbm(weights))


def pack_kernel(size, choose, *refs):
    count = len(choose(0))
    pieces, outs = refs[:size], refs[len(refs) - count :]
    agents = pieces[0].shape[1]
    me, plane = lax.axis_index("tm"), lax.axis_index("agent")
    for out, step in zip(outs, choose(plane)):
        for k in range(size):
            start = pl.multiple_of(jnp.bitwise_xor(me, k) * agents, agents)
            out[pl.ds(start, agents), :] = pieces[k][step]


def pack_stage(pieces, choose, after=()):
    size, count = len(pieces), len(choose(0))
    _, agents, features = pieces[0].shape
    return pl.pallas_call(
        functools.partial(pack_kernel, size, choose),
        out_shape=[jax.ShapeDtypeStruct((agents * size, features), jnp.bfloat16)] * count,
        in_specs=[spec(VMEM)] * size + [spec(pl.ANY)] * len(after),
        out_specs=[spec(VMEM)] * count,
        compiler_params=pltpu.CompilerParams(vmem_limit_bytes=8 * 2**20),
        name="pack_steps",
    )(*pieces, *after)


def agent_body(count, blocks, weights, outs, scratch):
    normed, query, key_e, key_o, value_e, value_o, mixed, after, inner, w_out, sems = scratch
    w_query, w_key, w_value, far_out, w_in, w_mlp_out = weights
    copies = fetch((far_out,), (w_out,), sems)
    agents, features = blocks[0].shape
    head_size = features // HEADS
    factor = math.log2(math.e) * head_size**-0.5
    for b in range(count):
        normed[pl.ds(b * agents, agents), :] = norm_of(blocks[b][...].astype(jnp.float32))
    query[...] = project(normed[...], w_query[...])
    split_heads(project(normed[...], w_key[...]), key_e, key_o)
    split_heads(project(normed[...], w_value[...]), value_e, value_o, True)

    for pair in range(HEADS // 2):
        lanes = pl.ds(pair * 2 * head_size, 2 * head_size)
        double = pl.ds(pair * 4 * head_size, 4 * head_size)
        mixed[:, lanes] = pair_attention(
            query[:, lanes],
            (key_e[:, lanes], key_o[:, lanes]),
            (value_e[:, double], value_o[:, double]),
            factor,
        )
    copies[0].wait()
    added = jnp.dot(mixed[...], w_out[...], preferred_element_type=jnp.float32)
    for b in range(count):
        at = pl.ds(b * agents, agents)
        own = blocks[b][...].astype(jnp.float32) + added[b * agents : (b + 1) * agents]
        after[at, :] = own.astype(jnp.bfloat16)
        normed[at, :] = norm_of(after[at, :].astype(jnp.float32))
    hidden = w_in.shape[1]
    for start in range(0, hidden, features):
        inner[:, pl.ds(start, features)] = gelu(
            jnp.dot(
                normed[...], w_in[:, pl.ds(start, features)], preferred_element_type=jnp.float32
            )
        ).astype(jnp.bfloat16)
    final = after[...].astype(jnp.float32) + jnp.dot(
        inner[...], w_mlp_out[...], preferred_element_type=jnp.float32
    )
    for b in range(count):
        outs[b][...] = final[b * agents : (b + 1) * agents].astype(jnp.bfloat16)


def agent_kernel(count, middle_only, *refs):
    blocks, weights = refs[:count], refs[count : count + 6]
    outs, scratch = refs[-11 - count : -11], refs[-11:]

    def run():
        agent_body(count, blocks, weights, outs, scratch)

    if middle_only:
        plane = lax.axis_index("agent")
        pl.when(jnp.logical_or(plane == 1, plane == 2))(run)
    else:
        run()


def agent_stage(blocks, weights, middle_only, after=()):
    count = len(blocks)
    agents, features = blocks[0].shape
    hidden = weights[4].shape[1]
    rows = count * agents
    kind = jnp.bfloat16
    return pl.pallas_call(
        functools.partial(agent_kernel, count, middle_only),
        out_shape=[jax.ShapeDtypeStruct((agents, features), kind)] * count,
        in_specs=[spec(VMEM)] * (count + 3)
        + [spec(HBM)]
        + [spec(VMEM)] * 2
        + [spec(pl.ANY)] * len(after),
        out_specs=[spec(VMEM)] * count,
        scratch_shapes=[VMEM((rows, features), kind)] * 4
        + [VMEM((rows, 2 * features), kind)] * 2
        + [VMEM((rows, features), kind)] * 2
        + [VMEM((rows, hidden), kind)]
        + [VMEM(weights[3].shape, kind), pltpu.SemaphoreType.DMA((1,))],
        compiler_params=pltpu.CompilerParams(vmem_limit_bytes=20 * 2**20),
        name="agent_step",
    )(*blocks, *weights[:3], *in_hbm(weights[3:4]), *weights[4:], *after)


def place_kernel(*refs):
    whole, extra, out, sems = refs[:4], refs[4:8], refs[8], refs[9]
    plane = lax.axis_index("agent")
    middle = jnp.logical_or(plane == 1, plane == 2)
    low = plane // 2
    copies = [
        pltpu.make_async_copy(source, out.at[jnp.bitwise_xor(plane, k)], sems.at[k])
        for k, source in enumerate(whole)
    ]
    inner = [
        pltpu.make_async_copy(extra[0], out.at[4 + low], sems.at[4]),
        pltpu.make_async_copy(extra[3], out.at[5 - low], sems.at[5]),
    ]
    outer = [
        pltpu.make_async_copy(extra[1], out.at[4 + low], sems.at[4]),
        pltpu.make_async_copy(extra[2], out.at[5 - low], sems.at[5]),
    ]
    for copy in copies:
        copy.start()

    @pl.when(middle)
    def _():
        for copy in inner:
            copy.start()
        for copy in inner:
            copy.wait()

    @pl.when(jnp.logical_not(middle))
    def _():
        for copy in outer:
            copy.start()
        for copy in outer:
            copy.wait()

    for copy in copies:
        copy.wait()


def place_stage(whole, extra):
    agents, features = whole[0].shape
    return pl.pallas_call(
        place_kernel,
        out_shape=jax.ShapeDtypeStruct((6, agents, features), jnp.bfloat16),
        in_specs=[spec(VMEM)] * 8,
        out_specs=spec(HBM),
        scratch_shapes=[pltpu.SemaphoreType.DMA((6,))],
        name="place_steps",
    )(*whole, *extra)


def xor_pairs(size, k, targets=None):
    return [(j, j ^ k) for j in range(size) if targets is None or j ^ k in targets]


def exchange(parts, axis, targets=None):
    size = len(parts)
    return [parts[0]] + [
        lax.ppermute(parts[k], axis, xor_pairs(size, k, targets)) for k in range(1, size)
    ]


def together(parts):
    return lax.optimization_barrier(tuple(parts))


def picked(plane, values):
    result = jnp.int32(values[0])
    for place in range(1, len(values)):
        result = jnp.where(plane == place, values[place], result)
    return result


def whole_steps(plane):
    return [jnp.bitwise_xor(plane, k) for k in range(4)]


def extra_steps(plane):
    return [
        4 + picked(plane, (0, 0, 1, 0)),
        4 + picked(plane, (0, 0, 0, 1)),
        4 + picked(plane, (1, 0, 0, 0)),
        4 + picked(plane, (0, 1, 0, 0)),
    ]


def local(
    states,
    neighbours,
    w_query_t,
    w_key_t,
    w_value_t,
    w_out_t,
    w_query_a,
    w_key_a,
    w_value_a,
    w_out_a,
    w_in,
    w_mlp_out,
):
    local_steps, local_agents, features = states.shape
    size, planes = lax.axis_size("tm"), lax.axis_size("agent")
    share = local_agents // size
    time_weights = (w_query_t, w_key_t, w_value_t, w_out_t)
    agent_weights = (w_query_a, w_key_a, w_value_a, w_out_a, w_in, w_mlp_out)
    fits = (
        size & (size - 1) == 0
        and share * size == local_agents
        and share % 16 == 0
        and planes == 4
        and neighbours.shape == (4, 4)
        and local_steps == 6
    )
    if not fits:
        after_time = general_time(states, *time_weights)
        return general_agent(after_time, neighbours, *agent_weights)

    me, plane = lax.axis_index("tm"), lax.axis_index("agent")
    parts = [
        lax.dynamic_slice_in_dim(states, jnp.bitwise_xor(me, k) * share, share, 1)
        for k in range(size)
    ]
    pieces = together(exchange(parts, "tm"))
    pieces = together(exchange(time_stage(pieces, time_weights), "tm"))
    blocks_a = exchange(pack_stage(pieces, whole_steps), "agent")
    blocks_b = exchange(pack_stage(pieces, extra_steps, blocks_a[2:3]), "agent", (1, 2))
    result_a = agent_stage(blocks_a, agent_weights, False)
    done_a = exchange(result_a, "agent")
    result_b = agent_stage(blocks_b, agent_weights, True, result_a[:1])
    done_b = [result_b[0]] + [
        lax.ppermute(result_b[k], "agent", [(j, j ^ k) for j in (1, 2)]) for k in range(1, 4)
    ]
    return place_stage(done_a, done_b)


def solution(mesh):
    placed = (P("tm", "agent", None), P(), P(), P(), P(), P(), P(), P(), P(), P(), P(), P())
    return jax.shard_map(
        local, mesh=mesh, in_specs=placed, out_specs=P("tm", "agent", None), check_vma=False
    )
```

```python
import functools
import math

import jax
import jax.numpy as jnp
from jax import lax
from jax.experimental import pallas as pl
from jax.experimental.pallas import tpu as pltpu
from jax.sharding import PartitionSpec as P

HEADS = 8


negative_floor = -1e30
epsilon = 1e-06


def rms_normed(values):
    wide = values.astype(jnp.float32)
    scale = lax.rsqrt(jnp.mean(wide * wide, axis=-1, keepdims=True) + epsilon)
    return (wide * scale).astype(jnp.bfloat16)


def project(normed, weight):
    return jnp.dot(normed, weight, preferred_element_type=jnp.float32).astype(jnp.bfloat16)


def attend(query, keys, values, allowed):
    batch, query_len, features = query.shape
    key_len = keys.shape[1]
    head_size = features // HEADS
    query_h = query.reshape(batch, query_len, HEADS, head_size)
    keys_h = keys.reshape(batch, key_len, HEADS, head_size)
    values_h = values.reshape(batch, key_len, HEADS, head_size)
    scores = jnp.einsum(
        "bqhe,bkhe->bhqk", query_h, keys_h, preferred_element_type=jnp.float32
    ) * head_size ** (-0.5)
    scores = jnp.where(allowed[:, None], scores, negative_floor)
    largest = jnp.max(scores, axis=-1, keepdims=True)
    weights = jnp.where(allowed[:, None], jnp.exp(scores - largest), 0.0)
    totals = jnp.sum(weights, axis=-1)
    summed = jnp.einsum(
        "bhqk,bkhe->bqhe",
        weights.astype(jnp.bfloat16),
        values_h,
        preferred_element_type=jnp.float32,
    )
    result = summed / jnp.transpose(totals, (0, 2, 1))[..., None]
    return result.reshape(batch, query_len, features).astype(jnp.bfloat16)


def general_time(states, w_query_t, w_key_t, w_value_t, w_out_t):
    local_steps = states.shape[0]
    normed = rms_normed(states)
    query = jnp.swapaxes(project(normed, w_query_t), 0, 1)
    keys = lax.all_gather(project(normed, w_key_t), "tm", axis=0, tiled=True)
    values = lax.all_gather(project(normed, w_value_t), "tm", axis=0, tiled=True)
    query_time = lax.axis_index("tm") * local_steps + jnp.arange(local_steps)
    allowed = (jnp.arange(keys.shape[0])[None, :] <= query_time[:, None])[None]
    mixed = attend(query, jnp.swapaxes(keys, 0, 1), jnp.swapaxes(values, 0, 1), allowed)
    return (
        states.astype(jnp.float32)
        + jnp.dot(jnp.swapaxes(mixed, 0, 1), w_out_t, preferred_element_type=jnp.float32)
    ).astype(jnp.bfloat16)


def general_agent(
    after_time, neighbours, w_query_a, w_key_a, w_value_a, w_out_a, w_in, w_mlp_out
):
    local_steps, local_agents, features = after_time.shape
    second_normed = rms_normed(after_time)
    agent_query = project(second_normed, w_query_a)
    block_count = lax.axis_size("agent")
    chosen_blocks = lax.dynamic_slice_in_dim(neighbours, lax.axis_index("agent"), 1, 0)[0]
    neighbour_count = neighbours.shape[1]
    everyone = lax.all_gather(second_normed, "agent", axis=1, tiled=True)
    picked = jnp.take(
        everyone.reshape(local_steps, block_count, local_agents, features), chosen_blocks, axis=1
    )
    picked = picked.reshape(local_steps, neighbour_count * local_agents, features)
    agent_key = project(picked, w_key_a)
    agent_value = project(picked, w_value_a)
    allowed_all = jnp.ones((1, local_agents, neighbour_count * local_agents), dtype=bool)
    agent_mixed = attend(agent_query, agent_key, agent_value, allowed_all)
    after_agent = (
        after_time.astype(jnp.float32)
        + jnp.dot(agent_mixed, w_out_a, preferred_element_type=jnp.float32)
    ).astype(jnp.bfloat16)
    inner = jax.nn.gelu(
        jnp.dot(rms_normed(after_agent), w_in, preferred_element_type=jnp.float32), approximate=True
    ).astype(jnp.bfloat16)
    final = after_agent.astype(jnp.float32) + jnp.dot(
        inner, w_mlp_out, preferred_element_type=jnp.float32
    )
    return final.astype(jnp.bfloat16)


NT = (((1,), (1,)), ((), ()))
VMEM, HBM = pltpu.VMEM, pltpu.HBM


def spec(space):
    return pl.BlockSpec(memory_space=space)


def norm_of(wide):
    scale = lax.rsqrt(jnp.mean(wide * wide, axis=-1, keepdims=True) + epsilon)
    return (wide * scale).astype(jnp.bfloat16)


def gelu(x):
    inside = x * (math.sqrt(2 / math.pi) + (math.sqrt(2 / math.pi) * 0.044715) * (x * x))
    half = 0.5 * x
    return half + half * jnp.tanh(inside)


def in_hbm(weights):
    return [pltpu.with_memory_space_constraint(w, HBM) for w in weights]


def fetch(sources, targets, sems):
    copies = [
        pltpu.make_async_copy(source, target, sems.at[k])
        for k, (source, target) in enumerate(zip(sources, targets))
    ]
    for copy in copies:
        copy.start()
    return copies


def split_heads(values, even, odd, ones=False):
    width = values.shape[1]
    for pair in range(HEADS // 2):
        wide = width // (HEADS // 2)
        own = values[:, pair * wide : (pair + 1) * wide]
        first = lax.broadcasted_iota(jnp.int32, own.shape, 1) < wide // 2
        zero = jnp.zeros_like(own)
        if ones:
            one = jnp.ones_like(own)
            at = 2 * pair * wide
            even[:, at : at + wide] = jnp.where(first, own, zero)
            odd[:, at : at + wide] = jnp.where(first, zero, own)
            even[:, at + wide : at + 2 * wide] = jnp.where(first, one, zero)
            odd[:, at + wide : at + 2 * wide] = jnp.where(first, zero, one)
        else:
            at = pair * wide
            even[:, at : at + wide] = jnp.where(first, own, zero)
            odd[:, at : at + wide] = jnp.where(first, zero, own)


def pair_attention(query, keys, values, factor, bias=None):
    sums = None
    for key, value in zip(keys, values):
        scores = lax.dot_general(query, key, NT, preferred_element_type=jnp.float32)
        if bias is not None:
            scores = scores + bias
        largest = jnp.max(scores, axis=-1, keepdims=True)
        weights = jnp.exp2((scores - largest) * factor).astype(jnp.bfloat16)
        part = jnp.dot(weights, value, preferred_element_type=jnp.float32)
        sums = part if sums is None else sums + part
    wide = query.shape[1]
    return (sums[:, :wide] / sums[:, wide:]).astype(jnp.bfloat16)


def share_kernel(size, *refs):
    states, outs, sems = refs[0], refs[1 : size + 1], refs[size + 1]
    agents = outs[0].shape[1]
    me = lax.axis_index("tm")
    copies = []
    for k, out in enumerate(outs):
        at = pl.ds(pl.multiple_of(jnp.bitwise_xor(me, k) * agents, agents), agents)
        copies.append(pltpu.make_async_copy(states.at[:, at, :], out, sems.at[k]))
    for copy in copies:
        copy.start()
    for copy in copies:
        copy.wait()


def share_stage(states, size):
    steps, agents, features = states.shape
    shape = jax.ShapeDtypeStruct((steps, agents // size, features), states.dtype)
    return pl.pallas_call(
        functools.partial(share_kernel, size),
        out_shape=[shape] * size,
        in_specs=[spec(HBM)],
        out_specs=[spec(VMEM)] * size,
        scratch_shapes=[pltpu.SemaphoreType.DMA((size,))],
        compiler_params=pltpu.CompilerParams(vmem_limit_bytes=4 * 2**20),
        cost_estimate=pl.CostEstimate(flops=2 * 10**10, bytes_accessed=10**7, transcendentals=0),
        name="cut_shares",
    )(*in_hbm([states]))


def time_kernel(size, *refs):
    pieces, weights = refs[:size], refs[size : size + 4]
    outs = refs[size + 4 : 2 * size + 4]
    wide, normed, query, key_e, key_o, value_e, value_o, mixed = refs[2 * size + 4 : 2 * size + 12]
    w_query, w_key, w_value, w_out = weights
    steps, agents, features = pieces[0].shape
    rows = steps * agents
    total_steps = steps * size
    me = lax.axis_index("tm")
    lanes_of = [slice(c * 128, (c + 1) * 128) for c in range(features // 128)]
    for k in range(size):
        start = pl.multiple_of(jnp.bitwise_xor(me, k) * rows, rows)
        piece = pieces[k][...].reshape(rows, features).astype(jnp.float32)
        for c, lanes in enumerate(lanes_of):
            wide[c, pl.ds(start, rows), :] = piece[:, lanes]
    for agent in range(agents):
        at = pl.ds(agent, total_steps, stride=agents)
        own = jnp.concatenate([wide[c, at, :] for c in range(len(lanes_of))], axis=1)
        normed[pl.ds(agent * total_steps, total_steps), :] = norm_of(own)
    query[...] = project(normed[...], w_query[...])
    split_heads(project(normed[...], w_key[...]), key_e, key_o)
    split_heads(project(normed[...], w_value[...]), value_e, value_o, True)

    group = 2 * total_steps
    row = lax.broadcasted_iota(jnp.int32, (group, group), 0)
    column = lax.broadcasted_iota(jnp.int32, (group, group), 1)
    same = (row >= total_steps) == (column >= total_steps)
    bias = jnp.where(jnp.logical_and(same, column <= row), 0.0, negative_floor)
    head_size = features // HEADS
    factor = math.log2(math.e) * head_size**-0.5

    def one_group(g, carry):
        at = pl.ds(pl.multiple_of(g * group, group), group)
        for pair in range(HEADS // 2):
            lanes = pl.ds(pair * 2 * head_size, 2 * head_size)
            double = pl.ds(pair * 4 * head_size, 4 * head_size)
            mixed[at, lanes] = pair_attention(
                query[at, lanes],
                (key_e[at, lanes], key_o[at, lanes]),
                (value_e[at, double], value_o[at, double]),
                factor,
                bias,
            )
        return carry

    lax.fori_loop(0, agents // 2, one_group, 0, unroll=True)
    added = jnp.dot(mixed[...], w_out[...], preferred_element_type=jnp.float32)
    for agent in range(agents):
        at = pl.ds(agent, total_steps, stride=agents)
        mine = added[agent * total_steps : (agent + 1) * total_steps]
        for c, lanes in enumerate(lanes_of):
            wide[c, at, :] = wide[c, at, :] + mine[:, lanes]
    for k in range(size):
        start = pl.multiple_of(jnp.bitwise_xor(me, k) * rows, rows)
        piece = jnp.concatenate(
            [wide[c, pl.ds(start, rows), :] for c in range(len(lanes_of))], axis=1
        )
        outs[k][...] = piece.astype(jnp.bfloat16).reshape(pieces[0].shape)


def time_stage(pieces, weights):
    size = len(pieces)
    steps, agents, features = pieces[0].shape
    rows = steps * agents * size
    kind = jnp.bfloat16
    return pl.pallas_call(
        functools.partial(time_kernel, size),
        out_shape=[jax.ShapeDtypeStruct((steps, agents, features), kind)] * size,
        in_specs=[spec(VMEM)] * (size + 4),
        out_specs=[spec(VMEM)] * size,
        scratch_shapes=[VMEM((features // 128, rows, 128), jnp.float32)]
        + [VMEM((rows, features), kind)] * 4
        + [VMEM((rows, 2 * features), kind)] * 2
        + [VMEM((rows, features), kind)],
        compiler_params=pltpu.CompilerParams(vmem_limit_bytes=24 * 2**20),
        cost_estimate=pl.CostEstimate(
            flops=8 * rows * features * features,
            bytes_accessed=2 * (2 * rows + 4 * features) * features,
            transcendentals=rows * HEADS * steps * size,
        ),
        name="time_attention",
    )(*pieces, *weights)


def pack_kernel(size, choose, *refs):
    count = len(choose(0))
    pieces, outs = refs[:size], refs[len(refs) - count :]
    agents = pieces[0].shape[1]
    me, plane = lax.axis_index("tm"), lax.axis_index("agent")
    for out, step in zip(outs, choose(plane)):
        for k in range(size):
            start = pl.multiple_of(jnp.bitwise_xor(me, k) * agents, agents)
            out[pl.ds(start, agents), :] = pieces[k][step]


def pack_stage(pieces, choose, after=()):
    size, count = len(pieces), len(choose(0))
    _, agents, features = pieces[0].shape
    return pl.pallas_call(
        functools.partial(pack_kernel, size, choose),
        out_shape=[jax.ShapeDtypeStruct((agents * size, features), jnp.bfloat16)] * count,
        in_specs=[spec(VMEM)] * size + [spec(pl.ANY)] * len(after),
        out_specs=[spec(VMEM)] * count,
        compiler_params=pltpu.CompilerParams(vmem_limit_bytes=8 * 2**20),
        name="pack_steps",
    )(*pieces, *after)


def agent_body(count, blocks, weights, outs, scratch):
    normed, query, key_e, key_o, value_e, value_o, mixed, after, inner, w_out, sems = scratch
    w_query, w_key, w_value, far_out, w_in, w_mlp_out = weights
    copies = fetch((far_out,), (w_out,), sems)
    agents, features = blocks[0].shape
    head_size = features // HEADS
    factor = math.log2(math.e) * head_size**-0.5
    for b in range(count):
        normed[pl.ds(b * agents, agents), :] = norm_of(blocks[b][...].astype(jnp.float32))
    query[...] = project(normed[...], w_query[...])
    split_heads(project(normed[...], w_key[...]), key_e, key_o)
    split_heads(project(normed[...], w_value[...]), value_e, value_o, True)
    for pair in range(HEADS // 2):
        lanes = pl.ds(pair * 2 * head_size, 2 * head_size)
        double = pl.ds(pair * 4 * head_size, 4 * head_size)
        mixed[:, lanes] = pair_attention(
            query[:, lanes],
            (key_e[:, lanes], key_o[:, lanes]),
            (value_e[:, double], value_o[:, double]),
            factor,
        )
    copies[0].wait()
    added = jnp.dot(mixed[...], w_out[...], preferred_element_type=jnp.float32)
    for b in range(count):
        at = pl.ds(b * agents, agents)
        own = blocks[b][...].astype(jnp.float32) + added[b * agents : (b + 1) * agents]
        after[at, :] = own.astype(jnp.bfloat16)
        normed[at, :] = norm_of(after[at, :].astype(jnp.float32))
    hidden = w_in.shape[1]
    for start in range(0, hidden, features):
        inner[:, pl.ds(start, features)] = gelu(
            jnp.dot(
                normed[...], w_in[:, pl.ds(start, features)], preferred_element_type=jnp.float32
            )
        ).astype(jnp.bfloat16)
    final = after[...].astype(jnp.float32) + jnp.dot(
        inner[...], w_mlp_out[...], preferred_element_type=jnp.float32
    )
    for b in range(count):
        outs[b][...] = final[b * agents : (b + 1) * agents].astype(jnp.bfloat16)


def agent_kernel(count, middle_only, *refs):
    blocks, weights = refs[:count], refs[count : count + 6]
    outs, scratch = refs[-11 - count : -11], refs[-11:]

    def run():
        agent_body(count, blocks, weights, outs, scratch)

    if middle_only:
        plane = lax.axis_index("agent")
        pl.when(jnp.logical_or(plane == 1, plane == 2))(run)
    else:
        run()


def agent_stage(blocks, weights, middle_only, after=()):
    count = len(blocks)
    agents, features = blocks[0].shape
    hidden = weights[4].shape[1]
    rows = count * agents
    kind = jnp.bfloat16
    return pl.pallas_call(
        functools.partial(agent_kernel, count, middle_only),
        out_shape=[jax.ShapeDtypeStruct((agents, features), kind)] * count,
        in_specs=[spec(VMEM)] * (count + 3)
        + [spec(HBM)]
        + [spec(VMEM)] * 2
        + [spec(pl.ANY)] * len(after),
        out_specs=[spec(VMEM)] * count,
        scratch_shapes=[VMEM((rows, features), kind)] * 4
        + [VMEM((rows, 2 * features), kind)] * 2
        + [VMEM((rows, features), kind)] * 2
        + [VMEM((rows, hidden), kind)]
        + [VMEM(weights[3].shape, kind), pltpu.SemaphoreType.DMA((1,))],
        compiler_params=pltpu.CompilerParams(vmem_limit_bytes=16 * 2**20),
        cost_estimate=pl.CostEstimate(
            flops=2 * rows * features * (4 * features + 2 * hidden + 2 * rows),
            bytes_accessed=2 * rows * features * 8,
            transcendentals=rows * (HEADS * rows + hidden),
        ),
        name="agent_step",
    )(*blocks, *weights[:3], *in_hbm(weights[3:4]), *weights[4:], *after)


def place_kernel(*refs):
    sources, out, sems = refs[:4], refs[4], refs[5]
    plane = lax.axis_index("agent")
    copies = [
        pltpu.make_async_copy(source, out.at[jnp.bitwise_xor(plane, k)], sems.at[k])
        for k, source in enumerate(sources)
    ]
    for copy in copies:
        copy.start()
    for copy in copies:
        copy.wait()


def place_extra_kernel(*refs):
    sources, out, sems = refs[:4], refs[5], refs[6]
    plane = lax.axis_index("agent")
    middle = jnp.logical_or(plane == 1, plane == 2)
    low = plane // 2

    def place(one, other):
        copies = [
            pltpu.make_async_copy(one, out.at[4 + low], sems.at[0]),
            pltpu.make_async_copy(other, out.at[5 - low], sems.at[1]),
        ]
        for copy in copies:
            copy.start()
        for copy in copies:
            copy.wait()

    pl.when(middle)(lambda: place(sources[0], sources[3]))
    pl.when(jnp.logical_not(middle))(lambda: place(sources[1], sources[2]))


def place_stage(whole, extra):
    agents, features = whole[0].shape
    shape = jax.ShapeDtypeStruct((6, agents, features), jnp.bfloat16)
    begun = pl.pallas_call(
        place_kernel,
        out_shape=shape,
        in_specs=[spec(VMEM)] * 4,
        out_specs=spec(HBM),
        scratch_shapes=[pltpu.SemaphoreType.DMA((4,))],
        compiler_params=pltpu.CompilerParams(vmem_limit_bytes=4 * 2**20),
        name="place_steps",
    )(*whole)
    return pl.pallas_call(
        place_extra_kernel,
        out_shape=shape,
        in_specs=[spec(VMEM)] * 4 + [spec(HBM)],
        out_specs=spec(HBM),
        input_output_aliases={4: 0},
        scratch_shapes=[pltpu.SemaphoreType.DMA((2,))],
        compiler_params=pltpu.CompilerParams(vmem_limit_bytes=4 * 2**20),
        name="place_extra",
    )(*extra, begun)


def xor_pairs(size, k, targets=None):
    return [(j, j ^ k) for j in range(size) if targets is None or j ^ k in targets]


def exchange(parts, axis, targets=None, ordered=False):
    size = len(parts)
    moved = {}
    for k in range(size - 1, 0, -1):
        part = parts[k]
        if ordered and k == 1:
            part, moved[size - 1] = lax.optimization_barrier((part, moved[size - 1]))
        moved[k] = lax.ppermute(part, axis, xor_pairs(size, k, targets))
    return [parts[0]] + [moved[k] for k in range(1, size)]


def together(parts):
    return lax.optimization_barrier(tuple(parts))


def picked(plane, values):
    result = jnp.int32(values[0])
    for place in range(1, len(values)):
        result = jnp.where(plane == place, values[place], result)
    return result


def whole_steps(plane):
    return [jnp.bitwise_xor(plane, k) for k in range(4)]


def extra_steps(plane):
    return [
        4 + picked(plane, (0, 0, 1, 0)),
        4 + picked(plane, (0, 0, 0, 1)),
        4 + picked(plane, (1, 0, 0, 0)),
        4 + picked(plane, (0, 1, 0, 0)),
    ]


def local(
    states,
    neighbours,
    w_query_t,
    w_key_t,
    w_value_t,
    w_out_t,
    w_query_a,
    w_key_a,
    w_value_a,
    w_out_a,
    w_in,
    w_mlp_out,
):
    local_steps, local_agents, features = states.shape
    size, planes = lax.axis_size("tm"), lax.axis_size("agent")
    share = local_agents // size
    time_weights = (w_query_t, w_key_t, w_value_t, w_out_t)
    agent_weights = (w_query_a, w_key_a, w_value_a, w_out_a, w_in, w_mlp_out)
    fits = (
        size & (size - 1) == 0
        and share * size == local_agents
        and share % 16 == 0
        and planes == 4
        and neighbours.shape == (4, 4)
        and local_steps == 6
    )
    if not fits:
        after_time = general_time(states, *time_weights)
        return general_agent(after_time, neighbours, *agent_weights)

    pieces = together(exchange(share_stage(states, size), "tm", ordered=True))
    pieces = together(exchange(time_stage(pieces, time_weights), "tm", ordered=True))
    blocks_a = exchange(pack_stage(pieces, whole_steps), "agent")
    blocks_b = exchange(pack_stage(pieces, extra_steps, blocks_a[2:3]), "agent", (1, 2))

    result_a = agent_stage(blocks_a, agent_weights, False)
    done_a = exchange(result_a, "agent")
    result_b = agent_stage(blocks_b, agent_weights, True, result_a[:1])
    done_b = [result_b[0]] + [
        lax.ppermute(result_b[k], "agent", [(j, j ^ k) for j in (1, 2)]) for k in (1, 2, 3)
    ]
    return place_stage(done_a, done_b)


def solution(mesh):
    placed = (P("tm", "agent", None), P(), P(), P(), P(), P(), P(), P(), P(), P(), P(), P())
    return jax.shard_map(
        local, mesh=mesh, in_specs=placed, out_specs=P("tm", "agent", None), check_vma=False
    )
```

```python
import functools
import math

import jax
import jax.numpy as jnp
from jax import lax
from jax.experimental import pallas as pl
from jax.experimental.pallas import tpu as pltpu
from jax.sharding import PartitionSpec as P

HEADS = 8


negative_floor = -1e30
epsilon = 1e-06


def rms_normed(values):
    wide = values.astype(jnp.float32)
    scale = lax.rsqrt(jnp.mean(wide * wide, axis=-1, keepdims=True) + epsilon)
    return (wide * scale).astype(jnp.bfloat16)


def project(normed, weight):
    return jnp.dot(normed, weight, preferred_element_type=jnp.float32).astype(jnp.bfloat16)


def attend(query, keys, values, allowed):
    batch, query_len, features = query.shape
    key_len = keys.shape[1]
    head_size = features // HEADS
    query_h = query.reshape(batch, query_len, HEADS, head_size)
    keys_h = keys.reshape(batch, key_len, HEADS, head_size)
    values_h = values.reshape(batch, key_len, HEADS, head_size)
    scores = jnp.einsum(
        "bqhe,bkhe->bhqk", query_h, keys_h, preferred_element_type=jnp.float32
    ) * head_size ** (-0.5)
    scores = jnp.where(allowed[:, None], scores, negative_floor)
    largest = jnp.max(scores, axis=-1, keepdims=True)
    weights = jnp.where(allowed[:, None], jnp.exp(scores - largest), 0.0)
    totals = jnp.sum(weights, axis=-1)
    summed = jnp.einsum(
        "bhqk,bkhe->bqhe",
        weights.astype(jnp.bfloat16),
        values_h,
        preferred_element_type=jnp.float32,
    )
    result = summed / jnp.transpose(totals, (0, 2, 1))[..., None]
    return result.reshape(batch, query_len, features).astype(jnp.bfloat16)


def general_time(states, w_query_t, w_key_t, w_value_t, w_out_t):
    local_steps = states.shape[0]
    normed = rms_normed(states)
    query = jnp.swapaxes(project(normed, w_query_t), 0, 1)
    keys = lax.all_gather(project(normed, w_key_t), "tm", axis=0, tiled=True)
    values = lax.all_gather(project(normed, w_value_t), "tm", axis=0, tiled=True)
    query_time = lax.axis_index("tm") * local_steps + jnp.arange(local_steps)
    allowed = (jnp.arange(keys.shape[0])[None, :] <= query_time[:, None])[None]
    mixed = attend(query, jnp.swapaxes(keys, 0, 1), jnp.swapaxes(values, 0, 1), allowed)
    return (
        states.astype(jnp.float32)
        + jnp.dot(jnp.swapaxes(mixed, 0, 1), w_out_t, preferred_element_type=jnp.float32)
    ).astype(jnp.bfloat16)


def general_agent(
    after_time, neighbours, w_query_a, w_key_a, w_value_a, w_out_a, w_in, w_mlp_out
):
    local_steps, local_agents, features = after_time.shape
    second_normed = rms_normed(after_time)
    agent_query = project(second_normed, w_query_a)
    block_count = lax.axis_size("agent")
    chosen_blocks = lax.dynamic_slice_in_dim(neighbours, lax.axis_index("agent"), 1, 0)[0]
    neighbour_count = neighbours.shape[1]
    everyone = lax.all_gather(second_normed, "agent", axis=1, tiled=True)
    picked = jnp.take(
        everyone.reshape(local_steps, block_count, local_agents, features), chosen_blocks, axis=1
    )
    picked = picked.reshape(local_steps, neighbour_count * local_agents, features)
    agent_key = project(picked, w_key_a)
    agent_value = project(picked, w_value_a)
    allowed_all = jnp.ones((1, local_agents, neighbour_count * local_agents), dtype=bool)
    agent_mixed = attend(agent_query, agent_key, agent_value, allowed_all)
    after_agent = (
        after_time.astype(jnp.float32)
        + jnp.dot(agent_mixed, w_out_a, preferred_element_type=jnp.float32)
    ).astype(jnp.bfloat16)
    inner = jax.nn.gelu(
        jnp.dot(rms_normed(after_agent), w_in, preferred_element_type=jnp.float32), approximate=True
    ).astype(jnp.bfloat16)
    final = after_agent.astype(jnp.float32) + jnp.dot(
        inner, w_mlp_out, preferred_element_type=jnp.float32
    )
    return final.astype(jnp.bfloat16)


NT = (((1,), (1,)), ((), ()))
VMEM, HBM = pltpu.VMEM, pltpu.HBM


def spec(space):
    return pl.BlockSpec(memory_space=space)


def norm_of(wide):
    scale = lax.rsqrt(jnp.mean(wide * wide, axis=-1, keepdims=True) + epsilon)
    return (wide * scale).astype(jnp.bfloat16)


def gelu(x):
    inside = x * (math.sqrt(2 / math.pi) + (math.sqrt(2 / math.pi) * 0.044715) * (x * x))
    half = 0.5 * x
    return half + half * jnp.tanh(inside)


def in_hbm(weights):
    return [pltpu.with_memory_space_constraint(w, HBM) for w in weights]


def fetch(sources, targets, sems):
    copies = [
        pltpu.make_async_copy(source, target, sems.at[k])
        for k, (source, target) in enumerate(zip(sources, targets))
    ]
    for copy in copies:
        copy.start()
    return copies


def split_heads(values, even, odd, ones=False):
    width = values.shape[1]
    for pair in range(HEADS // 2):
        wide = width // (HEADS // 2)
        own = values[:, pair * wide : (pair + 1) * wide]
        first = lax.broadcasted_iota(jnp.int32, own.shape, 1) < wide // 2
        zero = jnp.zeros_like(own)
        if ones:
            one = jnp.ones_like(own)
            at = 2 * pair * wide
            even[:, at : at + wide] = jnp.where(first, own, zero)
            odd[:, at : at + wide] = jnp.where(first, zero, own)
            even[:, at + wide : at + 2 * wide] = jnp.where(first, one, zero)
            odd[:, at + wide : at + 2 * wide] = jnp.where(first, zero, one)
        else:
            at = pair * wide
            even[:, at : at + wide] = jnp.where(first, own, zero)
            odd[:, at : at + wide] = jnp.where(first, zero, own)


def pair_attention(query, keys, values, factor, bias=None):
    sums = None
    for key, value in zip(keys, values):
        scores = lax.dot_general(query, key, NT, preferred_element_type=jnp.float32)
        if bias is not None:
            scores = scores + bias
        largest = jnp.max(scores, axis=-1, keepdims=True)
        weights = jnp.exp2((scores - largest) * factor).astype(jnp.bfloat16)
        part = jnp.dot(weights, value, preferred_element_type=jnp.float32)
        sums = part if sums is None else sums + part
    wide = query.shape[1]
    return (sums[:, :wide] / sums[:, wide:]).astype(jnp.bfloat16)


def share_kernel(size, *refs):
    states, outs, sems = refs[0], refs[1 : size + 1], refs[size + 1]
    agents = outs[0].shape[1]
    me = lax.axis_index("tm")
    copies = []
    for k, out in enumerate(outs):
        at = pl.ds(pl.multiple_of(jnp.bitwise_xor(me, k) * agents, agents), agents)
        copies.append(pltpu.make_async_copy(states.at[:, at, :], out, sems.at[k]))
    for copy in copies:
        copy.start()
    for copy in copies:
        copy.wait()


def share_stage(states, size):
    steps, agents, features = states.shape
    shape = jax.ShapeDtypeStruct((steps, agents // size, features), states.dtype)
    return pl.pallas_call(
        functools.partial(share_kernel, size),
        out_shape=[shape] * size,
        in_specs=[spec(HBM)],
        out_specs=[spec(VMEM)] * size,
        scratch_shapes=[pltpu.SemaphoreType.DMA((size,))],
        compiler_params=pltpu.CompilerParams(vmem_limit_bytes=4 * 2**20),
        cost_estimate=pl.CostEstimate(flops=2 * 10**10, bytes_accessed=10**7, transcendentals=0),
        name="cut_shares",
    )(*in_hbm([states]))


def time_kernel(size, *refs):
    pieces, weights = refs[:size], refs[size : size + 4]
    outs = refs[size + 4 : 2 * size + 4]
    wide, normed, query, keys, values, mixed = refs[2 * size + 4 :]
    w_query, w_key, w_value, w_out = weights
    steps, agents, features = pieces[0].shape
    rows = steps * agents
    total_steps = steps * size
    me = lax.axis_index("tm")
    lanes_of = [slice(c * 128, (c + 1) * 128) for c in range(features // 128)]
    for k in range(size):
        start = pl.multiple_of(jnp.bitwise_xor(me, k) * rows, rows)
        piece = pieces[k][...].reshape(rows, features).astype(jnp.float32)
        for c, lanes in enumerate(lanes_of):
            wide[c, pl.ds(start, rows), :] = piece[:, lanes]
    for agent in range(agents):
        at = pl.ds(agent, total_steps, stride=agents)
        own = jnp.concatenate([wide[c, at, :] for c in range(len(lanes_of))], axis=1)
        normed[pl.ds(agent * total_steps, total_steps), :] = norm_of(own)
    group = 2 * total_steps
    span = -(-group // 128) * 128
    head_size = features // HEADS
    factor = math.log2(math.e) * head_size**-0.5
    query[...] = project(normed[...], w_query[...])
    key = project(normed[...], w_key[...])
    value = project(normed[...], w_value[...])
    even = lax.broadcasted_iota(jnp.int32, (group, features), 1) % (2 * head_size) < head_size
    zero = jnp.zeros((group, features), jnp.bfloat16)
    spare = jnp.zeros((span - group, features), jnp.bfloat16)
    for g in range(agents // 2):
        rows_in = slice(g * group, (g + 1) * group)
        for h, mine in enumerate((even, jnp.logical_not(even))):
            at = (2 * g + h) * span
            keys[at : at + group, :] = jnp.where(mine, key[rows_in], zero)
            values[at : at + group, :] = jnp.where(mine, value[rows_in], zero)
            for target in (keys, values):
                target[at + group : at + span, :] = spare
    row = lax.broadcasted_iota(jnp.int32, (group, span), 0)
    column = lax.broadcasted_iota(jnp.int32, (group, span), 1)
    same = (row >= total_steps) == (column >= total_steps)
    bias = jnp.where(jnp.logical_and(same, column <= row), 0.0, negative_floor)
    second_rows = lax.broadcasted_iota(jnp.int32, (2 * span, 2 * head_size), 0) >= span
    second_lanes = lax.broadcasted_iota(jnp.int32, (2 * span, 2 * head_size), 1) >= head_size
    counts = (second_rows == second_lanes).astype(jnp.bfloat16)
    for g in range(agents // 2):
        at, both = pl.ds(g * group, group), pl.ds(2 * g * span, 2 * span)
        for pair in range(HEADS // 2):
            lanes = pl.ds(pair * 2 * head_size, 2 * head_size)
            scores = lax.dot_general(
                query[at, lanes], keys[both, lanes], NT, preferred_element_type=jnp.float32
            )
            weights = []
            for h in range(2):
                mine = scores[:, h * span : (h + 1) * span] + bias
                largest = jnp.max(mine, axis=-1, keepdims=True)
                weights.append(jnp.exp2((mine - largest) * factor).astype(jnp.bfloat16))
            weights = jnp.concatenate(weights, axis=1)
            value = jnp.concatenate([values[both, lanes], counts], axis=1)
            sums = jnp.dot(weights, value, preferred_element_type=jnp.float32)
            wide_lanes = 2 * head_size
            mixed[at, lanes] = (sums[:, :wide_lanes] / sums[:, wide_lanes:]).astype(jnp.bfloat16)
    added = jnp.dot(mixed[...], w_out[...], preferred_element_type=jnp.float32)
    for agent in range(agents):
        at = pl.ds(agent, total_steps, stride=agents)
        mine = added[agent * total_steps : (agent + 1) * total_steps]
        for c, lanes in enumerate(lanes_of):
            wide[c, at, :] = wide[c, at, :] + mine[:, lanes]
    for k in range(size):
        start = pl.multiple_of(jnp.bitwise_xor(me, k) * rows, rows)
        piece = jnp.concatenate(
            [wide[c, pl.ds(start, rows), :] for c in range(len(lanes_of))], axis=1
        )
        outs[k][...] = piece.astype(jnp.bfloat16).reshape(pieces[0].shape)


def time_stage(pieces, weights):
    size = len(pieces)
    steps, agents, features = pieces[0].shape
    rows = steps * agents * size
    kind = jnp.bfloat16
    return pl.pallas_call(
        functools.partial(time_kernel, size),
        out_shape=[jax.ShapeDtypeStruct((steps, agents, features), kind)] * size,
        in_specs=[spec(VMEM)] * (size + 4),
        out_specs=[spec(VMEM)] * size,
        scratch_shapes=[VMEM((features // 128, rows, 128), jnp.float32)]
        + [VMEM((rows, features), kind)] * 2
        + [VMEM((agents * (-(-2 * steps * size // 128) * 128), features), kind)] * 2
        + [VMEM((rows, features), kind)],
        compiler_params=pltpu.CompilerParams(vmem_limit_bytes=24 * 2**20),
        cost_estimate=pl.CostEstimate(
            flops=8 * rows * features * features,
            bytes_accessed=2 * (2 * rows + 4 * features) * features,
            transcendentals=rows * HEADS * steps * size,
        ),
        name="time_attention",
    )(*pieces, *weights)


def pack_kernel(size, choose, *refs):
    count = len(choose(0))
    pieces, outs = refs[:size], refs[len(refs) - count :]
    agents = pieces[0].shape[1]
    me, plane = lax.axis_index("tm"), lax.axis_index("agent")
    for out, step in zip(outs, choose(plane)):
        for k in range(size):
            start = pl.multiple_of(jnp.bitwise_xor(me, k) * agents, agents)
            out[pl.ds(start, agents), :] = pieces[k][step]


def pack_stage(pieces, choose, after=()):
    size, count = len(pieces), len(choose(0))
    _, agents, features = pieces[0].shape
    return pl.pallas_call(
        functools.partial(pack_kernel, size, choose),
        out_shape=[jax.ShapeDtypeStruct((agents * size, features), jnp.bfloat16)] * count,
        in_specs=[spec(VMEM)] * size + [spec(pl.ANY)] * len(after),
        out_specs=[spec(VMEM)] * count,
        compiler_params=pltpu.CompilerParams(vmem_limit_bytes=8 * 2**20),
        name="pack_steps",
    )(*pieces, *after)


def agent_body(count, blocks, weights, outs, scratch):
    normed, query, key_e, key_o, value_e, value_o, mixed, after, inner, w_out, sems = scratch
    w_query, w_key, w_value, far_out, w_in, w_mlp_out = weights
    copies = fetch((far_out,), (w_out,), sems)
    agents, features = blocks[0].shape
    head_size = features // HEADS
    factor = math.log2(math.e) * head_size**-0.5
    for b in range(count):
        normed[pl.ds(b * agents, agents), :] = norm_of(blocks[b][...].astype(jnp.float32))
    query[...] = project(normed[...], w_query[...])
    split_heads(project(normed[...], w_key[...]), key_e, key_o)
    split_heads(project(normed[...], w_value[...]), value_e, value_o, True)
    for pair in range(HEADS // 2):
        lanes = pl.ds(pair * 2 * head_size, 2 * head_size)
        double = pl.ds(pair * 4 * head_size, 4 * head_size)
        mixed[:, lanes] = pair_attention(
            query[:, lanes],
            (key_e[:, lanes], key_o[:, lanes]),
            (value_e[:, double], value_o[:, double]),
            factor,
        )
    copies[0].wait()
    added = jnp.dot(mixed[...], w_out[...], preferred_element_type=jnp.float32)
    for b in range(count):
        at = pl.ds(b * agents, agents)
        own = blocks[b][...].astype(jnp.float32) + added[b * agents : (b + 1) * agents]
        after[at, :] = own.astype(jnp.bfloat16)
        normed[at, :] = norm_of(after[at, :].astype(jnp.float32))
    hidden = w_in.shape[1]
    for start in range(0, hidden, features):
        inner[:, pl.ds(start, features)] = gelu(
            jnp.dot(
                normed[...], w_in[:, pl.ds(start, features)], preferred_element_type=jnp.float32
            )
        ).astype(jnp.bfloat16)
    final = after[...].astype(jnp.float32) + jnp.dot(
        inner[...], w_mlp_out[...], preferred_element_type=jnp.float32
    )
    for b in range(count):
        outs[b][...] = final[b * agents : (b + 1) * agents].astype(jnp.bfloat16)


def agent_kernel(count, middle_only, *refs):
    blocks, weights = refs[:count], refs[count : count + 6]
    outs, scratch = refs[-11 - count : -11], refs[-11:]

    def run():
        agent_body(count, blocks, weights, outs, scratch)

    if middle_only:
        plane = lax.axis_index("agent")
        pl.when(jnp.logical_or(plane == 1, plane == 2))(run)
    else:
        run()


def agent_stage(blocks, weights, middle_only, after=()):
    count = len(blocks)
    agents, features = blocks[0].shape
    hidden = weights[4].shape[1]
    rows = count * agents
    kind = jnp.bfloat16
    return pl.pallas_call(
        functools.partial(agent_kernel, count, middle_only),
        out_shape=[jax.ShapeDtypeStruct((agents, features), kind)] * count,
        in_specs=[spec(VMEM)] * (count + 3)
        + [spec(HBM)]
        + [spec(VMEM)] * 2
        + [spec(pl.ANY)] * len(after),
        out_specs=[spec(VMEM)] * count,
        scratch_shapes=[VMEM((rows, features), kind)] * 4
        + [VMEM((rows, 2 * features), kind)] * 2
        + [VMEM((rows, features), kind)] * 2
        + [VMEM((rows, hidden), kind)]
        + [VMEM(weights[3].shape, kind), pltpu.SemaphoreType.DMA((1,))],
        compiler_params=pltpu.CompilerParams(vmem_limit_bytes=16 * 2**20),
        cost_estimate=pl.CostEstimate(
            flops=2 * rows * features * (4 * features + 2 * hidden + 2 * rows),
            bytes_accessed=2 * rows * features * 8,
            transcendentals=rows * (HEADS * rows + hidden),
        ),
        name="agent_step",
    )(*blocks, *weights[:3], *in_hbm(weights[3:4]), *weights[4:], *after)


def place_kernel(*refs):
    sources, out, sems = [refs[k] for k in (0, 1, 2, 3)], refs[4], refs[5]
    plane = lax.axis_index("agent")
    copies = [
        pltpu.make_async_copy(source, out.at[jnp.bitwise_xor(plane, k)], sems.at[k])
        for k, source in enumerate(sources)
    ]
    for copy in copies:
        copy.start()
    for copy in copies:
        copy.wait()


def place_extra_kernel(*refs):
    sources, out, sems = [refs[k] for k in (0, 1, 2, 3)], refs[5], refs[6]
    plane = lax.axis_index("agent")
    middle = jnp.logical_or(plane == 1, plane == 2)
    low = plane // 2

    def place(one, other):
        copies = [
            pltpu.make_async_copy(one, out.at[4 + low], sems.at[0]),
            pltpu.make_async_copy(other, out.at[5 - low], sems.at[1]),
        ]
        for copy in copies:
            copy.start()
        for copy in copies:
            copy.wait()

    pl.when(middle)(lambda: place(sources[0], sources[3]))
    pl.when(jnp.logical_not(middle))(lambda: place(sources[1], sources[2]))


def place_stage(whole, extra):
    agents, features = whole[0].shape
    shape = jax.ShapeDtypeStruct((6, agents, features), jnp.bfloat16)
    begun = pl.pallas_call(
        place_kernel,
        out_shape=shape,
        in_specs=[spec(VMEM)] * 4,
        out_specs=spec(HBM),
        scratch_shapes=[pltpu.SemaphoreType.DMA((4,))],
        compiler_params=pltpu.CompilerParams(vmem_limit_bytes=4 * 2**20),
        name="place_steps",
    )(*[whole[k] for k in (0, 1, 2, 3)])
    return pl.pallas_call(
        place_extra_kernel,
        out_shape=shape,
        in_specs=[spec(VMEM)] * 4 + [spec(HBM)],
        out_specs=spec(HBM),
        input_output_aliases={4: 0},
        scratch_shapes=[pltpu.SemaphoreType.DMA((2,))],
        compiler_params=pltpu.CompilerParams(vmem_limit_bytes=4 * 2**20),
        name="place_extra",
    )(*[extra[k] for k in (0, 1, 2, 3)], begun)


def xor_pairs(size, k, targets=None):
    return [(j, j ^ k) for j in range(size) if targets is None or j ^ k in targets]


def exchange(parts, axis, targets=None, ordered=False):
    size = len(parts)
    moved = {}
    for k in range(size - 1, 0, -1):
        part = parts[k]
        if ordered and k == 1:
            part, moved[size - 1] = lax.optimization_barrier((part, moved[size - 1]))
        moved[k] = lax.ppermute(part, axis, xor_pairs(size, k, targets))
    return [parts[0]] + [moved[k] for k in range(1, size)]


def together(parts):
    return lax.optimization_barrier(tuple(parts[::-1]))[::-1]


def picked(plane, values):
    result = jnp.int32(values[0])
    for place in range(1, len(values)):
        result = jnp.where(plane == place, values[place], result)
    return result


def whole_steps(plane):
    return [jnp.bitwise_xor(plane, k) for k in range(4)]


def extra_steps(plane):
    return [
        4 + picked(plane, (0, 0, 1, 0)),
        4 + picked(plane, (0, 0, 0, 1)),
        4 + picked(plane, (1, 0, 0, 0)),
        4 + picked(plane, (0, 1, 0, 0)),
    ]


def local(
    states,
    neighbours,
    w_query_t,
    w_key_t,
    w_value_t,
    w_out_t,
    w_query_a,
    w_key_a,
    w_value_a,
    w_out_a,
    w_in,
    w_mlp_out,
):
    local_steps, local_agents, features = states.shape
    size, planes = lax.axis_size("tm"), lax.axis_size("agent")
    share = local_agents // size
    time_weights = (w_query_t, w_key_t, w_value_t, w_out_t)
    agent_weights = (w_query_a, w_key_a, w_value_a, w_out_a, w_in, w_mlp_out)
    fits = (
        size & (size - 1) == 0
        and share * size == local_agents
        and share % 16 == 0
        and planes == 4
        and neighbours.shape == (4, 4)
        and local_steps == 6
    )
    if not fits:
        after_time = general_time(states, *time_weights)
        return general_agent(after_time, neighbours, *agent_weights)

    pieces = together(exchange(share_stage(states, size), "tm", ordered=True))
    pieces = together(exchange(time_stage(pieces, time_weights), "tm", ordered=True))
    blocks_a = exchange(pack_stage(pieces, whole_steps), "agent")
    blocks_b = exchange(pack_stage(pieces, extra_steps, blocks_a[2:3]), "agent", (1, 2))

    result_a = agent_stage(blocks_a, agent_weights, False)
    done_a = exchange(result_a, "agent")
    result_b = agent_stage(blocks_b, agent_weights, True, result_a[:1])
    done_b = [result_b[0]] + [
        lax.ppermute(result_b[k], "agent", [(j, j ^ k) for j in (1, 2)]) for k in (1, 2, 3)
    ]
    return place_stage(done_a, done_b)


def solution(mesh):
    placed = (P("tm", "agent", None), P(), P(), P(), P(), P(), P(), P(), P(), P(), P(), P())
    return jax.shard_map(
        local, mesh=mesh, in_specs=placed, out_specs=P("tm", "agent", None), check_vma=False
    )
```

```python
import functools
import math

import jax
import jax.numpy as jnp
from jax import lax
from jax.experimental import pallas as pl
from jax.experimental.pallas import tpu as pltpu
from jax.sharding import PartitionSpec as P

HEADS = 8


negative_floor = -1e30
epsilon = 1e-06


def rms_normed(values):
    wide = values.astype(jnp.float32)
    scale = lax.rsqrt(jnp.mean(wide * wide, axis=-1, keepdims=True) + epsilon)
    return (wide * scale).astype(jnp.bfloat16)


def project(normed, weight):
    return jnp.dot(normed, weight, preferred_element_type=jnp.float32).astype(jnp.bfloat16)


def attend(query, keys, values, allowed):
    batch, query_len, features = query.shape
    key_len = keys.shape[1]
    head_size = features // HEADS
    query_h = query.reshape(batch, query_len, HEADS, head_size)
    keys_h = keys.reshape(batch, key_len, HEADS, head_size)
    values_h = values.reshape(batch, key_len, HEADS, head_size)
    scores = jnp.einsum(
        "bqhe,bkhe->bhqk", query_h, keys_h, preferred_element_type=jnp.float32
    ) * head_size ** (-0.5)
    scores = jnp.where(allowed[:, None], scores, negative_floor)
    largest = jnp.max(scores, axis=-1, keepdims=True)
    weights = jnp.where(allowed[:, None], jnp.exp(scores - largest), 0.0)
    totals = jnp.sum(weights, axis=-1)
    summed = jnp.einsum(
        "bhqk,bkhe->bqhe",
        weights.astype(jnp.bfloat16),
        values_h,
        preferred_element_type=jnp.float32,
    )
    result = summed / jnp.transpose(totals, (0, 2, 1))[..., None]
    return result.reshape(batch, query_len, features).astype(jnp.bfloat16)


def general_time(states, w_query_t, w_key_t, w_value_t, w_out_t):
    local_steps = states.shape[0]
    normed = rms_normed(states)
    query = jnp.swapaxes(project(normed, w_query_t), 0, 1)
    keys = lax.all_gather(project(normed, w_key_t), "tm", axis=0, tiled=True)
    values = lax.all_gather(project(normed, w_value_t), "tm", axis=0, tiled=True)
    query_time = lax.axis_index("tm") * local_steps + jnp.arange(local_steps)
    allowed = (jnp.arange(keys.shape[0])[None, :] <= query_time[:, None])[None]
    mixed = attend(query, jnp.swapaxes(keys, 0, 1), jnp.swapaxes(values, 0, 1), allowed)
    return (
        states.astype(jnp.float32)
        + jnp.dot(jnp.swapaxes(mixed, 0, 1), w_out_t, preferred_element_type=jnp.float32)
    ).astype(jnp.bfloat16)


def general_agent(
    after_time, neighbours, w_query_a, w_key_a, w_value_a, w_out_a, w_in, w_mlp_out
):
    local_steps, local_agents, features = after_time.shape
    second_normed = rms_normed(after_time)
    agent_query = project(second_normed, w_query_a)
    block_count = lax.axis_size("agent")
    chosen_blocks = lax.dynamic_slice_in_dim(neighbours, lax.axis_index("agent"), 1, 0)[0]
    neighbour_count = neighbours.shape[1]
    everyone = lax.all_gather(second_normed, "agent", axis=1, tiled=True)
    picked = jnp.take(
        everyone.reshape(local_steps, block_count, local_agents, features), chosen_blocks, axis=1
    )
    picked = picked.reshape(local_steps, neighbour_count * local_agents, features)
    agent_key = project(picked, w_key_a)
    agent_value = project(picked, w_value_a)
    allowed_all = jnp.ones((1, local_agents, neighbour_count * local_agents), dtype=bool)
    agent_mixed = attend(agent_query, agent_key, agent_value, allowed_all)
    after_agent = (
        after_time.astype(jnp.float32)
        + jnp.dot(agent_mixed, w_out_a, preferred_element_type=jnp.float32)
    ).astype(jnp.bfloat16)
    inner = jax.nn.gelu(
        jnp.dot(rms_normed(after_agent), w_in, preferred_element_type=jnp.float32), approximate=True
    ).astype(jnp.bfloat16)
    final = after_agent.astype(jnp.float32) + jnp.dot(
        inner, w_mlp_out, preferred_element_type=jnp.float32
    )
    return final.astype(jnp.bfloat16)


NT = (((1,), (1,)), ((), ()))
VMEM, HBM = pltpu.VMEM, pltpu.HBM


def spec(space):
    return pl.BlockSpec(memory_space=space)


def norm_of(wide):
    scale = lax.rsqrt(jnp.mean(wide * wide, axis=-1, keepdims=True) + epsilon)
    return (wide * scale).astype(jnp.bfloat16)


def gelu(x):
    inside = x * (math.sqrt(2 / math.pi) + (math.sqrt(2 / math.pi) * 0.044715) * (x * x))
    half = 0.5 * x
    return half + half * jnp.tanh(inside)


def in_hbm(weights):
    return [pltpu.with_memory_space_constraint(w, HBM) for w in weights]


def fetch(sources, targets, sems):
    copies = [
        pltpu.make_async_copy(source, target, sems.at[k])
        for k, (source, target) in enumerate(zip(sources, targets))
    ]
    for copy in copies:
        copy.start()
    return copies


def share_kernel(size, *refs):
    states, outs, sems = refs[0], refs[1 : size + 1], refs[size + 1]
    agents = outs[0].shape[1]
    me = lax.axis_index("tm")
    copies = []
    for k, out in enumerate(outs):
        at = pl.ds(pl.multiple_of(jnp.bitwise_xor(me, k) * agents, agents), agents)
        copies.append(pltpu.make_async_copy(states.at[:, at, :], out, sems.at[k]))
    for copy in copies:
        copy.start()
    for copy in copies:
        copy.wait()


def share_stage(states, size):
    steps, agents, features = states.shape
    shape = jax.ShapeDtypeStruct((steps, agents // size, features), states.dtype)
    return pl.pallas_call(
        functools.partial(share_kernel, size),
        out_shape=[shape] * size,
        in_specs=[spec(HBM)],
        out_specs=[spec(VMEM)] * size,
        scratch_shapes=[pltpu.SemaphoreType.DMA((size,))],
        compiler_params=pltpu.CompilerParams(vmem_limit_bytes=4 * 2**20),
        cost_estimate=pl.CostEstimate(flops=2 * 10**10, bytes_accessed=10**7, transcendentals=0),
        name="cut_shares",
    )(*in_hbm([states]))


def time_kernel(size, *refs):
    pieces, weights = refs[:size], refs[size : size + 4]
    outs = refs[size + 4 : 2 * size + 4]
    wide, normed, query, keys, values, mixed = refs[2 * size + 4 :]
    w_query, w_key, w_value, w_out = weights
    steps, agents, features = pieces[0].shape
    rows = steps * agents
    total_steps = steps * size
    me = lax.axis_index("tm")
    lanes_of = [slice(c * 128, (c + 1) * 128) for c in range(features // 128)]
    for k in range(size):
        start = pl.multiple_of(jnp.bitwise_xor(me, k) * rows, rows)
        piece = pieces[k][...].reshape(rows, features).astype(jnp.float32)
        for c, lanes in enumerate(lanes_of):
            wide[c, pl.ds(start, rows), :] = piece[:, lanes]
    for agent in range(agents):
        at = pl.ds(agent, total_steps, stride=agents)
        own = jnp.concatenate([wide[c, at, :] for c in range(len(lanes_of))], axis=1)
        normed[pl.ds(agent * total_steps, total_steps), :] = norm_of(own)
    group = 2 * total_steps
    span = -(-group // 128) * 128
    head_size = features // HEADS
    factor = math.log2(math.e) * head_size**-0.5
    query[...] = project(normed[...], w_query[...])
    key = project(normed[...], w_key[...])
    value = project(normed[...], w_value[...])
    even = lax.broadcasted_iota(jnp.int32, (group, features), 1) % (2 * head_size) < head_size
    zero = jnp.zeros((group, features), jnp.bfloat16)
    spare = jnp.zeros((span - group, features), jnp.bfloat16)
    for g in range(agents // 2):
        rows_in = slice(g * group, (g + 1) * group)
        for h, mine in enumerate((even, jnp.logical_not(even))):
            at = (2 * g + h) * span
            keys[at : at + group, :] = jnp.where(mine, key[rows_in], zero)
            values[at : at + group, :] = jnp.where(mine, value[rows_in], zero)
            for target in (keys, values):
                target[at + group : at + span, :] = spare
    row = lax.broadcasted_iota(jnp.int32, (group, span), 0)
    column = lax.broadcasted_iota(jnp.int32, (group, span), 1)
    same = (row >= total_steps) == (column >= total_steps)
    bias = jnp.where(jnp.logical_and(same, column <= row), 0.0, negative_floor)
    second_rows = lax.broadcasted_iota(jnp.int32, (2 * span, 2 * head_size), 0) >= span
    second_lanes = lax.broadcasted_iota(jnp.int32, (2 * span, 2 * head_size), 1) >= head_size
    counts = (second_rows == second_lanes).astype(jnp.bfloat16)
    for g in range(agents // 2):
        at, both = pl.ds(g * group, group), pl.ds(2 * g * span, 2 * span)
        for pair in range(HEADS // 2):
            lanes = pl.ds(pair * 2 * head_size, 2 * head_size)
            scores = lax.dot_general(
                query[at, lanes], keys[both, lanes], NT, preferred_element_type=jnp.float32
            )
            weights = []
            for h in range(2):
                mine = scores[:, h * span : (h + 1) * span] + bias
                largest = jnp.max(mine, axis=-1, keepdims=True)
                weights.append(jnp.exp2((mine - largest) * factor).astype(jnp.bfloat16))
            weights = jnp.concatenate(weights, axis=1)
            value = jnp.concatenate([values[both, lanes], counts], axis=1)
            sums = jnp.dot(weights, value, preferred_element_type=jnp.float32)
            wide_lanes = 2 * head_size
            mixed[at, lanes] = (sums[:, :wide_lanes] / sums[:, wide_lanes:]).astype(jnp.bfloat16)
    added = jnp.dot(mixed[...], w_out[...], preferred_element_type=jnp.float32)
    for agent in range(agents):
        at = pl.ds(agent, total_steps, stride=agents)
        mine = added[agent * total_steps : (agent + 1) * total_steps]
        for c, lanes in enumerate(lanes_of):
            wide[c, at, :] = wide[c, at, :] + mine[:, lanes]
    for k in range(size):
        start = pl.multiple_of(jnp.bitwise_xor(me, k) * rows, rows)
        piece = jnp.concatenate(
            [wide[c, pl.ds(start, rows), :] for c in range(len(lanes_of))], axis=1
        )
        outs[k][...] = piece.astype(jnp.bfloat16).reshape(pieces[0].shape)


def time_stage(pieces, weights):
    size = len(pieces)
    steps, agents, features = pieces[0].shape
    rows = steps * agents * size
    kind = jnp.bfloat16
    return pl.pallas_call(
        functools.partial(time_kernel, size),
        out_shape=[jax.ShapeDtypeStruct((steps, agents, features), kind)] * size,
        in_specs=[spec(VMEM)] * (size + 4),
        out_specs=[spec(VMEM)] * size,
        scratch_shapes=[VMEM((features // 128, rows, 128), jnp.float32)]
        + [VMEM((rows, features), kind)] * 2
        + [VMEM((agents * (-(-2 * steps * size // 128) * 128), features), kind)] * 2
        + [VMEM((rows, features), kind)],
        compiler_params=pltpu.CompilerParams(vmem_limit_bytes=24 * 2**20),
        cost_estimate=pl.CostEstimate(
            flops=8 * rows * features * features,
            bytes_accessed=2 * (2 * rows + 4 * features) * features,
            transcendentals=rows * HEADS * steps * size,
        ),
        name="time_attention",
    )(*pieces, *weights)


def pack_kernel(size, choose, *refs):
    count = len(choose(0))
    pieces, outs = refs[:size], refs[len(refs) - count :]
    agents = pieces[0].shape[1]
    me, plane = lax.axis_index("tm"), lax.axis_index("agent")
    for out, step in zip(outs, choose(plane)):
        for k in range(size):
            start = pl.multiple_of(jnp.bitwise_xor(me, k) * agents, agents)
            out[pl.ds(start, agents), :] = pieces[k][step]


def pack_stage(pieces, choose, after=()):
    size, count = len(pieces), len(choose(0))
    _, agents, features = pieces[0].shape
    return pl.pallas_call(
        functools.partial(pack_kernel, size, choose),
        out_shape=[jax.ShapeDtypeStruct((agents * size, features), jnp.bfloat16)] * count,
        in_specs=[spec(VMEM)] * size + [spec(pl.ANY)] * len(after),
        out_specs=[spec(VMEM)] * count,
        compiler_params=pltpu.CompilerParams(vmem_limit_bytes=8 * 2**20),
        name="pack_steps",
    )(*pieces, *after)


def agent_body(count, blocks, weights, outs, scratch):
    normed, query, keys, values, mixed, after, inner, w_out, sems = scratch
    w_query, w_key, w_value, far_out, w_in, w_mlp_out = weights
    copies = fetch((far_out,), (w_out,), sems)
    agents, features = blocks[0].shape
    head_size = features // HEADS
    factor = math.log2(math.e) * head_size**-0.5
    for b in range(count):
        normed[pl.ds(b * agents, agents), :] = norm_of(blocks[b][...].astype(jnp.float32))
    query[...] = project(normed[...], w_query[...])
    rows, wide_lanes = count * agents, 2 * head_size
    for weight, target in ((w_key, keys), (w_value, values)):
        found = project(normed[...], weight[...])
        even = lax.broadcasted_iota(jnp.int32, found.shape, 1) % wide_lanes < head_size
        zero = jnp.zeros_like(found)
        target[:rows, :] = jnp.where(even, found, zero)
        target[rows:, :] = jnp.where(even, zero, found)
    second_rows = lax.broadcasted_iota(jnp.int32, (2 * rows, wide_lanes), 0) >= rows
    second_lanes = lax.broadcasted_iota(jnp.int32, (2 * rows, wide_lanes), 1) >= head_size
    counts = (second_rows == second_lanes).astype(jnp.bfloat16)
    for pair, part in [(p, r) for p in range(HEADS // 2) for r in range(2)]:
        lanes = pl.ds(pair * wide_lanes, wide_lanes)
        at = pl.ds(part * (rows // 2), rows // 2)
        weights_of = []
        both = lax.dot_general(query[at, lanes], keys[:, lanes], NT, preferred_element_type=jnp.float32)
        for h in range(2):
            scores = both[:, h * rows : (h + 1) * rows]
            largest = jnp.max(scores, axis=-1, keepdims=True)
            weights_of.append(jnp.exp2((scores - largest) * factor).astype(jnp.bfloat16))
        sums = jnp.dot(
            jnp.concatenate(weights_of, axis=1),
            jnp.concatenate([values[:, lanes], counts], axis=1),
            preferred_element_type=jnp.float32,
        )
        mixed[at, lanes] = (sums[:, :wide_lanes] / sums[:, wide_lanes:]).astype(jnp.bfloat16)
    copies[0].wait()
    for b in range(count):
        at = pl.ds(b * agents, agents)
        if b % 2 == 0:
            two = pl.ds(b * agents, 2 * agents)
            added = jnp.dot(mixed[two, :], w_out[...], preferred_element_type=jnp.float32)
        own = blocks[b][...].astype(jnp.float32) + added[b % 2 * agents : (b % 2 + 1) * agents]
        after[at, :] = own.astype(jnp.bfloat16)
        normed[at, :] = norm_of(after[at, :].astype(jnp.float32))
    hidden = w_in.shape[1]
    for start in range(0, hidden, features):
        inner[:, pl.ds(start, features)] = gelu(
            jnp.dot(
                normed[...], w_in[:, pl.ds(start, features)], preferred_element_type=jnp.float32
            )
        ).astype(jnp.bfloat16)
    final = after[...].astype(jnp.float32) + jnp.dot(
        inner[...], w_mlp_out[...], preferred_element_type=jnp.float32
    )
    for b in range(count):
        outs[b][...] = final[b * agents : (b + 1) * agents].astype(jnp.bfloat16)


def agent_kernel(count, middle_only, *refs):
    blocks, weights = refs[:count], refs[count : count + 6]
    outs, scratch = refs[-9 - count : -9], refs[-9:]

    def run():
        agent_body(count, blocks, weights, outs, scratch)

    if middle_only:
        plane = lax.axis_index("agent")
        pl.when(jnp.logical_or(plane == 1, plane == 2))(run)
    else:
        run()


def agent_stage(blocks, weights, middle_only, after=()):
    count = len(blocks)
    agents, features = blocks[0].shape
    hidden = weights[4].shape[1]
    rows = count * agents
    kind = jnp.bfloat16
    return pl.pallas_call(
        functools.partial(agent_kernel, count, middle_only),
        out_shape=[jax.ShapeDtypeStruct((agents, features), kind)] * count,
        in_specs=[spec(VMEM)] * (count + 3)
        + [spec(HBM)]
        + [spec(VMEM)] * 2
        + [spec(pl.ANY)] * len(after),
        out_specs=[spec(VMEM)] * count,
        scratch_shapes=[VMEM((rows, features), kind)] * 2
        + [VMEM((2 * rows, features), kind)] * 2
        + [VMEM((rows, features), kind)] * 2
        + [VMEM((rows, hidden), kind)]
        + [VMEM(weights[3].shape, kind), pltpu.SemaphoreType.DMA((1,))],
        compiler_params=pltpu.CompilerParams(vmem_limit_bytes=16 * 2**20),
        cost_estimate=pl.CostEstimate(
            flops=2 * rows * features * (4 * features + 2 * hidden + 2 * rows),
            bytes_accessed=2 * rows * features * 8,
            transcendentals=rows * (HEADS * rows + hidden),
        ),
        name="agent_step",
    )(*blocks, *weights[:3], *in_hbm(weights[3:4]), *weights[4:], *after)


def place_kernel(*refs):
    sources, out, sems = [refs[k] for k in (0, 1, 2, 3)], refs[4], refs[5]
    plane = lax.axis_index("agent")
    copies = [
        pltpu.make_async_copy(source, out.at[jnp.bitwise_xor(plane, k)], sems.at[k])
        for k, source in enumerate(sources)
    ]
    for copy in copies:
        copy.start()
    for copy in copies:
        copy.wait()


def place_extra_kernel(*refs):
    sources, out, sems = [refs[k] for k in (0, 1, 2, 3)], refs[5], refs[6]
    plane = lax.axis_index("agent")
    middle = jnp.logical_or(plane == 1, plane == 2)
    low = plane // 2

    def place(one, other):
        copies = [
            pltpu.make_async_copy(one, out.at[4 + low], sems.at[0]),
            pltpu.make_async_copy(other, out.at[5 - low], sems.at[1]),
        ]
        for copy in copies:
            copy.start()
        for copy in copies:
            copy.wait()

    pl.when(middle)(lambda: place(sources[0], sources[3]))
    pl.when(jnp.logical_not(middle))(lambda: place(sources[1], sources[2]))


def place_stage(whole, extra):
    agents, features = whole[0].shape
    shape = jax.ShapeDtypeStruct((6, agents, features), jnp.bfloat16)
    begun = pl.pallas_call(
        place_kernel,
        out_shape=shape,
        in_specs=[spec(VMEM)] * 4,
        out_specs=spec(HBM),
        scratch_shapes=[pltpu.SemaphoreType.DMA((4,))],
        compiler_params=pltpu.CompilerParams(vmem_limit_bytes=4 * 2**20),
        name="place_steps",
    )(*[whole[k] for k in (0, 1, 2, 3)])
    return pl.pallas_call(
        place_extra_kernel,
        out_shape=shape,
        in_specs=[spec(VMEM)] * 4 + [spec(HBM)],
        out_specs=spec(HBM),
        input_output_aliases={4: 0},
        scratch_shapes=[pltpu.SemaphoreType.DMA((2,))],
        compiler_params=pltpu.CompilerParams(vmem_limit_bytes=4 * 2**20),
        name="place_extra",
    )(*[extra[k] for k in (0, 1, 2, 3)], begun)


def xor_pairs(size, k, targets=None):
    return [(j, j ^ k) for j in range(size) if targets is None or j ^ k in targets]


def exchange(parts, axis, targets=None, ordered=False):
    size = len(parts)
    moved = {}
    for k in range(size - 1, 0, -1):
        part = parts[k]
        if ordered and k == 1:
            part, moved[size - 1] = lax.optimization_barrier((part, moved[size - 1]))
        moved[k] = lax.ppermute(part, axis, xor_pairs(size, k, targets))
    return [parts[0]] + [moved[k] for k in range(1, size)]


def together(parts):
    return lax.optimization_barrier(tuple(parts[::-1]))[::-1]


def picked(plane, values):
    result = jnp.int32(values[0])
    for place in range(1, len(values)):
        result = jnp.where(plane == place, values[place], result)
    return result


def whole_steps(plane):
    return [jnp.bitwise_xor(plane, k) for k in range(4)]


def extra_steps(plane):
    return [
        4 + picked(plane, (0, 0, 1, 0)),
        4 + picked(plane, (0, 0, 0, 1)),
        4 + picked(plane, (1, 0, 0, 0)),
        4 + picked(plane, (0, 1, 0, 0)),
    ]


def local(
    states,
    neighbours,
    w_query_t,
    w_key_t,
    w_value_t,
    w_out_t,
    w_query_a,
    w_key_a,
    w_value_a,
    w_out_a,
    w_in,
    w_mlp_out,
):
    local_steps, local_agents, features = states.shape
    size, planes = lax.axis_size("tm"), lax.axis_size("agent")
    share = local_agents // size
    time_weights = (w_query_t, w_key_t, w_value_t, w_out_t)
    agent_weights = (w_query_a, w_key_a, w_value_a, w_out_a, w_in, w_mlp_out)
    fits = (
        size & (size - 1) == 0
        and share * size == local_agents
        and share % 16 == 0
        and planes == 4
        and neighbours.shape == (4, 4)
        and local_steps == 6
    )
    if not fits:
        after_time = general_time(states, *time_weights)
        return general_agent(after_time, neighbours, *agent_weights)

    pieces = together(exchange(share_stage(states, size), "tm", ordered=True))
    pieces = together(exchange(time_stage(pieces, time_weights), "tm", ordered=True))
    blocks_a = exchange(pack_stage(pieces, whole_steps), "agent")
    blocks_b = exchange(pack_stage(pieces, extra_steps, blocks_a[2:3]), "agent", (1, 2))

    result_a = agent_stage(blocks_a, agent_weights, False)
    done_a = exchange(result_a, "agent")
    result_b = agent_stage(blocks_b, agent_weights, True, result_a[:1])
    done_b = [result_b[0]] + [
        lax.ppermute(result_b[k], "agent", [(j, j ^ k) for j in (1, 2)]) for k in (1, 2, 3)
    ]
    return place_stage(done_a, done_b)


def solution(mesh):
    placed = (P("tm", "agent", None), P(), P(), P(), P(), P(), P(), P(), P(), P(), P(), P())
    return jax.shard_map(
        local, mesh=mesh, in_specs=placed, out_specs=P("tm", "agent", None), check_vma=False
    )
```

```python
import functools
import math

import jax
import jax.numpy as jnp
from jax import lax
from jax.experimental import pallas as pl
from jax.experimental.pallas import tpu as pltpu
from jax.sharding import PartitionSpec as P

HEADS = 8


negative_floor = -1e30
epsilon = 1e-06


def rms_normed(values):
    wide = values.astype(jnp.float32)
    scale = lax.rsqrt(jnp.mean(wide * wide, axis=-1, keepdims=True) + epsilon)
    return (wide * scale).astype(jnp.bfloat16)


def project(normed, weight):
    return jnp.dot(normed, weight, preferred_element_type=jnp.float32).astype(jnp.bfloat16)


def attend(query, keys, values, allowed):
    batch, query_len, features = query.shape
    key_len = keys.shape[1]
    head_size = features // HEADS
    query_h = query.reshape(batch, query_len, HEADS, head_size)
    keys_h = keys.reshape(batch, key_len, HEADS, head_size)
    values_h = values.reshape(batch, key_len, HEADS, head_size)
    scores = jnp.einsum(
        "bqhe,bkhe->bhqk", query_h, keys_h, preferred_element_type=jnp.float32
    ) * head_size ** (-0.5)
    scores = jnp.where(allowed[:, None], scores, negative_floor)
    largest = jnp.max(scores, axis=-1, keepdims=True)
    weights = jnp.where(allowed[:, None], jnp.exp(scores - largest), 0.0)
    totals = jnp.sum(weights, axis=-1)
    summed = jnp.einsum(
        "bhqk,bkhe->bqhe",
        weights.astype(jnp.bfloat16),
        values_h,
        preferred_element_type=jnp.float32,
    )
    result = summed / jnp.transpose(totals, (0, 2, 1))[..., None]
    return result.reshape(batch, query_len, features).astype(jnp.bfloat16)


def general_time(states, w_query_t, w_key_t, w_value_t, w_out_t):
    local_steps = states.shape[0]
    normed = rms_normed(states)
    query = jnp.swapaxes(project(normed, w_query_t), 0, 1)
    keys = lax.all_gather(project(normed, w_key_t), "tm", axis=0, tiled=True)
    values = lax.all_gather(project(normed, w_value_t), "tm", axis=0, tiled=True)
    query_time = lax.axis_index("tm") * local_steps + jnp.arange(local_steps)
    allowed = (jnp.arange(keys.shape[0])[None, :] <= query_time[:, None])[None]
    mixed = attend(query, jnp.swapaxes(keys, 0, 1), jnp.swapaxes(values, 0, 1), allowed)
    return (
        states.astype(jnp.float32)
        + jnp.dot(jnp.swapaxes(mixed, 0, 1), w_out_t, preferred_element_type=jnp.float32)
    ).astype(jnp.bfloat16)


def general_agent(
    after_time, neighbours, w_query_a, w_key_a, w_value_a, w_out_a, w_in, w_mlp_out
):
    local_steps, local_agents, features = after_time.shape
    second_normed = rms_normed(after_time)
    agent_query = project(second_normed, w_query_a)
    block_count = lax.axis_size("agent")
    chosen_blocks = lax.dynamic_slice_in_dim(neighbours, lax.axis_index("agent"), 1, 0)[0]
    neighbour_count = neighbours.shape[1]
    everyone = lax.all_gather(second_normed, "agent", axis=1, tiled=True)
    picked = jnp.take(
        everyone.reshape(local_steps, block_count, local_agents, features), chosen_blocks, axis=1
    )
    picked = picked.reshape(local_steps, neighbour_count * local_agents, features)
    agent_key = project(picked, w_key_a)
    agent_value = project(picked, w_value_a)
    allowed_all = jnp.ones((1, local_agents, neighbour_count * local_agents), dtype=bool)
    agent_mixed = attend(agent_query, agent_key, agent_value, allowed_all)
    after_agent = (
        after_time.astype(jnp.float32)
        + jnp.dot(agent_mixed, w_out_a, preferred_element_type=jnp.float32)
    ).astype(jnp.bfloat16)
    inner = jax.nn.gelu(
        jnp.dot(rms_normed(after_agent), w_in, preferred_element_type=jnp.float32), approximate=True
    ).astype(jnp.bfloat16)
    final = after_agent.astype(jnp.float32) + jnp.dot(
        inner, w_mlp_out, preferred_element_type=jnp.float32
    )
    return final.astype(jnp.bfloat16)


NT = (((1,), (1,)), ((), ()))
VMEM, HBM = pltpu.VMEM, pltpu.HBM


def spec(space):
    return pl.BlockSpec(memory_space=space)


def norm_of(wide):
    scale = lax.rsqrt(jnp.mean(wide * wide, axis=-1, keepdims=True) + epsilon)
    return (wide * scale).astype(jnp.bfloat16)


def gelu(x):
    inside = x * (math.sqrt(2 / math.pi) + (math.sqrt(2 / math.pi) * 0.044715) * (x * x))
    half = 0.5 * x
    return half + half * jnp.tanh(inside)


def in_hbm(weights):
    return [pltpu.with_memory_space_constraint(w, HBM) for w in weights]


def fetch(sources, targets, sems):
    copies = [
        pltpu.make_async_copy(source, target, sems.at[k])
        for k, (source, target) in enumerate(zip(sources, targets))
    ]
    for copy in copies:
        copy.start()
    return copies


def share_kernel(size, *refs):
    states, outs, sems = refs[0], refs[1 : size + 1], refs[size + 1]
    agents = outs[0].shape[1]
    me = lax.axis_index("tm")
    copies = []
    for k, out in enumerate(outs):
        at = pl.ds(pl.multiple_of(jnp.bitwise_xor(me, k) * agents, agents), agents)
        copies.append(pltpu.make_async_copy(states.at[:, at, :], out, sems.at[k]))
    for copy in copies:
        copy.start()
    for copy in copies:
        copy.wait()


def share_stage(states, size):
    steps, agents, features = states.shape
    shape = jax.ShapeDtypeStruct((steps, agents // size, features), states.dtype)
    return pl.pallas_call(
        functools.partial(share_kernel, size),
        out_shape=[shape] * size,
        in_specs=[spec(HBM)],
        out_specs=[spec(VMEM)] * size,
        scratch_shapes=[pltpu.SemaphoreType.DMA((size,))],
        compiler_params=pltpu.CompilerParams(vmem_limit_bytes=4 * 2**20),
        cost_estimate=pl.CostEstimate(flops=2 * 10**10, bytes_accessed=10**7, transcendentals=0),
        name="cut_shares",
    )(*in_hbm([states]))


def time_kernel(size, *refs):
    pieces, weights = refs[:size], refs[size : size + 4]
    outs = refs[size + 4 : 2 * size + 4]
    wide, normed, query, keys, values, mixed = refs[2 * size + 4 :]
    w_query, w_key, w_value, w_out = weights
    steps, agents, features = pieces[0].shape
    rows = steps * agents
    total_steps = steps * size
    me = lax.axis_index("tm")
    lanes_of = [slice(c * 128, (c + 1) * 128) for c in range(features // 128)]
    for k in range(size):
        start = pl.multiple_of(jnp.bitwise_xor(me, k) * rows, rows)
        piece = norm_of(pieces[k][...].reshape(rows, features).astype(jnp.float32)).astype(jnp.float32)
        for c, lanes in enumerate(lanes_of):
            wide[c, pl.ds(start, rows), :] = piece[:, lanes]
    for agent in range(agents):
        at = pl.ds(agent, total_steps, stride=agents)
        own = jnp.concatenate([wide[c, at, :] for c in range(len(lanes_of))], axis=1)
        normed[pl.ds(agent * total_steps, total_steps), :] = own.astype(jnp.bfloat16)
    group = 2 * total_steps
    span = -(-group // 128) * 128
    head_size = features // HEADS
    factor = math.log2(math.e) * head_size**-0.5
    query[...] = project(normed[...], w_query[...])
    key = project(normed[...], w_key[...])
    value = project(normed[...], w_value[...])
    even = lax.broadcasted_iota(jnp.int32, (group, features), 1) % (2 * head_size) < head_size
    zero = jnp.zeros((group, features), jnp.bfloat16)
    spare = jnp.zeros((span - group, features), jnp.bfloat16)
    for g in range(agents // 2):
        rows_in = slice(g * group, (g + 1) * group)
        for h, mine in enumerate((even, jnp.logical_not(even))):
            at = (2 * g + h) * span
            keys[at : at + group, :] = jnp.where(mine, key[rows_in], zero)
            values[at : at + group, :] = jnp.where(mine, value[rows_in], zero)
            for target in (keys, values):
                target[at + group : at + span, :] = spare
    row = lax.broadcasted_iota(jnp.int32, (group, span), 0)
    column = lax.broadcasted_iota(jnp.int32, (group, span), 1)
    same = (row >= total_steps) == (column >= total_steps)
    bias = jnp.where(jnp.logical_and(same, column <= row), 0.0, negative_floor)
    second_rows = lax.broadcasted_iota(jnp.int32, (2 * span, 2 * head_size), 0) >= span
    second_lanes = lax.broadcasted_iota(jnp.int32, (2 * span, 2 * head_size), 1) >= head_size
    counts = (second_rows == second_lanes).astype(jnp.bfloat16)
    for g in range(agents // 2):
        at, both = pl.ds(g * group, group), pl.ds(2 * g * span, 2 * span)
        for pair in range(HEADS // 2):
            lanes = pl.ds(pair * 2 * head_size, 2 * head_size)
            scores = lax.dot_general(
                query[at, lanes], keys[both, lanes], NT, preferred_element_type=jnp.float32
            )
            weights = []
            for h in range(2):
                mine = scores[:, h * span : (h + 1) * span] + bias
                largest = jnp.max(mine, axis=-1, keepdims=True)
                weights.append(jnp.exp2((mine - largest) * factor).astype(jnp.bfloat16))
            weights = jnp.concatenate(weights, axis=1)
            value = jnp.concatenate([values[both, lanes], counts], axis=1)
            sums = jnp.dot(weights, value, preferred_element_type=jnp.float32)
            wide_lanes = 2 * head_size
            mixed[at, lanes] = (sums[:, :wide_lanes] / sums[:, wide_lanes:]).astype(jnp.bfloat16)
    added = jnp.dot(mixed[...], w_out[...], preferred_element_type=jnp.float32)
    for agent in range(agents):
        at = pl.ds(agent, total_steps, stride=agents)
        mine = added[agent * total_steps : (agent + 1) * total_steps]
        for c, lanes in enumerate(lanes_of):
            wide[c, at, :] = mine[:, lanes]
    for k in range(size):
        start = pl.multiple_of(jnp.bitwise_xor(me, k) * rows, rows)
        piece = jnp.concatenate(
            [wide[c, pl.ds(start, rows), :] for c in range(len(lanes_of))], axis=1
        )
        piece = piece + pieces[k][...].reshape(rows, features).astype(jnp.float32)
        outs[k][...] = piece.astype(jnp.bfloat16).reshape(pieces[0].shape)


def time_stage(pieces, weights):
    size = len(pieces)
    steps, agents, features = pieces[0].shape
    rows = steps * agents * size
    kind = jnp.bfloat16
    return pl.pallas_call(
        functools.partial(time_kernel, size),
        out_shape=[jax.ShapeDtypeStruct((steps, agents, features), kind)] * size,
        in_specs=[spec(VMEM)] * (size + 4),
        out_specs=[spec(VMEM)] * size,
        scratch_shapes=[VMEM((features // 128, rows, 128), jnp.float32)]
        + [VMEM((rows, features), kind)] * 2
        + [VMEM((agents * (-(-2 * steps * size // 128) * 128), features), kind)] * 2
        + [VMEM((rows, features), kind)],
        compiler_params=pltpu.CompilerParams(vmem_limit_bytes=24 * 2**20),
        cost_estimate=pl.CostEstimate(
            flops=8 * rows * features * features,
            bytes_accessed=2 * (2 * rows + 4 * features) * features,
            transcendentals=rows * HEADS * steps * size,
        ),
        name="time_attention",
    )(*pieces, *weights)


def pack_kernel(size, choose, *refs):
    count = len(choose(0))
    pieces, outs = refs[:size], refs[len(refs) - count :]
    agents = pieces[0].shape[1]
    me, plane = lax.axis_index("tm"), lax.axis_index("agent")
    for out, step in zip(outs, choose(plane)):
        for k in range(size):
            start = pl.multiple_of(jnp.bitwise_xor(me, k) * agents, agents)
            out[pl.ds(start, agents), :] = pieces[k][step]


def pack_stage(pieces, choose, after=()):
    size, count = len(pieces), len(choose(0))
    _, agents, features = pieces[0].shape
    return pl.pallas_call(
        functools.partial(pack_kernel, size, choose),
        out_shape=[jax.ShapeDtypeStruct((agents * size, features), jnp.bfloat16)] * count,
        in_specs=[spec(VMEM)] * size + [spec(pl.ANY)] * len(after),
        out_specs=[spec(VMEM)] * count,
        compiler_params=pltpu.CompilerParams(vmem_limit_bytes=8 * 2**20),
        name="pack_steps",
    )(*pieces, *after)


def agent_body(count, blocks, weights, outs, scratch):
    normed, query, keys, values, mixed, after, inner, w_out, sems = scratch
    w_query, w_key, w_value, far_out, w_in, w_mlp_out = weights
    copies = fetch((far_out,), (w_out,), sems)
    agents, features = blocks[0].shape
    head_size = features // HEADS
    factor = math.log2(math.e) * head_size**-0.5
    for b in range(count):
        normed[pl.ds(b * agents, agents), :] = norm_of(blocks[b][...].astype(jnp.float32))
    query[...] = project(normed[...], w_query[...])
    rows, wide_lanes = count * agents, 2 * head_size
    for weight, target in ((w_key, keys), (w_value, values)):
        found = project(normed[...], weight[...])
        even = lax.broadcasted_iota(jnp.int32, found.shape, 1) % wide_lanes < head_size
        zero = jnp.zeros_like(found)
        target[:rows, :] = jnp.where(even, found, zero)
        target[rows:, :] = jnp.where(even, zero, found)
    second_rows = lax.broadcasted_iota(jnp.int32, (2 * rows, wide_lanes), 0) >= rows
    second_lanes = lax.broadcasted_iota(jnp.int32, (2 * rows, wide_lanes), 1) >= head_size
    counts = (second_rows == second_lanes).astype(jnp.bfloat16)
    for pair, part in [(p, r) for p in range(HEADS // 2) for r in range(2)]:
        lanes = pl.ds(pair * wide_lanes, wide_lanes)
        at = pl.ds(part * (rows // 2), rows // 2)
        weights_of = []
        both = lax.dot_general(query[at, lanes], keys[:, lanes], NT, preferred_element_type=jnp.float32)
        for h in range(2):
            scores = both[:, h * rows : (h + 1) * rows]
            largest = jnp.max(scores, axis=-1, keepdims=True)
            weights_of.append(jnp.exp2((scores - largest) * factor).astype(jnp.bfloat16))
        sums = jnp.dot(
            jnp.concatenate(weights_of, axis=1),
            jnp.concatenate([values[:, lanes], counts], axis=1),
            preferred_element_type=jnp.float32,
        )
        mixed[at, lanes] = (sums[:, :wide_lanes] / sums[:, wide_lanes:]).astype(jnp.bfloat16)
    copies[0].wait()
    for b in range(count):
        at = pl.ds(b * agents, agents)
        if b % 2 == 0:
            two = pl.ds(b * agents, 2 * agents)
            added = jnp.dot(mixed[two, :], w_out[...], preferred_element_type=jnp.float32)
        own = blocks[b][...].astype(jnp.float32) + added[b % 2 * agents : (b % 2 + 1) * agents]
        after[at, :] = own.astype(jnp.bfloat16)
        normed[at, :] = norm_of(after[at, :].astype(jnp.float32))
    hidden = w_in.shape[1]
    for start in range(0, hidden, features):
        inner[:, pl.ds(start, features)] = gelu(
            jnp.dot(
                normed[...], w_in[:, pl.ds(start, features)], preferred_element_type=jnp.float32
            )
        ).astype(jnp.bfloat16)
    final = after[...].astype(jnp.float32) + jnp.dot(
        inner[...], w_mlp_out[...], preferred_element_type=jnp.float32
    )
    for b in range(count):
        outs[b][...] = final[b * agents : (b + 1) * agents].astype(jnp.bfloat16)


def agent_kernel(count, middle_only, *refs):
    blocks, weights = refs[:count], refs[count : count + 6]
    outs, scratch = refs[-9 - count : -9], refs[-9:]

    def run():
        agent_body(count, blocks, weights, outs, scratch)

    if middle_only:
        plane = lax.axis_index("agent")
        pl.when(jnp.logical_or(plane == 1, plane == 2))(run)
    else:
        run()


def agent_stage(blocks, weights, middle_only, after=()):
    count = len(blocks)
    agents, features = blocks[0].shape
    hidden = weights[4].shape[1]
    rows = count * agents
    kind = jnp.bfloat16
    return pl.pallas_call(
        functools.partial(agent_kernel, count, middle_only),
        out_shape=[jax.ShapeDtypeStruct((agents, features), kind)] * count,
        in_specs=[spec(VMEM)] * (count + 3)
        + [spec(HBM)]
        + [spec(VMEM)] * 2
        + [spec(pl.ANY)] * len(after),
        out_specs=[spec(VMEM)] * count,
        scratch_shapes=[VMEM((rows, features), kind)] * 2
        + [VMEM((2 * rows, features), kind)] * 2
        + [VMEM((rows, features), kind)] * 2
        + [VMEM((rows, hidden), kind)]
        + [VMEM(weights[3].shape, kind), pltpu.SemaphoreType.DMA((1,))],
        compiler_params=pltpu.CompilerParams(vmem_limit_bytes=16 * 2**20),
        cost_estimate=pl.CostEstimate(
            flops=2 * rows * features * (4 * features + 2 * hidden + 2 * rows),
            bytes_accessed=2 * rows * features * 8,
            transcendentals=rows * (HEADS * rows + hidden),
        ),
        name="agent_step",
    )(*blocks, *weights[:3], *in_hbm(weights[3:4]), *weights[4:], *after)


def place_kernel(*refs):
    sources, out, sems = [refs[k] for k in (0, 1, 2, 3)], refs[4], refs[5]
    plane = lax.axis_index("agent")
    copies = [
        pltpu.make_async_copy(source, out.at[jnp.bitwise_xor(plane, k)], sems.at[k])
        for k, source in enumerate(sources)
    ]
    for copy in copies:
        copy.start()
    for copy in copies:
        copy.wait()


def place_extra_kernel(*refs):
    sources, out, sems = [refs[k] for k in (0, 1, 2, 3)], refs[5], refs[6]
    plane = lax.axis_index("agent")
    middle = jnp.logical_or(plane == 1, plane == 2)
    low = plane // 2

    def place(one, other):
        rows = one.shape[0] // 4
        copies = []
        for n, (source, step) in enumerate(((one, 4 + low), (other, 5 - low))):
            for part in range(4):
                at = pl.ds(part * rows, rows)
                copies.append(
                    pltpu.make_async_copy(source.at[at], out.at[step, at], sems.at[n, part])
                )
        for copy in copies:
            copy.start()
        for copy in copies:
            copy.wait()

    pl.when(middle)(lambda: place(sources[0], sources[3]))
    pl.when(jnp.logical_not(middle))(lambda: place(sources[1], sources[2]))


def place_stage(whole, extra):
    agents, features = whole[0].shape
    shape = jax.ShapeDtypeStruct((6, agents, features), jnp.bfloat16)
    begun = pl.pallas_call(
        place_kernel,
        out_shape=shape,
        in_specs=[spec(VMEM)] * 4,
        out_specs=spec(HBM),
        scratch_shapes=[pltpu.SemaphoreType.DMA((4,))],
        compiler_params=pltpu.CompilerParams(vmem_limit_bytes=4 * 2**20),
        name="place_steps",
    )(*[whole[k] for k in (0, 1, 2, 3)])
    return pl.pallas_call(
        place_extra_kernel,
        out_shape=shape,
        in_specs=[spec(VMEM)] * 4 + [spec(HBM)],
        out_specs=spec(HBM),
        input_output_aliases={4: 0},
        scratch_shapes=[pltpu.SemaphoreType.DMA((2, 4))],
        compiler_params=pltpu.CompilerParams(vmem_limit_bytes=4 * 2**20),
        name="place_extra",
    )(*[extra[k] for k in (0, 1, 2, 3)], begun)


def xor_pairs(size, k, targets=None):
    return [(j, j ^ k) for j in range(size) if targets is None or j ^ k in targets]


def exchange(parts, axis, targets=None, ordered=False):
    size = len(parts)
    moved = {}
    for k in range(size - 1, 0, -1):
        part = parts[k]
        if ordered and k == 1:
            part, moved[size - 1] = lax.optimization_barrier((part, moved[size - 1]))
        moved[k] = lax.ppermute(part, axis, xor_pairs(size, k, targets))
    return [parts[0]] + [moved[k] for k in range(1, size)]


def together(parts):
    return lax.optimization_barrier(tuple(parts[::-1]))[::-1]


def picked(plane, values):
    result = jnp.int32(values[0])
    for place in range(1, len(values)):
        result = jnp.where(plane == place, values[place], result)
    return result


def whole_steps(plane):
    return [jnp.bitwise_xor(plane, k) for k in range(4)]


def extra_steps(plane):
    return [
        4 + picked(plane, (0, 0, 1, 0)),
        4 + picked(plane, (0, 0, 0, 1)),
        4 + picked(plane, (1, 0, 0, 0)),
        4 + picked(plane, (0, 1, 0, 0)),
    ]


def local(
    states,
    neighbours,
    w_query_t,
    w_key_t,
    w_value_t,
    w_out_t,
    w_query_a,
    w_key_a,
    w_value_a,
    w_out_a,
    w_in,
    w_mlp_out,
):
    local_steps, local_agents, features = states.shape
    size, planes = lax.axis_size("tm"), lax.axis_size("agent")
    share = local_agents // size
    time_weights = (w_query_t, w_key_t, w_value_t, w_out_t)
    agent_weights = (w_query_a, w_key_a, w_value_a, w_out_a, w_in, w_mlp_out)
    fits = (
        size & (size - 1) == 0
        and share * size == local_agents
        and share % 16 == 0
        and planes == 4
        and neighbours.shape == (4, 4)
        and local_steps == 6
    )
    if not fits:
        after_time = general_time(states, *time_weights)
        return general_agent(after_time, neighbours, *agent_weights)

    pieces = together(exchange(share_stage(states, size), "tm", ordered=True))
    pieces = together(exchange(time_stage(pieces, time_weights), "tm", ordered=True))
    blocks_a = exchange(pack_stage(pieces, whole_steps), "agent")
    blocks_b = exchange(pack_stage(pieces, extra_steps, blocks_a[2:3]), "agent", (1, 2))

    result_a = agent_stage(blocks_a, agent_weights, False)
    done_a = exchange(result_a, "agent")
    result_b = agent_stage(blocks_b, agent_weights, True, result_a[:1])
    done_b = [result_b[0]] + [
        lax.ppermute(result_b[k], "agent", [(j, j ^ k) for j in (1, 2)]) for k in (1, 2, 3)
    ]
    return place_stage(done_a, done_b)


def solution(mesh):
    placed = (P("tm", "agent", None), P(), P(), P(), P(), P(), P(), P(), P(), P(), P(), P())
    return jax.shard_map(
        local, mesh=mesh, in_specs=placed, out_specs=P("tm", "agent", None), check_vma=False
    )
```

```python
import functools
import math

import jax
import jax.numpy as jnp
from jax import lax
from jax.experimental import pallas as pl
from jax.experimental.pallas import tpu as pltpu
from jax.sharding import PartitionSpec as P

HEADS = 8


negative_floor = -1e30
epsilon = 1e-06


def rms_normed(values):
    wide = values.astype(jnp.float32)
    scale = lax.rsqrt(jnp.mean(wide * wide, axis=-1, keepdims=True) + epsilon)
    return (wide * scale).astype(jnp.bfloat16)


def project(normed, weight):
    return jnp.dot(normed, weight, preferred_element_type=jnp.float32).astype(jnp.bfloat16)


def attend(query, keys, values, allowed):
    batch, query_len, features = query.shape
    key_len = keys.shape[1]
    head_size = features // HEADS
    query_h = query.reshape(batch, query_len, HEADS, head_size)
    keys_h = keys.reshape(batch, key_len, HEADS, head_size)
    values_h = values.reshape(batch, key_len, HEADS, head_size)
    scores = jnp.einsum(
        "bqhe,bkhe->bhqk", query_h, keys_h, preferred_element_type=jnp.float32
    ) * head_size ** (-0.5)
    scores = jnp.where(allowed[:, None], scores, negative_floor)
    largest = jnp.max(scores, axis=-1, keepdims=True)
    weights = jnp.where(allowed[:, None], jnp.exp(scores - largest), 0.0)
    totals = jnp.sum(weights, axis=-1)
    summed = jnp.einsum(
        "bhqk,bkhe->bqhe",
        weights.astype(jnp.bfloat16),
        values_h,
        preferred_element_type=jnp.float32,
    )
    result = summed / jnp.transpose(totals, (0, 2, 1))[..., None]
    return result.reshape(batch, query_len, features).astype(jnp.bfloat16)


def general_time(states, w_query_t, w_key_t, w_value_t, w_out_t):
    local_steps = states.shape[0]
    normed = rms_normed(states)
    query = jnp.swapaxes(project(normed, w_query_t), 0, 1)
    keys = lax.all_gather(project(normed, w_key_t), "tm", axis=0, tiled=True)
    values = lax.all_gather(project(normed, w_value_t), "tm", axis=0, tiled=True)
    query_time = lax.axis_index("tm") * local_steps + jnp.arange(local_steps)
    allowed = (jnp.arange(keys.shape[0])[None, :] <= query_time[:, None])[None]
    mixed = attend(query, jnp.swapaxes(keys, 0, 1), jnp.swapaxes(values, 0, 1), allowed)
    return (
        states.astype(jnp.float32)
        + jnp.dot(jnp.swapaxes(mixed, 0, 1), w_out_t, preferred_element_type=jnp.float32)
    ).astype(jnp.bfloat16)


def general_agent(
    after_time, neighbours, w_query_a, w_key_a, w_value_a, w_out_a, w_in, w_mlp_out
):
    local_steps, local_agents, features = after_time.shape
    second_normed = rms_normed(after_time)
    agent_query = project(second_normed, w_query_a)
    block_count = lax.axis_size("agent")
    chosen_blocks = lax.dynamic_slice_in_dim(neighbours, lax.axis_index("agent"), 1, 0)[0]
    neighbour_count = neighbours.shape[1]
    everyone = lax.all_gather(second_normed, "agent", axis=1, tiled=True)
    picked = jnp.take(
        everyone.reshape(local_steps, block_count, local_agents, features), chosen_blocks, axis=1
    )
    picked = picked.reshape(local_steps, neighbour_count * local_agents, features)
    agent_key = project(picked, w_key_a)
    agent_value = project(picked, w_value_a)
    allowed_all = jnp.ones((1, local_agents, neighbour_count * local_agents), dtype=bool)
    agent_mixed = attend(agent_query, agent_key, agent_value, allowed_all)
    after_agent = (
        after_time.astype(jnp.float32)
        + jnp.dot(agent_mixed, w_out_a, preferred_element_type=jnp.float32)
    ).astype(jnp.bfloat16)
    inner = jax.nn.gelu(
        jnp.dot(rms_normed(after_agent), w_in, preferred_element_type=jnp.float32), approximate=True
    ).astype(jnp.bfloat16)
    final = after_agent.astype(jnp.float32) + jnp.dot(
        inner, w_mlp_out, preferred_element_type=jnp.float32
    )
    return final.astype(jnp.bfloat16)


NT = (((1,), (1,)), ((), ()))
VMEM, HBM = pltpu.VMEM, pltpu.HBM


def spec(space):
    return pl.BlockSpec(memory_space=space)


def norm_of(wide):
    scale = lax.rsqrt(jnp.mean(wide * wide, axis=-1, keepdims=True) + epsilon)
    return (wide * scale).astype(jnp.bfloat16)


def gelu(x):
    inside = x * (math.sqrt(2 / math.pi) + (math.sqrt(2 / math.pi) * 0.044715) * (x * x))
    half = 0.5 * x
    return half + half * jnp.tanh(inside)


def in_hbm(weights):
    return [pltpu.with_memory_space_constraint(w, HBM) for w in weights]


def fetch(sources, targets, sems):
    copies = [
        pltpu.make_async_copy(source, target, sems.at[k])
        for k, (source, target) in enumerate(zip(sources, targets))
    ]
    for copy in copies:
        copy.start()
    return copies


def share_kernel(size, *refs):
    states, outs, sems = refs[0], refs[1 : size + 1], refs[size + 1]
    agents = outs[0].shape[1]
    me = lax.axis_index("tm")
    copies = []
    for k, out in enumerate(outs):
        at = pl.ds(pl.multiple_of(jnp.bitwise_xor(me, k) * agents, agents), agents)
        copies.append(pltpu.make_async_copy(states.at[:, at, :], out, sems.at[k]))
    for copy in copies:
        copy.start()
    for copy in copies:
        copy.wait()


def share_stage(states, size):
    steps, agents, features = states.shape
    shape = jax.ShapeDtypeStruct((steps, agents // size, features), states.dtype)
    return pl.pallas_call(
        functools.partial(share_kernel, size),
        out_shape=[shape] * size,
        in_specs=[spec(HBM)],
        out_specs=[spec(VMEM)] * size,
        scratch_shapes=[pltpu.SemaphoreType.DMA((size,))],
        compiler_params=pltpu.CompilerParams(vmem_limit_bytes=4 * 2**20),
        cost_estimate=pl.CostEstimate(flops=2 * 10**10, bytes_accessed=10**7, transcendentals=0),
        name="cut_shares",
    )(*in_hbm([states]))


def time_kernel(size, *refs):
    pieces, weights = refs[:size], refs[size : size + 4]
    outs = refs[size + 4 : 2 * size + 4]
    wide, normed, query, keys, values, mixed = refs[2 * size + 4 :]
    w_query, w_key, w_value, w_out = weights
    steps, agents, features = pieces[0].shape
    rows = steps * agents
    total_steps = steps * size
    me = lax.axis_index("tm")
    lanes_of = [slice(c * 128, (c + 1) * 128) for c in range(features // 128)]
    for k in range(size):
        start = pl.multiple_of(jnp.bitwise_xor(me, k) * rows, rows)
        piece = norm_of(pieces[k][...].reshape(rows, features).astype(jnp.float32)).astype(jnp.float32)
        for c, lanes in enumerate(lanes_of):
            wide[c, pl.ds(start, rows), :] = piece[:, lanes]
    for agent in range(agents):
        at = pl.ds(agent, total_steps, stride=agents)
        own = jnp.concatenate([wide[c, at, :] for c in range(len(lanes_of))], axis=1)
        normed[pl.ds(agent * total_steps, total_steps), :] = own.astype(jnp.bfloat16)
    group = 2 * total_steps
    span = -(-group // 128) * 128
    head_size = features // HEADS
    factor = math.log2(math.e) * head_size**-0.5
    query[...] = project(normed[...], w_query[...])
    key = project(normed[...], w_key[...])
    value = project(normed[...], w_value[...])
    even = lax.broadcasted_iota(jnp.int32, (group, features), 1) % (2 * head_size) < head_size
    zero = jnp.zeros((group, features), jnp.bfloat16)
    spare = jnp.zeros((span - group, features), jnp.bfloat16)
    for g in range(agents // 2):
        rows_in = slice(g * group, (g + 1) * group)
        for h, mine in enumerate((even, jnp.logical_not(even))):
            at = (2 * g + h) * span
            keys[at : at + group, :] = jnp.where(mine, key[rows_in], zero)
            values[at : at + group, :] = jnp.where(mine, value[rows_in], zero)
            for target in (keys, values):
                target[at + group : at + span, :] = spare
    row = lax.broadcasted_iota(jnp.int32, (group, span), 0)
    column = lax.broadcasted_iota(jnp.int32, (group, span), 1)
    same = (row >= total_steps) == (column >= total_steps)
    bias = jnp.where(jnp.logical_and(same, column <= row), 0.0, negative_floor)
    second_rows = lax.broadcasted_iota(jnp.int32, (2 * span, 2 * head_size), 0) >= span
    second_lanes = lax.broadcasted_iota(jnp.int32, (2 * span, 2 * head_size), 1) >= head_size
    counts = (second_rows == second_lanes).astype(jnp.bfloat16)
    for g in range(agents // 2):
        at, both = pl.ds(g * group, group), pl.ds(2 * g * span, 2 * span)
        for pair in range(HEADS // 2):
            lanes = pl.ds(pair * 2 * head_size, 2 * head_size)
            scores = lax.dot_general(
                query[at, lanes], keys[both, lanes], NT, preferred_element_type=jnp.float32
            )
            weights = []
            for h in range(2):
                mine = scores[:, h * span : (h + 1) * span] + bias
                largest = jnp.max(mine, axis=-1, keepdims=True)
                weights.append(jnp.exp2((mine - largest) * factor).astype(jnp.bfloat16))
            weights = jnp.concatenate(weights, axis=1)
            value = jnp.concatenate([values[both, lanes], counts], axis=1)
            sums = jnp.dot(weights, value, preferred_element_type=jnp.float32)
            wide_lanes = 2 * head_size
            mixed[at, lanes] = (sums[:, :wide_lanes] / sums[:, wide_lanes:]).astype(jnp.bfloat16)
    added = jnp.dot(mixed[...], w_out[...], preferred_element_type=jnp.float32)
    for agent in range(agents):
        at = pl.ds(agent, total_steps, stride=agents)
        mine = added[agent * total_steps : (agent + 1) * total_steps]
        for c, lanes in enumerate(lanes_of):
            wide[c, at, :] = mine[:, lanes]
    for k in range(size):
        start = pl.multiple_of(jnp.bitwise_xor(me, k) * rows, rows)
        piece = jnp.concatenate(
            [wide[c, pl.ds(start, rows), :] for c in range(len(lanes_of))], axis=1
        )
        piece = piece + pieces[k][...].reshape(rows, features).astype(jnp.float32)
        outs[k][...] = piece.astype(jnp.bfloat16).reshape(pieces[0].shape)


def time_stage(pieces, weights):
    size = len(pieces)
    steps, agents, features = pieces[0].shape
    rows = steps * agents * size
    kind = jnp.bfloat16
    return pl.pallas_call(
        functools.partial(time_kernel, size),
        out_shape=[jax.ShapeDtypeStruct((steps, agents, features), kind)] * size,
        in_specs=[spec(VMEM)] * (size + 4),
        out_specs=[spec(VMEM)] * size,
        scratch_shapes=[VMEM((features // 128, rows, 128), jnp.float32)]
        + [VMEM((rows, features), kind)] * 2
        + [VMEM((agents * (-(-2 * steps * size // 128) * 128), features), kind)] * 2
        + [VMEM((rows, features), kind)],
        compiler_params=pltpu.CompilerParams(vmem_limit_bytes=24 * 2**20),
        cost_estimate=pl.CostEstimate(
            flops=8 * rows * features * features,
            bytes_accessed=2 * (2 * rows + 4 * features) * features,
            transcendentals=rows * HEADS * steps * size,
        ),
        name="time_attention",
    )(*pieces, *weights)


def pack_kernel(size, choose, *refs):
    count = len(choose(0))
    pieces, outs = refs[:size], refs[len(refs) - count :]
    agents = pieces[0].shape[1]
    me, plane = lax.axis_index("tm"), lax.axis_index("agent")
    for out, step in zip(outs, choose(plane)):
        for k in range(size):
            start = pl.multiple_of(jnp.bitwise_xor(me, k) * agents, agents)
            out[pl.ds(start, agents), :] = pieces[k][step]


def pack_stage(pieces, choose, after=()):
    size, count = len(pieces), len(choose(0))
    _, agents, features = pieces[0].shape
    return pl.pallas_call(
        functools.partial(pack_kernel, size, choose),
        out_shape=[jax.ShapeDtypeStruct((agents * size, features), jnp.bfloat16)] * count,
        in_specs=[spec(VMEM)] * size + [spec(pl.ANY)] * len(after),
        out_specs=[spec(VMEM)] * count,
        compiler_params=pltpu.CompilerParams(vmem_limit_bytes=8 * 2**20),
        name="pack_steps",
    )(*pieces, *after)


def near_kernel(count, *refs):
    blocks, weights = refs[:count], refs[count : count + 3]
    outs, normed = refs[count + 3 : count + 6], refs[-1]
    agents = blocks[0].shape[0]
    for b, block in enumerate(blocks):
        normed[pl.ds(b * agents, agents), :] = norm_of(block[...].astype(jnp.float32))
    for weight, out in zip(weights, outs):
        out[...] = project(normed[...], weight[...])


def near_stage(blocks, weights):
    count = len(blocks)
    agents, features = blocks[0].shape
    shape = (count * agents, features)
    return pl.pallas_call(
        functools.partial(near_kernel, count),
        out_shape=[jax.ShapeDtypeStruct(shape, jnp.bfloat16)] * 3,
        in_specs=[spec(VMEM)] * (count + 3),
        out_specs=[spec(VMEM)] * 3,
        scratch_shapes=[VMEM(shape, jnp.bfloat16)],
        compiler_params=pltpu.CompilerParams(vmem_limit_bytes=8 * 2**20),
        name="near_blocks",
    )(*blocks, *weights)


def agent_body(count, blocks, weights, given, outs, scratch):
    normed, query, keys, values, mixed, after, inner, w_out, sems = scratch
    w_query, w_key, w_value, far_out, w_in, w_mlp_out = weights
    copies = fetch((far_out,), (w_out,), sems)
    agents, features = blocks[0].shape
    head_size = features // HEADS
    factor = math.log2(math.e) * head_size**-0.5
    rows, wide_lanes = count * agents, 2 * head_size
    ready = given[0].shape[0] if given else 0
    rest = pl.ds(ready, rows - ready)
    for b in range(ready // agents, count):
        normed[pl.ds(b * agents, agents), :] = norm_of(blocks[b][...].astype(jnp.float32))
    query[rest, :] = project(normed[rest, :], w_query[...])
    if given:
        query[:ready, :] = given[0][...]
    for n, (weight, target) in enumerate(((w_key, keys), (w_value, values))):
        parts = [(ready, project(normed[rest, :], weight[...]))]
        if given:
            parts.append((0, given[n + 1][...]))
        for start, found in parts:
            even = lax.broadcasted_iota(jnp.int32, found.shape, 1) % wide_lanes < head_size
            zero = jnp.zeros_like(found)
            length = found.shape[0]
            target[start : start + length, :] = jnp.where(even, found, zero)
            target[rows + start : rows + start + length, :] = jnp.where(even, zero, found)
    second_rows = lax.broadcasted_iota(jnp.int32, (2 * rows, wide_lanes), 0) >= rows
    second_lanes = lax.broadcasted_iota(jnp.int32, (2 * rows, wide_lanes), 1) >= head_size
    counts = (second_rows == second_lanes).astype(jnp.bfloat16)
    for pair, part in [(p, r) for p in range(HEADS // 2) for r in range(2)]:
        lanes = pl.ds(pair * wide_lanes, wide_lanes)
        at = pl.ds(part * (rows // 2), rows // 2)
        weights_of = []
        both = lax.dot_general(query[at, lanes], keys[:, lanes], NT, preferred_element_type=jnp.float32)
        for h in range(2):
            scores = both[:, h * rows : (h + 1) * rows]
            largest = jnp.max(scores, axis=-1, keepdims=True)
            weights_of.append(jnp.exp2((scores - largest) * factor).astype(jnp.bfloat16))
        sums = jnp.dot(
            jnp.concatenate(weights_of, axis=1),
            jnp.concatenate([values[:, lanes], counts], axis=1),
            preferred_element_type=jnp.float32,
        )
        mixed[at, lanes] = (sums[:, :wide_lanes] / sums[:, wide_lanes:]).astype(jnp.bfloat16)
    copies[0].wait()
    for b in range(count):
        at = pl.ds(b * agents, agents)
        if b % 2 == 0:
            two = pl.ds(b * agents, 2 * agents)
            added = jnp.dot(mixed[two, :], w_out[...], preferred_element_type=jnp.float32)
        own = blocks[b][...].astype(jnp.float32) + added[b % 2 * agents : (b % 2 + 1) * agents]
        after[at, :] = own.astype(jnp.bfloat16)
        normed[at, :] = norm_of(after[at, :].astype(jnp.float32))
    hidden = w_in.shape[1]
    for start in range(0, hidden, features):
        inner[:, pl.ds(start, features)] = gelu(
            jnp.dot(
                normed[...], w_in[:, pl.ds(start, features)], preferred_element_type=jnp.float32
            )
        ).astype(jnp.bfloat16)
    final = after[...].astype(jnp.float32) + jnp.dot(
        inner[...], w_mlp_out[...], preferred_element_type=jnp.float32
    )
    for b in range(count):
        outs[b][...] = final[b * agents : (b + 1) * agents].astype(jnp.bfloat16)


def agent_kernel(count, ready, middle_only, *refs):
    blocks, weights = refs[:count], refs[count : count + 6]
    given = refs[count + 6 : count + 6 + ready]
    outs, scratch = refs[-9 - count : -9], refs[-9:]

    def run():
        agent_body(count, blocks, weights, given, outs, scratch)

    if middle_only:
        plane = lax.axis_index("agent")
        pl.when(jnp.logical_or(plane == 1, plane == 2))(run)
    else:
        run()


def agent_stage(blocks, weights, middle_only, after=(), given=()):
    count = len(blocks)
    agents, features = blocks[0].shape
    hidden = weights[4].shape[1]
    rows = count * agents
    kind = jnp.bfloat16
    return pl.pallas_call(
        functools.partial(agent_kernel, count, len(given), middle_only),
        out_shape=[jax.ShapeDtypeStruct((agents, features), kind)] * count,
        in_specs=[spec(VMEM)] * (count + 3)
        + [spec(HBM)]
        + [spec(VMEM)] * (2 + len(given))
        + [spec(pl.ANY)] * len(after),
        out_specs=[spec(VMEM)] * count,
        scratch_shapes=[VMEM((rows, features), kind)] * 2
        + [VMEM((2 * rows, features), kind)] * 2
        + [VMEM((rows, features), kind)] * 2
        + [VMEM((rows, hidden), kind)]
        + [VMEM(weights[3].shape, kind), pltpu.SemaphoreType.DMA((1,))],
        compiler_params=pltpu.CompilerParams(vmem_limit_bytes=16 * 2**20),
        cost_estimate=pl.CostEstimate(
            flops=2 * rows * features * (4 * features + 2 * hidden + 2 * rows),
            bytes_accessed=2 * rows * features * 8,
            transcendentals=rows * (HEADS * rows + hidden),
        ),
        name="agent_step",
    )(*blocks, *weights[:3], *in_hbm(weights[3:4]), *weights[4:], *given, *after)


def place_kernel(*refs):
    sources, out, sems = [refs[k] for k in (0, 1, 2, 3)], refs[4], refs[5]
    plane = lax.axis_index("agent")
    copies = [
        pltpu.make_async_copy(source, out.at[jnp.bitwise_xor(plane, k)], sems.at[k])
        for k, source in enumerate(sources)
    ]
    for copy in copies:
        copy.start()
    for copy in copies:
        copy.wait()


def place_extra_kernel(*refs):
    sources, out, sems = [refs[k] for k in (0, 1, 2, 3)], refs[5], refs[6]
    plane = lax.axis_index("agent")
    middle = jnp.logical_or(plane == 1, plane == 2)
    low = plane // 2

    def place(one, other):
        rows = one.shape[0] // 4
        copies = []
        for n, (source, step) in enumerate(((one, 4 + low), (other, 5 - low))):
            for part in range(4):
                at = pl.ds(part * rows, rows)
                copies.append(
                    pltpu.make_async_copy(source.at[at], out.at[step, at], sems.at[n, part])
                )
        for copy in copies:
            copy.start()
        for copy in copies:
            copy.wait()

    pl.when(middle)(lambda: place(sources[0], sources[3]))
    pl.when(jnp.logical_not(middle))(lambda: place(sources[1], sources[2]))


def place_stage(whole, extra):
    agents, features = whole[0].shape
    shape = jax.ShapeDtypeStruct((6, agents, features), jnp.bfloat16)
    begun = pl.pallas_call(
        place_kernel,
        out_shape=shape,
        in_specs=[spec(VMEM)] * 4,
        out_specs=spec(HBM),
        scratch_shapes=[pltpu.SemaphoreType.DMA((4,))],
        compiler_params=pltpu.CompilerParams(vmem_limit_bytes=4 * 2**20),
        name="place_steps",
    )(*[whole[k] for k in (0, 1, 2, 3)])
    return pl.pallas_call(
        place_extra_kernel,
        out_shape=shape,
        in_specs=[spec(VMEM)] * 4 + [spec(HBM)],
        out_specs=spec(HBM),
        input_output_aliases={4: 0},
        scratch_shapes=[pltpu.SemaphoreType.DMA((2, 4))],
        compiler_params=pltpu.CompilerParams(vmem_limit_bytes=4 * 2**20),
        name="place_extra",
    )(*[extra[k] for k in (0, 1, 2, 3)], begun)


def xor_pairs(size, k, targets=None):
    return [(j, j ^ k) for j in range(size) if targets is None or j ^ k in targets]


def exchange(parts, axis, targets=None, ordered=False):
    size = len(parts)
    moved = {}
    for k in range(size - 1, 0, -1):
        part = parts[k]
        if ordered and k == 1:
            part, moved[size - 1] = lax.optimization_barrier((part, moved[size - 1]))
        moved[k] = lax.ppermute(part, axis, xor_pairs(size, k, targets))
    return [parts[0]] + [moved[k] for k in range(1, size)]


def together(parts):
    return lax.optimization_barrier(tuple(parts[::-1]))[::-1]


def picked(plane, values):
    result = jnp.int32(values[0])
    for place in range(1, len(values)):
        result = jnp.where(plane == place, values[place], result)
    return result


def whole_steps(plane):
    return [jnp.bitwise_xor(plane, k) for k in range(4)]


def extra_steps(plane):
    return [
        4 + picked(plane, (0, 0, 1, 0)),
        4 + picked(plane, (0, 0, 0, 1)),
        4 + picked(plane, (1, 0, 0, 0)),
        4 + picked(plane, (0, 1, 0, 0)),
    ]


def local(
    states,
    neighbours,
    w_query_t,
    w_key_t,
    w_value_t,
    w_out_t,
    w_query_a,
    w_key_a,
    w_value_a,
    w_out_a,
    w_in,
    w_mlp_out,
):
    local_steps, local_agents, features = states.shape
    size, planes = lax.axis_size("tm"), lax.axis_size("agent")
    share = local_agents // size
    time_weights = (w_query_t, w_key_t, w_value_t, w_out_t)
    agent_weights = (w_query_a, w_key_a, w_value_a, w_out_a, w_in, w_mlp_out)
    fits = (
        size & (size - 1) == 0
        and share * size == local_agents
        and share % 16 == 0
        and planes == 4
        and neighbours.shape == (4, 4)
        and local_steps == 6
    )
    if not fits:
        after_time = general_time(states, *time_weights)
        return general_agent(after_time, neighbours, *agent_weights)

    pieces = together(exchange(share_stage(states, size), "tm", ordered=True))
    pieces = together(exchange(time_stage(pieces, time_weights), "tm", ordered=True))
    blocks_a = exchange(pack_stage(pieces, whole_steps), "agent")
    blocks_b = exchange(pack_stage(pieces, extra_steps, blocks_a[2:3]), "agent", (1, 2))

    near = near_stage(blocks_a[:3], agent_weights[:3])
    result_a = agent_stage(blocks_a, agent_weights, False, (), near)
    done_a = exchange(result_a, "agent")
    result_b = agent_stage(blocks_b, agent_weights, True, result_a[:1])
    done_b = [result_b[0]] + [
        lax.ppermute(result_b[k], "agent", [(j, j ^ k) for j in (1, 2)]) for k in (1, 2, 3)
    ]
    return place_stage(done_a, done_b)


def solution(mesh):
    placed = (P("tm", "agent", None), P(), P(), P(), P(), P(), P(), P(), P(), P(), P(), P())
    return jax.shard_map(
        local, mesh=mesh, in_specs=placed, out_specs=P("tm", "agent", None), check_vma=False
    )
```

```python
import functools
import math

import jax
import jax.numpy as jnp
from jax import lax
from jax.experimental import pallas as pl
from jax.experimental.pallas import tpu as pltpu
from jax.sharding import PartitionSpec as P

HEADS = 8


negative_floor = -1e30
epsilon = 1e-06


def rms_normed(values):
    wide = values.astype(jnp.float32)
    scale = lax.rsqrt(jnp.mean(wide * wide, axis=-1, keepdims=True) + epsilon)
    return (wide * scale).astype(jnp.bfloat16)


def project(normed, weight):
    return jnp.dot(normed, weight, preferred_element_type=jnp.float32).astype(jnp.bfloat16)


def attend(query, keys, values, allowed):
    batch, query_len, features = query.shape
    key_len = keys.shape[1]
    head_size = features // HEADS
    query_h = query.reshape(batch, query_len, HEADS, head_size)
    keys_h = keys.reshape(batch, key_len, HEADS, head_size)
    values_h = values.reshape(batch, key_len, HEADS, head_size)
    scores = jnp.einsum(
        "bqhe,bkhe->bhqk", query_h, keys_h, preferred_element_type=jnp.float32
    ) * head_size ** (-0.5)
    scores = jnp.where(allowed[:, None], scores, negative_floor)
    largest = jnp.max(scores, axis=-1, keepdims=True)
    weights = jnp.where(allowed[:, None], jnp.exp(scores - largest), 0.0)
    totals = jnp.sum(weights, axis=-1)
    summed = jnp.einsum(
        "bhqk,bkhe->bqhe",
        weights.astype(jnp.bfloat16),
        values_h,
        preferred_element_type=jnp.float32,
    )
    result = summed / jnp.transpose(totals, (0, 2, 1))[..., None]
    return result.reshape(batch, query_len, features).astype(jnp.bfloat16)


def general_time(states, w_query_t, w_key_t, w_value_t, w_out_t):
    local_steps = states.shape[0]
    normed = rms_normed(states)
    query = jnp.swapaxes(project(normed, w_query_t), 0, 1)
    keys = lax.all_gather(project(normed, w_key_t), "tm", axis=0, tiled=True)
    values = lax.all_gather(project(normed, w_value_t), "tm", axis=0, tiled=True)
    query_time = lax.axis_index("tm") * local_steps + jnp.arange(local_steps)
    allowed = (jnp.arange(keys.shape[0])[None, :] <= query_time[:, None])[None]
    mixed = attend(query, jnp.swapaxes(keys, 0, 1), jnp.swapaxes(values, 0, 1), allowed)
    return (
        states.astype(jnp.float32)
        + jnp.dot(jnp.swapaxes(mixed, 0, 1), w_out_t, preferred_element_type=jnp.float32)
    ).astype(jnp.bfloat16)


def general_agent(
    after_time, neighbours, w_query_a, w_key_a, w_value_a, w_out_a, w_in, w_mlp_out
):
    local_steps, local_agents, features = after_time.shape
    second_normed = rms_normed(after_time)
    agent_query = project(second_normed, w_query_a)
    block_count = lax.axis_size("agent")
    chosen_blocks = lax.dynamic_slice_in_dim(neighbours, lax.axis_index("agent"), 1, 0)[0]
    neighbour_count = neighbours.shape[1]
    everyone = lax.all_gather(second_normed, "agent", axis=1, tiled=True)
    picked = jnp.take(
        everyone.reshape(local_steps, block_count, local_agents, features), chosen_blocks, axis=1
    )
    picked = picked.reshape(local_steps, neighbour_count * local_agents, features)
    agent_key = project(picked, w_key_a)
    agent_value = project(picked, w_value_a)
    allowed_all = jnp.ones((1, local_agents, neighbour_count * local_agents), dtype=bool)
    agent_mixed = attend(agent_query, agent_key, agent_value, allowed_all)
    after_agent = (
        after_time.astype(jnp.float32)
        + jnp.dot(agent_mixed, w_out_a, preferred_element_type=jnp.float32)
    ).astype(jnp.bfloat16)
    inner = jax.nn.gelu(
        jnp.dot(rms_normed(after_agent), w_in, preferred_element_type=jnp.float32), approximate=True
    ).astype(jnp.bfloat16)
    final = after_agent.astype(jnp.float32) + jnp.dot(
        inner, w_mlp_out, preferred_element_type=jnp.float32
    )
    return final.astype(jnp.bfloat16)


NT = (((1,), (1,)), ((), ()))
VMEM, HBM = pltpu.VMEM, pltpu.HBM


def spec(space):
    return pl.BlockSpec(memory_space=space)


def norm_of(wide):
    scale = lax.rsqrt(jnp.mean(wide * wide, axis=-1, keepdims=True) + epsilon)
    return (wide * scale).astype(jnp.bfloat16)


def gelu(x):
    inside = x * (math.sqrt(2 / math.pi) + (math.sqrt(2 / math.pi) * 0.044715) * (x * x))
    half = 0.5 * x
    return half + half * jnp.tanh(inside)


def in_hbm(weights):
    return [pltpu.with_memory_space_constraint(w, HBM) for w in weights]


def fetch(sources, targets, sems):
    copies = [
        pltpu.make_async_copy(source, target, sems.at[k])
        for k, (source, target) in enumerate(zip(sources, targets))
    ]
    for copy in copies:
        copy.start()
    return copies


def share_kernel(size, *refs):
    states, outs, sems = refs[0], refs[1 : size + 1], refs[size + 1]
    agents = outs[0].shape[1]
    me = lax.axis_index("tm")
    copies = []
    for k, out in enumerate(outs):
        at = pl.ds(pl.multiple_of(jnp.bitwise_xor(me, k) * agents, agents), agents)
        copies.append(pltpu.make_async_copy(states.at[:, at, :], out, sems.at[k]))
    for copy in copies:
        copy.start()
    for copy in copies:
        copy.wait()


def share_stage(states, size):
    steps, agents, features = states.shape
    shape = jax.ShapeDtypeStruct((steps, agents // size, features), states.dtype)
    return pl.pallas_call(
        functools.partial(share_kernel, size),
        out_shape=[shape] * size,
        in_specs=[spec(HBM)],
        out_specs=[spec(VMEM)] * size,
        scratch_shapes=[pltpu.SemaphoreType.DMA((size,))],
        compiler_params=pltpu.CompilerParams(vmem_limit_bytes=4 * 2**20),
        cost_estimate=pl.CostEstimate(flops=2 * 10**10, bytes_accessed=10**7, transcendentals=0),
        name="cut_shares",
    )(*in_hbm([states]))


def time_kernel(size, *refs):
    pieces, weights = refs[:size], refs[size : size + 4]
    outs = refs[size + 4 : 2 * size + 4]
    wide, normed, query, keys, values, mixed = refs[2 * size + 4 :]
    w_query, w_key, w_value, w_out = weights
    steps, agents, features = pieces[0].shape
    rows = steps * agents
    total_steps = steps * size
    me = lax.axis_index("tm")
    lanes_of = [slice(c * 128, (c + 1) * 128) for c in range(features // 128)]
    for k in range(size):
        start = pl.multiple_of(jnp.bitwise_xor(me, k) * rows, rows)
        piece = norm_of(pieces[k][...].reshape(rows, features).astype(jnp.float32)).astype(jnp.float32)
        for c, lanes in enumerate(lanes_of):
            wide[c, pl.ds(start, rows), :] = piece[:, lanes]
    for agent in range(agents):
        at = pl.ds(agent, total_steps, stride=agents)
        own = jnp.concatenate([wide[c, at, :] for c in range(len(lanes_of))], axis=1)
        normed[pl.ds(agent * total_steps, total_steps), :] = own.astype(jnp.bfloat16)
    group = 2 * total_steps
    span = -(-group // 128) * 128
    head_size = features // HEADS
    factor = math.log2(math.e) * head_size**-0.5
    query[...] = project(normed[...], w_query[...])
    key = project(normed[...], w_key[...])
    value = project(normed[...], w_value[...])
    even = lax.broadcasted_iota(jnp.int32, (group, features), 1) % (2 * head_size) < head_size
    zero = jnp.zeros((group, features), jnp.bfloat16)
    spare = jnp.zeros((span - group, features), jnp.bfloat16)
    for g in range(agents // 2):
        rows_in = slice(g * group, (g + 1) * group)
        for h, mine in enumerate((even, jnp.logical_not(even))):
            at = (2 * g + h) * span
            keys[at : at + group, :] = jnp.where(mine, key[rows_in], zero)
            values[at : at + group, :] = jnp.where(mine, value[rows_in], zero)
            for target in (keys, values):
                target[at + group : at + span, :] = spare
    row = lax.broadcasted_iota(jnp.int32, (group, span), 0)
    column = lax.broadcasted_iota(jnp.int32, (group, span), 1)
    same = (row >= total_steps) == (column >= total_steps)
    bias = jnp.where(jnp.logical_and(same, column <= row), 0.0, negative_floor)
    second_rows = lax.broadcasted_iota(jnp.int32, (2 * span, 2 * head_size), 0) >= span
    second_lanes = lax.broadcasted_iota(jnp.int32, (2 * span, 2 * head_size), 1) >= head_size
    counts = (second_rows == second_lanes).astype(jnp.bfloat16)
    for g in range(agents // 2):
        at, both = pl.ds(g * group, group), pl.ds(2 * g * span, 2 * span)
        for pair in range(HEADS // 2):
            lanes = pl.ds(pair * 2 * head_size, 2 * head_size)
            scores = lax.dot_general(
                query[at, lanes], keys[both, lanes], NT, preferred_element_type=jnp.float32
            )
            weights = []
            for h in range(2):
                mine = scores[:, h * span : (h + 1) * span] + bias
                largest = jnp.max(mine, axis=-1, keepdims=True)
                weights.append(jnp.exp2((mine - largest) * factor).astype(jnp.bfloat16))
            weights = jnp.concatenate(weights, axis=1)
            value = jnp.concatenate([values[both, lanes], counts], axis=1)
            sums = jnp.dot(weights, value, preferred_element_type=jnp.float32)
            wide_lanes = 2 * head_size
            mixed[at, lanes] = (sums[:, :wide_lanes] / sums[:, wide_lanes:]).astype(jnp.bfloat16)
    added = jnp.dot(mixed[...], w_out[...], preferred_element_type=jnp.float32)
    for agent in range(agents):
        at = pl.ds(agent, total_steps, stride=agents)
        mine = added[agent * total_steps : (agent + 1) * total_steps]
        for c, lanes in enumerate(lanes_of):
            wide[c, at, :] = mine[:, lanes]
    for k in range(size):
        start = pl.multiple_of(jnp.bitwise_xor(me, k) * rows, rows)
        piece = jnp.concatenate(
            [wide[c, pl.ds(start, rows), :] for c in range(len(lanes_of))], axis=1
        )
        piece = piece + pieces[k][...].reshape(rows, features).astype(jnp.float32)
        outs[k][...] = piece.astype(jnp.bfloat16).reshape(pieces[0].shape)


def time_stage(pieces, weights):
    size = len(pieces)
    steps, agents, features = pieces[0].shape
    rows = steps * agents * size
    kind = jnp.bfloat16
    return pl.pallas_call(
        functools.partial(time_kernel, size),
        out_shape=[jax.ShapeDtypeStruct((steps, agents, features), kind)] * size,
        in_specs=[spec(VMEM)] * (size + 4),
        out_specs=[spec(VMEM)] * size,
        scratch_shapes=[VMEM((features // 128, rows + agents, 128), jnp.float32)]
        + [VMEM((rows, features), kind)] * 2
        + [VMEM((agents * (-(-2 * steps * size // 128) * 128), features), kind)] * 2
        + [VMEM((rows, features), kind)],
        compiler_params=pltpu.CompilerParams(vmem_limit_bytes=24 * 2**20),
        cost_estimate=pl.CostEstimate(
            flops=8 * rows * features * features,
            bytes_accessed=2 * (2 * rows + 4 * features) * features,
            transcendentals=rows * HEADS * steps * size,
        ),
        name="time_attention",
    )(*pieces, *weights)


def pack_kernel(size, choose, *refs):
    count = len(choose(0))
    pieces, outs = refs[:size], refs[len(refs) - count :]
    agents = pieces[0].shape[1]
    me, plane = lax.axis_index("tm"), lax.axis_index("agent")
    for out, step in zip(outs, choose(plane)):
        for k in range(size):
            start = pl.multiple_of(jnp.bitwise_xor(me, k) * agents, agents)
            out[pl.ds(start, agents), :] = pieces[k][step]


def pack_stage(pieces, choose, after=()):
    size, count = len(pieces), len(choose(0))
    _, agents, features = pieces[0].shape
    return pl.pallas_call(
        functools.partial(pack_kernel, size, choose),
        out_shape=[jax.ShapeDtypeStruct((agents * size, features), jnp.bfloat16)] * count,
        in_specs=[spec(VMEM)] * size + [spec(pl.ANY)] * len(after),
        out_specs=[spec(VMEM)] * count,
        compiler_params=pltpu.CompilerParams(vmem_limit_bytes=8 * 2**20),
        name="pack_steps",
    )(*pieces, *after)


def near_kernel(count, *refs):
    blocks, weights = refs[:count], refs[count : count + 3]
    outs, normed = refs[count + 3 : count + 6], refs[-1]
    agents = blocks[0].shape[0]
    for b, block in enumerate(blocks):
        normed[pl.ds(b * agents, agents), :] = norm_of(block[...].astype(jnp.float32))
    for weight, out in zip(weights, outs):
        out[...] = project(normed[...], weight[...])


def near_stage(blocks, weights):
    count = len(blocks)
    agents, features = blocks[0].shape
    shape = (count * agents, features)
    return pl.pallas_call(
        functools.partial(near_kernel, count),
        out_shape=[jax.ShapeDtypeStruct(shape, jnp.bfloat16)] * 3,
        in_specs=[spec(VMEM)] * (count + 3),
        out_specs=[spec(VMEM)] * 3,
        scratch_shapes=[VMEM(shape, jnp.bfloat16)],
        compiler_params=pltpu.CompilerParams(vmem_limit_bytes=8 * 2**20),
        name="near_blocks",
    )(*blocks, *weights)


def agent_body(count, blocks, weights, given, outs, scratch):
    normed, query, keys, values, mixed, after, inner, w_out, sems = scratch
    w_query, w_key, w_value, far_out, w_in, w_mlp_out = weights
    copies = fetch((far_out,), (w_out,), sems)
    agents, features = blocks[0].shape
    head_size = features // HEADS
    factor = math.log2(math.e) * head_size**-0.5
    rows, wide_lanes = count * agents, 2 * head_size
    ready = given[0].shape[0] if given else 0
    rest = pl.ds(ready, rows - ready)
    for b in range(ready // agents, count):
        normed[pl.ds(b * agents, agents), :] = norm_of(blocks[b][...].astype(jnp.float32))
    query[rest, :] = project(normed[rest, :], w_query[...])
    if given:
        query[:ready, :] = given[0][...]
    for n, (weight, target) in enumerate(((w_key, keys), (w_value, values))):
        parts = [(ready, project(normed[rest, :], weight[...]))]
        if given:
            parts.append((0, given[n + 1][...]))
        for start, found in parts:
            even = lax.broadcasted_iota(jnp.int32, found.shape, 1) % wide_lanes < head_size
            zero = jnp.zeros_like(found)
            length = found.shape[0]
            target[start : start + length, :] = jnp.where(even, found, zero)
            target[rows + start : rows + start + length, :] = jnp.where(even, zero, found)
    second_rows = lax.broadcasted_iota(jnp.int32, (2 * rows, wide_lanes), 0) >= rows
    second_lanes = lax.broadcasted_iota(jnp.int32, (2 * rows, wide_lanes), 1) >= head_size
    counts = (second_rows == second_lanes).astype(jnp.bfloat16)
    for pair, part in [(p, r) for p in range(HEADS // 2) for r in range(2)]:
        lanes = pl.ds(pair * wide_lanes, wide_lanes)
        at = pl.ds(part * (rows // 2), rows // 2)
        weights_of = []
        both = lax.dot_general(query[at, lanes], keys[:, lanes], NT, preferred_element_type=jnp.float32)
        for h in range(2):
            scores = both[:, h * rows : (h + 1) * rows]
            largest = jnp.max(scores, axis=-1, keepdims=True)
            weights_of.append(jnp.exp2((scores - largest) * factor).astype(jnp.bfloat16))
        sums = jnp.dot(
            jnp.concatenate(weights_of, axis=1),
            jnp.concatenate([values[:, lanes], counts], axis=1),
            preferred_element_type=jnp.float32,
        )
        mixed[at, lanes] = (sums[:, :wide_lanes] / sums[:, wide_lanes:]).astype(jnp.bfloat16)
    copies[0].wait()
    for b in range(count):
        at = pl.ds(b * agents, agents)
        if b % 2 == 0:
            two = pl.ds(b * agents, 2 * agents)
            added = jnp.dot(mixed[two, :], w_out[...], preferred_element_type=jnp.float32)
        own = blocks[b][...].astype(jnp.float32) + added[b % 2 * agents : (b % 2 + 1) * agents]
        after[at, :] = own.astype(jnp.bfloat16)
        normed[at, :] = norm_of(after[at, :].astype(jnp.float32))
    hidden = w_in.shape[1]
    for start in range(0, hidden, features):
        inner[:, pl.ds(start, features)] = gelu(
            jnp.dot(
                normed[...], w_in[:, pl.ds(start, features)], preferred_element_type=jnp.float32
            )
        ).astype(jnp.bfloat16)
    final = after[...].astype(jnp.float32) + jnp.dot(
        inner[...], w_mlp_out[...], preferred_element_type=jnp.float32
    )
    for b in range(count):
        outs[b][...] = final[b * agents : (b + 1) * agents].astype(jnp.bfloat16)


def agent_kernel(count, ready, middle_only, *refs):
    blocks, weights = refs[:count], refs[count : count + 6]
    given = refs[count + 6 : count + 6 + ready]
    outs, scratch = refs[-9 - count : -9], refs[-9:]

    def run():
        agent_body(count, blocks, weights, given, outs, scratch)

    if middle_only:
        plane = lax.axis_index("agent")
        pl.when(jnp.logical_or(plane == 1, plane == 2))(run)
    else:
        run()


def agent_stage(blocks, weights, middle_only, after=(), given=()):
    count = len(blocks)
    agents, features = blocks[0].shape
    hidden = weights[4].shape[1]
    rows = count * agents
    kind = jnp.bfloat16
    return pl.pallas_call(
        functools.partial(agent_kernel, count, len(given), middle_only),
        out_shape=[jax.ShapeDtypeStruct((agents, features), kind)] * count,
        in_specs=[spec(VMEM)] * (count + 3)
        + [spec(HBM)]
        + [spec(VMEM)] * (2 + len(given))
        + [spec(pl.ANY)] * len(after),
        out_specs=[spec(VMEM)] * count,
        scratch_shapes=[VMEM((rows, features), kind)] * 2
        + [VMEM((2 * rows, features), kind)] * 2
        + [VMEM((rows, features), kind)] * 2
        + [VMEM((rows, hidden), kind)]
        + [VMEM(weights[3].shape, kind), pltpu.SemaphoreType.DMA((1,))],
        compiler_params=pltpu.CompilerParams(vmem_limit_bytes=16 * 2**20),
        cost_estimate=pl.CostEstimate(
            flops=2 * rows * features * (4 * features + 2 * hidden + 2 * rows),
            bytes_accessed=2 * rows * features * 8,
            transcendentals=rows * (HEADS * rows + hidden),
        ),
        name="agent_step",
    )(*blocks, *weights[:3], *in_hbm(weights[3:4]), *weights[4:], *given, *after)


def place_kernel(*refs):
    sources, out, sems = [refs[k] for k in (0, 1, 2, 3)], refs[4], refs[5]
    plane = lax.axis_index("agent")
    copies = [
        pltpu.make_async_copy(source, out.at[jnp.bitwise_xor(plane, k)], sems.at[k])
        for k, source in enumerate(sources)
    ]
    for copy in copies:
        copy.start()
    for copy in copies:
        copy.wait()


def place_extra_kernel(*refs):
    sources, out, sems = [refs[k] for k in (0, 1, 2, 3)], refs[5], refs[6]
    plane = lax.axis_index("agent")
    middle = jnp.logical_or(plane == 1, plane == 2)
    low = plane // 2

    def place(one, other):
        rows = one.shape[0] // 4
        copies = []
        for n, (source, step) in enumerate(((one, 4 + low), (other, 5 - low))):
            for part in range(4):
                at = pl.ds(part * rows, rows)
                copies.append(
                    pltpu.make_async_copy(source.at[at], out.at[step, at], sems.at[n, part])
                )
        for copy in copies:
            copy.start()
        for copy in copies:
            copy.wait()

    pl.when(middle)(lambda: place(sources[0], sources[3]))
    pl.when(jnp.logical_not(middle))(lambda: place(sources[1], sources[2]))


def place_stage(whole, extra):
    agents, features = whole[0].shape
    shape = jax.ShapeDtypeStruct((6, agents, features), jnp.bfloat16)
    begun = pl.pallas_call(
        place_kernel,
        out_shape=shape,
        in_specs=[spec(VMEM)] * 4,
        out_specs=spec(HBM),
        scratch_shapes=[pltpu.SemaphoreType.DMA((4,))],
        compiler_params=pltpu.CompilerParams(vmem_limit_bytes=4 * 2**20),
        name="place_steps",
    )(*[whole[k] for k in (0, 1, 2, 3)])
    return pl.pallas_call(
        place_extra_kernel,
        out_shape=shape,
        in_specs=[spec(VMEM)] * 4 + [spec(HBM)],
        out_specs=spec(HBM),
        input_output_aliases={4: 0},
        scratch_shapes=[pltpu.SemaphoreType.DMA((2, 4))],
        compiler_params=pltpu.CompilerParams(vmem_limit_bytes=4 * 2**20),
        name="place_extra",
    )(*[extra[k] for k in (0, 1, 2, 3)], begun)


def xor_pairs(size, k, targets=None):
    return [(j, j ^ k) for j in range(size) if targets is None or j ^ k in targets]


def exchange(parts, axis, targets=None, ordered=False):
    size = len(parts)
    moved = {}
    for k in range(size - 1, 0, -1):
        part = parts[k]
        if ordered and k == 1:
            part, moved[size - 1] = lax.optimization_barrier((part, moved[size - 1]))
        moved[k] = lax.ppermute(part, axis, xor_pairs(size, k, targets))
    return [parts[0]] + [moved[k] for k in range(1, size)]


def together(parts):
    return lax.optimization_barrier(tuple(parts[::-1]))[::-1]


def picked(plane, values):
    result = jnp.int32(values[0])
    for place in range(1, len(values)):
        result = jnp.where(plane == place, values[place], result)
    return result


def whole_steps(plane):
    return [jnp.bitwise_xor(plane, k) for k in range(4)]


def extra_steps(plane):
    return [
        4 + picked(plane, (0, 0, 1, 0)),
        4 + picked(plane, (0, 0, 0, 1)),
        4 + picked(plane, (1, 0, 0, 0)),
        4 + picked(plane, (0, 1, 0, 0)),
    ]


def local(
    states,
    neighbours,
    w_query_t,
    w_key_t,
    w_value_t,
    w_out_t,
    w_query_a,
    w_key_a,
    w_value_a,
    w_out_a,
    w_in,
    w_mlp_out,
):
    local_steps, local_agents, features = states.shape
    size, planes = lax.axis_size("tm"), lax.axis_size("agent")
    share = local_agents // size
    time_weights = (w_query_t, w_key_t, w_value_t, w_out_t)
    agent_weights = (w_query_a, w_key_a, w_value_a, w_out_a, w_in, w_mlp_out)
    fits = (
        size & (size - 1) == 0
        and share * size == local_agents
        and share % 16 == 0
        and planes == 4
        and neighbours.shape == (4, 4)
        and local_steps == 6
    )
    if not fits:
        after_time = general_time(states, *time_weights)
        return general_agent(after_time, neighbours, *agent_weights)

    pieces = together(exchange(share_stage(states, size), "tm", ordered=True))
    pieces = together(exchange(time_stage(pieces, time_weights), "tm", ordered=True))
    blocks_a = exchange(pack_stage(pieces, whole_steps), "agent")
    blocks_b = exchange(pack_stage(pieces, extra_steps, blocks_a[2:3]), "agent", (1, 2))

    near = near_stage(blocks_a[:3], agent_weights[:3])
    result_a = agent_stage(blocks_a, agent_weights, False, (), near)
    done_a = exchange(result_a, "agent")
    result_b = agent_stage(blocks_b, agent_weights, True, result_a[:1])
    done_b = [result_b[0]] + [
        lax.ppermute(result_b[k], "agent", [(j, j ^ k) for j in (1, 2)]) for k in (1, 2, 3)
    ]
    return place_stage(done_a, done_b)


def solution(mesh):
    placed = (P("tm", "agent", None), P(), P(), P(), P(), P(), P(), P(), P(), P(), P(), P())
    return jax.shard_map(
        local, mesh=mesh, in_specs=placed, out_specs=P("tm", "agent", None), check_vma=False
    )
```
